32 devices in a mesh: item: 8 (over z, x), head: 4 (over y, core).
Axes of the slice: x: 2, y: 2, z: 4, core: 2. Of those that a mesh axis runs over, the one named last changes fastest.
Arguments:
- media: bfloat16 [32, 512, 1536], P('item', 'head'), may hold values from -6 to 6
- latents: bfloat16 [32, 64, 1536], P('item', 'head'), may hold values from -6 to 6
- cotangent: bfloat16 [32, 64, 1536], P('item', 'head'), may hold values from -6 to 6
- frame_counts: int32 [32], P('item'), may hold values from 1 to 8, as said below
- query_weight: bfloat16 [1536, 1536], P('item', 'head'), may hold values from -0.15625 to 0.15625
- key_weight: bfloat16 [1536, 1536], P('item', 'head'), may hold values from -0.15625 to 0.15625
- value_weight: bfloat16 [1536, 1536], P('item', 'head'), may hold values from -0.15625 to 0.15625
- output_weight: bfloat16 [1536, 1536], P('item', 'head'), may hold values from -2.5 to 2.5
- up_weight: bfloat16 [1536, 6144], P('item', 'head'), may hold values from -0.15625 to 0.15625
- down_weight: bfloat16 [1536, 6144], P('item', 'head'), may hold values from -0.078125 to 0.078125
- media_gain: bfloat16 [1536], P('item'), may hold values from 0.25 to 1.75
- media_bias: bfloat16 [1536], P('item'), may hold values from -3 to 3
- latent_gain: bfloat16 [1536], P('item'), may hold values from 0.25 to 1.75
- latent_bias: bfloat16 [1536], P('item'), may hold values from -3 to 3
- ffn_gain: bfloat16 [1536], P('item'), may hold values from 0.25 to 1.75
- ffn_bias: bfloat16 [1536], P('item'), may hold values from -3 to 3
- time_embed: bfloat16 [8, 1536], P(None, 'item'), may hold values from -3 to 3
Outputs:
- latents_out: bfloat16 [32, 64, 1536], P('item', 'head')
- latents_grad: float32 [32, 64, 1536], P('item', 'head')
- media_grad: float32 [32, 512, 1536], P('item', 'head')
- query_grad: float32 [1536, 1536], P('item', 'head')
- key_grad: float32 [1536, 1536], P('item', 'head')
- value_grad: float32 [1536, 1536], P('item', 'head')
- output_grad: float32 [1536, 1536], P('item', 'head')
- up_grad: float32 [1536, 6144], P('item', 'head')
- down_grad: float32 [1536, 6144], P('item', 'head')
- media_gain_grad: float32 [1536], P('item')
- media_bias_grad: float32 [1536], P('item')
- latent_gain_grad: float32 [1536], P('item')
- latent_bias_grad: float32 [1536], P('item')
- ffn_gain_grad: float32 [1536], P('item')
- ffn_bias_grad: float32 [1536], P('item')
- time_grad: float32 [8, 1536], P(None, 'item')
The draws below stay inside these ranges and needn't reach their ends.
Inputs may be any that keep to these rules, and one draw needn't show every extreme that they name: `frame_counts`: an item's true frame count; single images have 1, and some item in every draw has all 8.
All inputs are finite; a program needn't handle non-finite values.
Results may differ from the reference program's by a relative error of at most 0.02.
Values may be sent and summed in bfloat16 or wider, within the bound.
A program may use at most 88 MiB of HBM per device.

```python
import jax
import jax.numpy as jnp
from jax import lax

HEADS = 16
HEAD_DIM = 96
D = 1536
FF = 6144
L = 64
F = 8
P_SIZE = 64
ITEMS = 32


def draw_frame_counts(key, part):
    key = jax.random.fold_in(key, 7)
    first, second, third = jax.random.split(key, 3)
    is_clip = jax.random.randint(first, (ITEMS,), 0, 2) == 1
    clip_frames = jax.random.randint(second, (ITEMS,), 1, F + 1)
    counts = jnp.where(is_clip, clip_frames, 1)
    chosen = jax.random.randint(third, (), 0, ITEMS)
    counts = jnp.where(jnp.arange(ITEMS) == chosen, F, counts)
    return counts.astype(jnp.int32)


def block_scale(rng, shape, cuts, low, largest):
    loudness, own = 1.0, jax.random.fold_in(rng, 6)
    for dim, parts in cuts:
        steps = jnp.exp(jax.random.uniform(jax.random.fold_in(own, dim), (parts,), jnp.float32, low / len(cuts), largest / len(cuts)))
        loudness = loudness * jnp.repeat(steps, shape[dim] // parts).reshape([-1 if axis == dim else 1 for axis in range(len(shape))])
    return loudness


def bell_draw(stream_key, shape, width, most, cuts=(), kind=jnp.bfloat16):
    factor_of = block_scale(stream_key, shape, cuts, -0.22, 0.18) if cuts else 1.0
    values = jax.random.normal(stream_key, shape, jnp.float32) * width * factor_of
    return jnp.minimum(jnp.maximum(values, -most), most).astype(kind)


def setup_inputs(seed: int = 0) -> dict:
    seeds = jax.random.split(jax.random.key(seed), 18)
    return {
        "media": bell_draw(seeds[0], (ITEMS, F * P_SIZE, D), 1.0, 6.0, ((0, 8), (1, 4))),
        "latents": bell_draw(seeds[1], (ITEMS, L, D), 1.0, 6.0, ((0, 8), (1, 4))),
        "cotangent": bell_draw(seeds[2], (ITEMS, L, D), 1.0, 6.0, ((0, 8), (1, 4))),
        "frame_counts": draw_frame_counts(jax.random.fold_in(seeds[17], 71), 0),
        "query_weight": bell_draw(seeds[4], (D, D), D ** -0.5, 0.15625, ((0, 8), (1, 4))),
        "key_weight": bell_draw(seeds[5], (D, D), D ** -0.5, 0.15625, ((0, 8), (1, 4))),
        "value_weight": bell_draw(seeds[6], (D, D), D ** -0.5, 0.15625, ((0, 8), (1, 4))),
        "output_weight": bell_draw(seeds[7], (D, D), (max(D // 256, 1)) ** -0.5, 2.5, ((0, 8), (1, 4))),
        "up_weight": bell_draw(seeds[8], (D, FF), D ** -0.5, 0.15625, ((0, 8), (1, 4))),
        "down_weight": bell_draw(seeds[9], (D, FF), FF ** -0.5, 0.078125, ((0, 8), (1, 4))),
        "media_gain": jnp.clip(1.0 + 0.15 * jax.random.normal(seeds[10], (D,), jnp.float32), 0.25, 1.75).astype(jnp.bfloat16),
        "media_bias": bell_draw(seeds[11], (D,), 0.3, 3.0, ((0, 8),)),
        "latent_gain": jnp.clip(1.0 + 0.15 * jax.random.normal(seeds[12], (D,), jnp.float32), 0.25, 1.75).astype(jnp.bfloat16),
        "latent_bias": bell_draw(seeds[13], (D,), 0.3, 3.0, ((0, 8),)),
        "ffn_gain": jnp.clip(1.0 + 0.15 * jax.random.normal(seeds[14], (D,), jnp.float32), 0.25, 1.75).astype(jnp.bfloat16),
        "ffn_bias": bell_draw(seeds[15], (D,), 0.3, 3.0, ((0, 8),)),
        "time_embed": bell_draw(seeds[16], (F, D), 0.5, 3.0, ((1, 8),)),
    }


@jax.custom_vjp
def low(v):
    return lax.optimization_barrier(v.astype(jnp.bfloat16)).astype(jnp.float32)

@jax.custom_vjp
def low_back(v):
    return v

def low_keep(v):
    return (low(v), None)

def low_pass(kept, grad):
    return (grad,)

def back_keep(v):
    return (v, None)

def back_low(kept, grad):
    return (low(grad),)
low.defvjp(low_keep, low_pass)
low_back.defvjp(back_keep, back_low)
eps = 1e-05
HIGH = lax.Precision.HIGHEST

def layer_norm(rows, gain, bias):
    row_mean = lax.optimization_barrier(jnp.mean(rows, axis=-1, keepdims=True))
    centered = rows - row_mean
    variance = lax.optimization_barrier(jnp.mean(centered * centered, axis=-1, keepdims=True))
    return centered * lax.rsqrt(variance + eps) * gain + bias

def matmul(left, right):
    return jnp.dot(left, right, precision=HIGH, preferred_element_type=jnp.float32)

def times_transposed(left, right):
    return lax.dot_general(left, right, (((1,), (1,)), ((), ())), precision=HIGH, preferred_element_type=jnp.float32)

def item_forward(params, media_item, latent_item, count):
    w_query, w_key, w_value, w_output, w_up, w_down, g_media, b_media, g_latent, b_latent, g_ffn, b_ffn, time_table = params
    key_count = F * P_SIZE + L
    attn_scale = HEAD_DIM ** (-0.5)
    frame_of_row = jnp.arange(F * P_SIZE, dtype=jnp.int32) // P_SIZE
    shifted = media_item + jnp.repeat(time_table, P_SIZE, axis=0)
    media_hat = low(layer_norm(shifted, g_media, b_media))
    latent_hat = low(layer_norm(latent_item, g_latent, b_latent))
    joined = jnp.concatenate([media_hat, latent_hat], axis=0)
    query = low_back(low(attn_scale * matmul(latent_hat, w_query)))
    keys = low_back(low(matmul(joined, w_key)))
    values = low_back(low(matmul(joined, w_value)))
    query_heads = query.reshape(L, HEADS, HEAD_DIM)
    key_heads = keys.reshape(key_count, HEADS, HEAD_DIM)
    value_heads = values.reshape(key_count, HEADS, HEAD_DIM)
    scores = low_back(jnp.einsum('lhe,nhe->hln', query_heads, key_heads, precision=HIGH))
    key_valid = jnp.concatenate([frame_of_row < count, jnp.ones((L,), dtype=bool)])
    scores = jnp.where(key_valid[None, None, :], scores, -1e+30)
    row_peak = lax.optimization_barrier(jnp.max(scores, axis=-1, keepdims=True))
    expo = jnp.exp(scores - row_peak)
    weights = expo / lax.optimization_barrier(jnp.sum(expo, axis=-1, keepdims=True))
    mixed = jnp.einsum('hln,nhe->lhe', low(weights), value_heads, precision=HIGH).reshape(L, D)
    mixed = low_back(low(mixed))
    attended = low_back(times_transposed(mixed, w_output))
    middle = latent_item + attended
    ffn_in = low(layer_norm(middle, g_ffn, b_ffn))
    pre_act = low_back(matmul(ffn_in, w_up))
    activated = low(jax.nn.gelu(pre_act))
    ffn_out = low_back(times_transposed(activated, w_down))
    return middle + ffn_out

def reference(media, latents, cotangent, frame_counts, query_weight, key_weight, value_weight, output_weight, up_weight, down_weight, media_gain, media_bias, latent_gain, latent_bias, ffn_gain, ffn_bias, time_embed):
    params = tuple((p.astype(jnp.float32) for p in (query_weight, key_weight, value_weight, output_weight, up_weight, down_weight, media_gain, media_bias, latent_gain, latent_bias, ffn_gain, ffn_bias, time_embed)))
    media_f = media.astype(jnp.float32)
    latents_f = latents.astype(jnp.float32)

    def forward(media_all, latents_all, param_set):
        step_fn = jax.checkpoint(item_forward)

        def one_item(packed):
            return step_fn(param_set, packed[0], packed[1], packed[2])
        return lax.map(one_item, (media_all, latents_all, frame_counts))
    result, pull = jax.vjp(forward, media_f, latents_f, params)
    media_grad, latents_grad, param_grads = pull(cotangent.astype(jnp.float32))
    return (result.astype(jnp.bfloat16), latents_grad, media_grad, param_grads[0], param_grads[1], param_grads[2], param_grads[3], param_grads[4], param_grads[5], param_grads[6], param_grads[7], param_grads[8], param_grads[9], param_grads[10], param_grads[11], param_grads[12])
```

```python
import jax
import jax.numpy as jnp
from jax import lax
from jax.sharding import PartitionSpec as P

HEAD_DIM = 96
P_SIZE = 64
EPS = 1e-05
BF = jnp.bfloat16
F32 = jnp.float32


def norm_forward(rows, gain, bias):
    mean = jnp.mean(rows, axis=-1, keepdims=True)
    centered = rows - mean
    inverse = lax.rsqrt(jnp.mean(centered * centered, axis=-1, keepdims=True) + EPS)
    normed = centered * inverse
    return normed * gain + bias, normed, inverse


def norm_backward(upstream, normed, inverse, gain):
    scaled = upstream * gain
    first = jnp.mean(scaled, axis=-1, keepdims=True)
    second = jnp.mean(scaled * normed, axis=-1, keepdims=True)
    axes = tuple(range(upstream.ndim - 1))
    return (
        inverse * (scaled - first - normed * second),
        jnp.sum(upstream * normed, axis=axes),
        jnp.sum(upstream, axis=axes),
    )


def dot(left, right, a, b):
    return lax.dot_general(left, right, (((a,), (b,)), ((), ())), preferred_element_type=F32)


def gather_rows(rows):
    return lax.all_gather(rows, "head", axis=1, tiled=True)


def scatter_rows(rows):
    return lax.psum_scatter(rows.astype(BF), "head", scatter_dimension=1, tiled=True).astype(F32)


def item_scatter(grad):
    return lax.psum_scatter(grad.astype(BF), "item", scatter_dimension=0, tiled=True).astype(F32)


def on_device(
    media, latents, cotangent, frame_counts,
    query_weight, key_weight, value_weight, output_weight, up_weight, down_weight,
    media_gain, media_bias, latent_gain, latent_bias, ffn_gain, ffn_bias, time_embed,
):
    items, local_media, width = media.shape
    frames = time_embed.shape[0]
    local_frames = local_media // P_SIZE
    place = lax.axis_index("head")
    scale = HEAD_DIM ** (-0.5)
    small = jnp.concatenate(
        [jnp.stack([media_gain, media_bias, latent_gain, latent_bias, ffn_gain, ffn_bias]), time_embed]
    )
    small = lax.all_gather(small, "item", axis=1, tiled=True).astype(F32)
    g_media, b_media, g_latent, b_latent, g_ffn, b_ffn = (small[k] for k in range(6))
    time_rows = lax.dynamic_slice_in_dim(small[6:], place * local_frames, local_frames, 0)
    w_query, w_key, w_value, w_output, w_up, w_down = (
        lax.all_gather(w, "item", axis=0, tiled=True)
        for w in (query_weight, key_weight, value_weight, output_weight, up_weight, down_weight)
    )
    shifted = (
        media.astype(F32).reshape(items, local_frames, P_SIZE, width) + time_rows[None, :, None, :]
    ).reshape(media.shape)
    media_norm, media_hat, media_inv = norm_forward(shifted, g_media, b_media)
    latent_f = latents.astype(F32)
    latent_norm, latent_hat, latent_inv = norm_forward(latent_f, g_latent, b_latent)
    media_all = gather_rows(media_norm.astype(BF))
    latent_all = gather_rows(latent_norm.astype(BF))
    upstream = gather_rows(cotangent)
    media_count, latent_count = media_all.shape[1], latent_all.shape[1]
    joined = jnp.concatenate([media_all, latent_all], axis=1)
    key_count = joined.shape[1]
    local_heads = w_query.shape[1] // HEAD_DIM
    query = (scale * dot(latent_all, w_query, 2, 0)).astype(BF)
    keys = dot(joined, w_key, 2, 0).astype(BF)
    values = dot(joined, w_value, 2, 0).astype(BF)
    query_h = query.reshape(items, latent_count, local_heads, HEAD_DIM)
    key_h = keys.reshape(items, key_count, local_heads, HEAD_DIM)
    value_h = values.reshape(items, key_count, local_heads, HEAD_DIM)
    index = jnp.arange(key_count, dtype=jnp.int32)
    valid = (index[None, :] // P_SIZE < frame_counts[:, None]) | (index[None, :] >= media_count)
    valid = valid[:, None, None, :]

    def mix(spec, left, right):
        return jnp.einsum(spec, left, right, preferred_element_type=F32)

    scores = jnp.where(valid, mix("blhe,bnhe->bhln", query_h, key_h), -1e30)
    peak = jnp.max(scores, axis=-1, keepdims=True)
    expo = jnp.exp(scores - peak)
    weights = expo / jnp.sum(expo, axis=-1, keepdims=True)
    weights_low = weights.astype(BF)
    mixed = mix("bhln,bnhe->blhe", weights_low, value_h).reshape(items, latent_count, -1).astype(BF)
    middle = latent_f + scatter_rows(dot(mixed, w_output, 2, 1))
    ffn_norm, ffn_hat, ffn_inv = norm_forward(middle, g_ffn, b_ffn)
    ffn_all = gather_rows(ffn_norm.astype(BF))
    rows = items * latent_count
    ffn_rows = ffn_all.reshape(rows, width)
    up_rows = upstream.reshape(rows, width)
    pre = dot(ffn_rows, w_up, 1, 0)
    act, gelu_back = jax.vjp(jax.nn.gelu, pre)
    act = act.astype(BF)
    ffn_out = scatter_rows(dot(act, w_down, 1, 1).reshape(items, latent_count, width))
    output = (middle + ffn_out).astype(BF)
    grad_down = dot(up_rows, act, 0, 0)
    grad_pre = gelu_back(dot(up_rows, w_down, 1, 0))[0].astype(BF)
    grad_up = dot(ffn_rows, grad_pre, 0, 0)
    grad_ffn = scatter_rows(dot(grad_pre, w_up, 1, 1).reshape(items, latent_count, width))
    grad_mid, grad_fgain, grad_fbias = norm_backward(grad_ffn, ffn_hat, ffn_inv, g_ffn)
    grad_middle = cotangent.astype(F32) + grad_mid
    attended_grad = gather_rows(grad_middle.astype(BF)).reshape(rows, width)
    grad_output = dot(attended_grad, mixed.reshape(rows, -1), 0, 0)
    grad_mixed = dot(attended_grad, w_output, 1, 0).astype(BF)
    gm_h = grad_mixed.reshape(items, latent_count, local_heads, HEAD_DIM)
    grad_values = mix("bhln,blhe->bnhe", weights_low, gm_h).astype(BF).reshape(items * key_count, -1)
    grad_weights = mix("blhe,bnhe->bhln", gm_h, value_h)
    inner = jnp.sum(weights * grad_weights, axis=-1, keepdims=True)
    grad_scores = (weights * (grad_weights - inner)).astype(BF)
    grad_query = mix("bhln,bnhe->blhe", grad_scores, key_h).astype(BF).reshape(rows, -1)
    grad_keys = mix("bhln,blhe->bnhe", grad_scores, query_h).astype(BF).reshape(items * key_count, -1)
    joined_rows = joined.reshape(items * key_count, width)
    grad_wquery = scale * dot(latent_all.reshape(rows, width), grad_query, 0, 0)
    grad_wkey = dot(joined_rows, grad_keys, 0, 0)
    grad_wvalue = dot(joined_rows, grad_values, 0, 0)
    grad_joined = dot(grad_keys, w_key, 1, 1) + dot(grad_values, w_value, 1, 1)
    grad_joined = grad_joined.reshape(items, key_count, width)
    grad_latent_all = grad_joined[:, media_count:] + scale * dot(grad_query, w_query, 1, 1).reshape(
        items, latent_count, width
    )
    media_back = scatter_rows(grad_joined[:, :media_count])
    latent_back = scatter_rows(grad_latent_all)
    grad_media, grad_mgain, grad_mbias = norm_backward(media_back, media_hat, media_inv, g_media)
    grad_lat, grad_lgain, grad_lbias = norm_backward(latent_back, latent_hat, latent_inv, g_latent)
    time_local = jnp.sum(grad_media.reshape(items, local_frames, P_SIZE, width), axis=(0, 2))
    grad_time = lax.dynamic_update_slice_in_dim(
        jnp.zeros((frames, width), F32), time_local, place * local_frames, 0
    )
    smalls = jnp.concatenate(
        [jnp.stack([grad_mgain, grad_mbias, grad_lgain, grad_lbias, grad_fgain, grad_fbias]), grad_time]
    )
    smalls = lax.psum_scatter(smalls, ("item",), scatter_dimension=1, tiled=True)
    smalls = lax.psum(smalls, "head")
    return (
        output,
        grad_middle + grad_lat,
        grad_media,
        *(item_scatter(g) for g in (grad_wquery, grad_wkey, grad_wvalue, grad_output, grad_up, grad_down)),
        *(smalls[k] for k in range(6)),
        smalls[6:],
    )


def solution(mesh):
    rows = P("item", "head", None)
    block = P("item", "head")
    vector = P("item")
    table = P(None, "item")
    return jax.shard_map(
        on_device,
        mesh=mesh,
        in_specs=(rows,) * 3 + (vector,) + (block,) * 6 + (vector,) * 6 + (table,),
        out_specs=(rows,) * 3 + (block,) * 6 + (vector,) * 6 + (table,),
        check_vma=False,
    )
```

```python
import functools

import jax
import jax.numpy as jnp
from jax import lax
from jax.experimental import pallas as pl
from jax.experimental.pallas import tpu as pltpu
from jax.sharding import PartitionSpec as P

HEAD_DIM = 96
P_SIZE = 64
EPS = 1e-05
BF = jnp.bfloat16
F32 = jnp.float32


def norm_forward(rows, gain, bias):
    mean = jnp.mean(rows, axis=-1, keepdims=True)
    centered = rows - mean
    inverse = lax.rsqrt(jnp.mean(centered * centered, axis=-1, keepdims=True) + EPS)
    normed = centered * inverse
    return normed * gain + bias, normed, inverse


def norm_backward(upstream, normed, inverse, gain):
    scaled = upstream * gain
    first = jnp.mean(scaled, axis=-1, keepdims=True)
    second = jnp.mean(scaled * normed, axis=-1, keepdims=True)
    axes = tuple(range(upstream.ndim - 1))
    return (
        inverse * (scaled - first - normed * second),
        jnp.sum(upstream * normed, axis=axes),
        jnp.sum(upstream, axis=axes),
    )


def dot(left, right, a, b):
    return lax.dot_general(left, right, (((a,), (b,)), ((), ())), preferred_element_type=F32)


def gather_rows(rows):
    return lax.all_gather(rows, "head", axis=1, tiled=True)


def scatter_rows(rows):
    return lax.psum_scatter(rows.astype(BF), "head", scatter_dimension=1, tiled=True).astype(F32)


def item_scatter(grad):
    return lax.psum_scatter(grad.astype(BF), "item", scatter_dimension=0, tiled=True).astype(F32)


def plain_step(
    media, latents, cotangent, frame_counts,
    query_weight, key_weight, value_weight, output_weight, up_weight, down_weight,
    media_gain, media_bias, latent_gain, latent_bias, ffn_gain, ffn_bias, time_embed,
):
    items, local_media, width = media.shape
    frames = time_embed.shape[0]
    local_frames = local_media // P_SIZE
    place = lax.axis_index("head")
    scale = HEAD_DIM ** (-0.5)
    small = jnp.concatenate(
        [jnp.stack([media_gain, media_bias, latent_gain, latent_bias, ffn_gain, ffn_bias]), time_embed]
    )
    small = lax.all_gather(small, "item", axis=1, tiled=True).astype(F32)
    g_media, b_media, g_latent, b_latent, g_ffn, b_ffn = (small[k] for k in range(6))
    time_rows = lax.dynamic_slice_in_dim(small[6:], place * local_frames, local_frames, 0)
    w_query, w_key, w_value, w_output, w_up, w_down = (
        lax.all_gather(w, "item", axis=0, tiled=True)
        for w in (query_weight, key_weight, value_weight, output_weight, up_weight, down_weight)
    )
    shifted = (
        media.astype(F32).reshape(items, local_frames, P_SIZE, width) + time_rows[None, :, None, :]
    ).reshape(media.shape)
    media_norm, media_hat, media_inv = norm_forward(shifted, g_media, b_media)
    latent_f = latents.astype(F32)
    latent_norm, latent_hat, latent_inv = norm_forward(latent_f, g_latent, b_latent)
    media_all = gather_rows(media_norm.astype(BF))
    latent_all = gather_rows(latent_norm.astype(BF))
    upstream = gather_rows(cotangent)
    media_count, latent_count = media_all.shape[1], latent_all.shape[1]
    joined = jnp.concatenate([media_all, latent_all], axis=1)
    key_count = joined.shape[1]
    local_heads = w_query.shape[1] // HEAD_DIM
    query = (scale * dot(latent_all, w_query, 2, 0)).astype(BF)
    keys = dot(joined, w_key, 2, 0).astype(BF)
    values = dot(joined, w_value, 2, 0).astype(BF)
    query_h = query.reshape(items, latent_count, local_heads, HEAD_DIM)
    key_h = keys.reshape(items, key_count, local_heads, HEAD_DIM)
    value_h = values.reshape(items, key_count, local_heads, HEAD_DIM)
    index = jnp.arange(key_count, dtype=jnp.int32)
    valid = (index[None, :] // P_SIZE < frame_counts[:, None]) | (index[None, :] >= media_count)
    valid = valid[:, None, None, :]

    def mix(spec, left, right):
        return jnp.einsum(spec, left, right, preferred_element_type=F32)

    scores = jnp.where(valid, mix("blhe,bnhe->bhln", query_h, key_h), -1e30)
    peak = jnp.max(scores, axis=-1, keepdims=True)
    expo = jnp.exp(scores - peak)
    weights = expo / jnp.sum(expo, axis=-1, keepdims=True)
    weights_low = weights.astype(BF)
    mixed = mix("bhln,bnhe->blhe", weights_low, value_h).reshape(items, latent_count, -1).astype(BF)
    middle = latent_f + scatter_rows(dot(mixed, w_output, 2, 1))
    ffn_norm, ffn_hat, ffn_inv = norm_forward(middle, g_ffn, b_ffn)
    ffn_all = gather_rows(ffn_norm.astype(BF))
    rows = items * latent_count
    ffn_rows = ffn_all.reshape(rows, width)
    up_rows = upstream.reshape(rows, width)
    pre = dot(ffn_rows, w_up, 1, 0)
    act, gelu_back = jax.vjp(jax.nn.gelu, pre)
    act = act.astype(BF)
    ffn_out = scatter_rows(dot(act, w_down, 1, 1).reshape(items, latent_count, width))
    output = (middle + ffn_out).astype(BF)
    grad_down = dot(up_rows, act, 0, 0)
    grad_pre = gelu_back(dot(up_rows, w_down, 1, 0))[0].astype(BF)
    grad_up = dot(ffn_rows, grad_pre, 0, 0)
    grad_ffn = scatter_rows(dot(grad_pre, w_up, 1, 1).reshape(items, latent_count, width))
    grad_mid, grad_fgain, grad_fbias = norm_backward(grad_ffn, ffn_hat, ffn_inv, g_ffn)
    grad_middle = cotangent.astype(F32) + grad_mid
    attended_grad = gather_rows(grad_middle.astype(BF)).reshape(rows, width)
    grad_output = dot(attended_grad, mixed.reshape(rows, -1), 0, 0)
    grad_mixed = dot(attended_grad, w_output, 1, 0).astype(BF)
    gm_h = grad_mixed.reshape(items, latent_count, local_heads, HEAD_DIM)
    grad_values = mix("bhln,blhe->bnhe", weights_low, gm_h).astype(BF).reshape(items * key_count, -1)
    grad_weights = mix("blhe,bnhe->bhln", gm_h, value_h)
    inner = jnp.sum(weights * grad_weights, axis=-1, keepdims=True)
    grad_scores = (weights * (grad_weights - inner)).astype(BF)
    grad_query = mix("bhln,bnhe->blhe", grad_scores, key_h).astype(BF).reshape(rows, -1)
    grad_keys = mix("bhln,blhe->bnhe", grad_scores, query_h).astype(BF).reshape(items * key_count, -1)
    joined_rows = joined.reshape(items * key_count, width)
    grad_wquery = scale * dot(latent_all.reshape(rows, width), grad_query, 0, 0)
    grad_wkey = dot(joined_rows, grad_keys, 0, 0)
    grad_wvalue = dot(joined_rows, grad_values, 0, 0)
    grad_joined = dot(grad_keys, w_key, 1, 1) + dot(grad_values, w_value, 1, 1)
    grad_joined = grad_joined.reshape(items, key_count, width)
    grad_latent_all = grad_joined[:, media_count:] + scale * dot(grad_query, w_query, 1, 1).reshape(
        items, latent_count, width
    )
    media_back = scatter_rows(grad_joined[:, :media_count])
    latent_back = scatter_rows(grad_latent_all)
    grad_media, grad_mgain, grad_mbias = norm_backward(media_back, media_hat, media_inv, g_media)
    grad_lat, grad_lgain, grad_lbias = norm_backward(latent_back, latent_hat, latent_inv, g_latent)
    time_local = jnp.sum(grad_media.reshape(items, local_frames, P_SIZE, width), axis=(0, 2))
    grad_time = lax.dynamic_update_slice_in_dim(
        jnp.zeros((frames, width), F32), time_local, place * local_frames, 0
    )
    smalls = jnp.concatenate(
        [jnp.stack([grad_mgain, grad_mbias, grad_lgain, grad_lbias, grad_fgain, grad_fbias]), grad_time]
    )
    smalls = lax.psum_scatter(smalls, ("item",), scatter_dimension=1, tiled=True)
    smalls = lax.psum(smalls, "head")
    return (
        output,
        grad_middle + grad_lat,
        grad_media,
        *(item_scatter(g) for g in (grad_wquery, grad_wkey, grad_wvalue, grad_output, grad_up, grad_down)),
        *(smalls[k] for k in range(6)),
        smalls[6:],
    )


MESH = pl.DeviceIdType.MESH
VMEM = pltpu.VMEM
ANY = pl.ANY
SPREAD = 4


class Place:
    def __init__(self, count, sems):
        self.count = count
        self.sems = sems
        self.used = 0
        self.sent = []
        i, h = lax.axis_index("item"), lax.axis_index("head")
        self.item, self.head = i, h
        self.y, self.core = h // 2, h % 2
        self.quarter = i % SPREAD
        self.group = i // SPREAD
        odd = i % 2
        self.spot = (1 - odd) * (i // 2) + odd * (count - 1 - i // 2)
        self.sibling = {"item": i, "head": 2 * self.y + 1 - self.core}
        self.across = {"item": i, "head": 2 * (1 - self.y) + self.core}
        self.chip = 2 * self.quarter + self.y

    def ring(self, spot):
        spot = (spot + self.count) % self.count
        back = spot // (self.count // 2)
        return (1 - back) * 2 * spot + back * (2 * (self.count - 1 - spot) + 1)

    def member(self, k):
        bits = [self.quarter // 2, self.quarter % 2, self.y]
        want = [k // 4, (k // 2) % 2, k % 2]
        a, b, y = (u + w - 2 * u * w for u, w in zip(bits, want))
        quarter = 2 * a + b
        device = {"item": self.group * SPREAD + quarter, "head": 2 * y + self.core}
        return 2 * quarter + y, device

    def other(self, k):
        return (self.item + k) % self.count

    def barrier(self):
        sem = pltpu.get_barrier_semaphore()
        peers = [{"item": self.other(k), "head": self.head} for k in range(1, self.count)]
        peers += [self.sibling, self.across]
        peers += [self.member(k)[1] for k in (3, 5, 7)]
        for peer in peers:
            pl.semaphore_signal(sem, inc=1, device_id=peer, device_id_type=MESH)
        pl.semaphore_wait(sem, len(peers))

    def send(self, src, dst, device):
        copy = pltpu.make_async_remote_copy(
            src_ref=src,
            dst_ref=dst,
            send_sem=self.sems.at[self.used],
            recv_sem=self.sems.at[self.used + 1],
            device_id=device,
            device_id_type=MESH,
        )
        self.used += 2
        copy.start()
        self.sent.append(copy)
        return copy

    def local(self, src, dst):
        copy = pltpu.make_async_copy(src, dst, self.sems.at[self.used])
        self.used += 1
        copy.start()
        return copy

    def settle(self, copy):
        copy.wait_send()
        self.sent = [other for other in self.sent if other is not copy]

    def drain(self):
        for copy in self.sent:
            copy.wait_send()


class Pump:
    def __init__(self, steps):
        self.steps = list(steps)
        self.at = 0

    def __call__(self, count=None):
        end = len(self.steps) if count is None else min(self.at + count, len(self.steps))
        while self.at < end:
            self.steps[self.at]()
            self.at += 1


class GatherPipe:
    def __init__(self, place, source, target, way):
        self.place, self.target, self.way = place, target, way
        self.device = {"item": place.ring(place.spot + way), "head": place.head}
        self.copy = place.send(source, target(place.item), self.device)

    def step(self, s):
        self.copy.wait_recv()
        if s < self.place.count - 1:
            part = self.target(self.place.ring(self.place.spot - self.way * s))
            self.copy = self.place.send(part, part, self.device)


class ScatterPipe:
    def __init__(self, place, part, slots, finish, way):
        self.place, self.part, self.slots, self.finish, self.way = place, part, slots, finish, way
        self.device = {"item": place.ring(place.spot + way), "head": place.head}
        self.copy = place.send(part(place.ring(place.spot - way)), slots.at[0], self.device)

    def step(self, s):
        self.copy.wait_recv()
        if s < self.place.count - 2:
            own = self.part(self.place.ring(self.place.spot - self.way * (s + 2)))
            self.slots[s] = (self.slots[s].astype(F32) + own[...].astype(F32)).astype(BF)
            self.copy = self.place.send(self.slots.at[s], self.slots.at[s + 1], self.device)
        else:
            self.finish(self.slots[s].astype(F32) + self.part(self.place.item)[...].astype(F32))


def weave(*pipes, steps):
    return [functools.partial(pipe.step, s) for s in steps for pipe in pipes]


class HeadGather:
    def __init__(self, place, ref):
        self.place, self.ref = place, ref
        own = ref.at[place.y, place.core]
        self.near = place.send(own, own, place.sibling)
        self.far = place.send(own, own, place.across)

    def forward(self):
        place = self.place
        self.far.wait_recv()
        block = self.ref.at[1 - place.y, place.core]
        self.passed = place.send(block, block, place.sibling)

    def finish(self):
        self.near.wait_recv()
        self.passed.wait_recv()


class HeadScatter:
    def __init__(self, place, part, near, far):
        self.place, self.part, self.near, self.far = place, part, near, far
        self.copy = place.send(part.at[:, 1 - place.core], near, place.sibling)

    def forward(self):
        place, part, near = self.place, self.part, self.near
        self.copy.wait_recv()
        block = part.at[1 - place.y, place.core]
        block[...] = (block[...].astype(F32) + near[1 - place.y].astype(F32)).astype(BF)
        self.copy = place.send(block, self.far, place.across)

    def finish(self):
        place = self.place
        own = self.part[place.y, place.core].astype(F32) + self.near[place.y].astype(F32)
        self.copy.wait_recv()
        return own + self.far[...].astype(F32)


class GroupGather:
    def __init__(self, place, ref):
        self.place, self.ref = place, ref
        own = ref.at[place.core, place.chip]
        self.copies = [place.send(own, own, place.member(k)[1]) for k in range(1, 2 * SPREAD)]
        self.passed = [place.send(own, own, place.sibling)]

    def forward(self, k):
        self.copies[k - 1].wait_recv()
        block = self.ref.at[self.place.core, self.place.member(k)[0]]
        self.passed.append(self.place.send(block, block, self.place.sibling))

    def steps(self):
        return [functools.partial(self.forward, k) for k in range(1, 2 * SPREAD)]

    def finish(self):
        for copy in self.passed:
            copy.wait_recv()


class GroupScatter:
    def __init__(self, place, part, kept, near, far):
        self.place, self.kept, self.near, self.far = place, kept, near, far
        self.copy = place.send(part.at[1 - place.core], near, place.sibling)
        self.load = place.local(part.at[place.core], kept)

    def forward(self):
        place, kept, near = self.place, self.kept, self.near
        self.load.wait()
        self.copy.wait_recv()
        self.copies = []
        for k in range(1, 2 * SPREAD):
            chip, device = place.member(k)
            kept[chip] = (kept[chip].astype(F32) + near[chip].astype(F32)).astype(BF)
            self.copies.append(place.send(kept.at[chip], self.far.at[k - 1], device))

    def finish(self):
        chip = self.place.chip
        total = self.kept[chip].astype(F32) + self.near[chip].astype(F32)
        for k, copy in enumerate(self.copies):
            copy.wait_recv()
            total = total + self.far[k].astype(F32)
        return total


def head_masks(rows, columns):
    lane = lax.broadcasted_iota(jnp.int32, (rows, columns), 1)
    return [(lane >= at) & (lane < at + HEAD_DIM) for at in range(0, columns, HEAD_DIM)]


def stack_heads(block, masks):
    zero = jnp.zeros_like(block)
    return jnp.concatenate([jnp.where(mask, block, zero) for mask in masks], axis=0)


def fold_heads(block, masks):
    rows = masks[0].shape[0]
    total = 0.0
    for h, mask in enumerate(masks):
        total = total + jnp.where(mask, block[h * rows : (h + 1) * rows], 0.0)
    return total


def norm_parts(rows):
    mean = jnp.mean(rows, axis=-1, keepdims=True)
    centered = rows - mean
    inverse = lax.rsqrt(jnp.mean(centered * centered, axis=-1, keepdims=True) + EPS)
    return centered * inverse, inverse


def norm_back(upstream, rows, gain):
    normed, inverse = norm_parts(rows)
    scaled = upstream * gain
    first = jnp.mean(scaled, axis=-1, keepdims=True)
    second = jnp.mean(scaled * normed, axis=-1, keepdims=True)
    return (
        inverse * (scaled - first - normed * second),
        jnp.sum(upstream * normed, axis=0, keepdims=True),
        jnp.sum(upstream, axis=0, keepdims=True),
    )


def gelu_parts(x):
    root = 0.7978845608028654
    t = jnp.tanh(root * (x + 0.044715 * (x * x * x)))
    half = 0.5 * (1.0 + t)
    return x * half, half + 0.5 * x * (1.0 - t * t) * (root * (1.0 + 3 * 0.044715 * (x * x)))


def window(width, k):
    return (width * k) // 128 * 128


def forward_kernel(
    count,
    small_in, frames_ref, media, latents, cotangent, w_query, w_key, w_value, w_output, w_up, w_down,
    o_joined, o_kv, o_query, o_weights, o_mixed, o_latent, o_wkv, o_wquery, o_woutput,
    o_back, o_out, o_gup, o_gdown, o_middle, o_small,
    joined, kv, query, weights, mixed, latent, wkv, wq, wo, up, down,
    tokens, upstream, pre, act, gpre, back, out, gup, gdown, middle, small, smalls, att, att_near, att_far,
    sems,
):
    place = Place(count, sems)
    items, local_media, width = media.shape
    local_latents = latents.shape[1]
    rows = local_media + local_latents
    keys_count = 4 * rows
    columns = w_query.shape[1]
    part = w_query.shape[0] // 2
    latent_count = 4 * local_latents
    item, y, core = place.item, place.y, place.core
    place.barrier()

    def pipes(source, slab, lanes):
        made = []
        for half, way in ((0, 1), (1, -1)):
            span = pl.ds(half * part, part)
            made.append(
                GatherPipe(place, source.at[span], lambda o, span=span: slab.at[o, span, lanes], way)
            )
        return made

    whole, second = pl.ds(0, columns), pl.ds(columns, columns)
    kv_pipes = pipes(w_key, wkv, whole) + pipes(w_value, wkv, second)
    own_small = place.local(small_in, smalls.at[item])
    small_copies = [
        place.send(small_in, smalls.at[item], {"item": place.other(k), "head": place.head})
        for k in range(1, count)
    ]
    hidden = up.shape[2]
    quarter = pl.ds(pl.multiple_of(place.quarter * hidden, 128), hidden)
    owns = [
        place.local(w_key, wkv.at[item, :, whole]),
        place.local(w_value, wkv.at[item, :, second]),
        place.local(w_query, wq.at[item]),
        place.local(w_output, wo.at[item]),
    ]
    own_hidden = [
        place.local(w_up.at[:, quarter], up.at[item]),
        place.local(w_down.at[:, quarter], down.at[item]),
    ]

    own_small.wait()
    for copy in small_copies:
        copy.wait_recv()
    small[...] = jnp.zeros_like(small)
    for j in range(count):
        lanes = pl.ds(window(width // count, j), smalls.shape[2])
        small[:, lanes] += smalls[j].astype(F32)
    local_frames = local_media // P_SIZE
    time_rows = [small[pl.ds(6 + place.head * local_frames + f, 1), :] for f in range(local_frames)]

    gathers = []
    for b in range(items):
        for f in range(local_frames):
            span = pl.ds(f * P_SIZE, P_SIZE)
            normed, _ = norm_parts(media[b, span].astype(F32) + time_rows[f])
            joined[b, y, core, span] = (normed * small[0:1] + small[1:2]).astype(BF)
        normed, _ = norm_parts(latents[b].astype(F32))
        joined[b, y, core, pl.ds(local_media, local_latents)] = (
            normed * small[2:3] + small[3:4]
        ).astype(BF)
        gathers.append(HeadGather(place, joined.at[b]))

    ring = Pump(weave(*kv_pipes, steps=range(1, count)))

    def project(b):
        gathers[b].finish()
        kv[b] = dot(joined[b].reshape(keys_count, width), wkv[...].reshape(width, 2 * columns), 1, 0).astype(BF)
        for p in range(4):
            latent[p, pl.ds(b * local_latents, local_latents)] = joined[
                b, p // 2, p % 2, pl.ds(local_media, local_latents)
            ]

    ring(12)
    gathers[0].forward()
    ring(12)
    gathers[1].forward()
    qo_pipes = pipes(w_query, wq, whole) + pipes(w_output, wo, whole)
    ring()
    owns[0].wait()
    owns[1].wait()
    ring = Pump(weave(*qo_pipes, steps=range(1, count)))
    project(0)
    ring(4)
    project(1)
    ring(4)
    gathers[2].forward()
    ring(8)
    project(2)
    ring(4)
    gathers[3].forward()
    ring()
    owns[2].wait()
    owns[3].wait()

    def spread(source, slab):
        copies = []
        for k in (4, 3, 5, 2, 6, 1, 7):
            to = place.other(k)
            lanes = pl.ds(pl.multiple_of((to % SPREAD) * hidden, 128), hidden)
            copies.append(
                place.send(source.at[:, lanes], slab.at[item], {"item": to, "head": place.head})
            )
        return copies

    up_copies = spread(w_up, up)
    down_copies = spread(w_down, down)

    project(3)
    scale = HEAD_DIM ** (-0.5)
    query[...] = (
        (scale * dot(latent[...].reshape(4 * items * local_latents, width), wq[...].reshape(width, columns), 1, 0))
        .astype(BF)
        .reshape(query.shape)
    )
    keeps = [
        place.local(joined, o_joined),
        place.local(kv, o_kv),
        place.local(query, o_query),
        place.local(latent, o_latent),
        place.local(wkv, o_wkv),
        place.local(wq, o_wquery),
        place.local(wo, o_woutput),
        place.local(small, o_small),
    ]
    masks = head_masks(latent_count, columns)
    index = lax.broadcasted_iota(jnp.int32, (1, keys_count), 1)
    local = index % rows
    frame = jnp.where(local < local_media, (index // rows) * local_frames + local // P_SIZE, -1)
    for b in range(items):
        mine = pl.ds(b * local_latents, local_latents)
        stacked = stack_heads(query[:, mine].reshape(latent_count, columns), masks)
        scores = dot(stacked, kv[b, :, :columns], 1, 1)
        shown = jnp.broadcast_to(frame, scores.shape) < frames_ref[b]
        scores = jnp.where(shown, scores, -1e30)
        expo = jnp.exp(scores - jnp.max(scores, axis=1, keepdims=True))
        weight = expo / jnp.sum(expo, axis=1, keepdims=True)
        weights[b] = weight
        result = fold_heads(dot(weight.astype(BF), kv[b, :, columns:], 1, 0), masks)
        mixed[:, mine] = result.astype(BF).reshape(4, local_latents, columns)
    att[...] = (
        dot(mixed[...].reshape(4 * items * local_latents, columns), wo[...].reshape(width, columns), 1, 1)
        .astype(BF)
        .reshape(att.shape)
    )
    keeps += [place.local(weights, o_weights), place.local(mixed, o_mixed)]
    scatter = HeadScatter(place, att, att_near, att_far)
    scatter.forward()
    middle[...] = latents[...].astype(F32).reshape(middle.shape) + scatter.finish()
    normed, _ = norm_parts(middle[...])
    tokens[core, place.chip] = (normed * small[4:5] + small[5:6]).astype(BF)
    token_gather = GroupGather(place, tokens)
    keeps.append(place.local(middle, o_middle))
    upstream[core, place.chip] = cotangent[...].reshape(middle.shape)
    upstream_gather = GroupGather(place, upstream)
    for step in token_gather.steps() + upstream_gather.steps():
        step()
    token_gather.finish()
    for copy in own_hidden:
        copy.wait()
    for copy in up_copies:
        copy.wait_recv()
    blocks = 4
    size = 2 * SPREAD * 2 // blocks

    def block(ref, n):
        return ref[n // 2, pl.ds((n % 2) * size, size)].reshape(-1, width)

    tall = tokens.shape[2] * size
    for n in range(blocks):
        span = pl.ds(n * tall, tall)
        pre[span] = dot(block(tokens, n), up[...].reshape(width, hidden), 1, 0)
    upstream_gather.finish()
    for copy in down_copies:
        copy.wait_recv()
    for n in range(blocks):
        span = pl.ds(n * tall, tall)
        value, slope = gelu_parts(pre[span])
        act[span] = value.astype(BF)
        grad_act = dot(block(upstream, n), down[...].reshape(width, hidden), 1, 0)
        gpre[span] = (grad_act * slope).astype(BF)
        where = (n // 2, pl.ds((n % 2) * size, size))
        shape = (size, tokens.shape[2], width)
        back[where] = dot(gpre[span], up[...].reshape(width, hidden), 1, 1).astype(BF).reshape(shape)
        out[where] = dot(act[span], down[...].reshape(width, hidden), 1, 1).astype(BF).reshape(shape)
    keeps += [place.local(back, o_back), place.local(out, o_out)]
    tile = 2 * part * 2
    for t in range(width // tile):
        span = pl.ds(t * tile, tile)
        owners = pl.ds(2 * t, 2)
        shape = (2, 2 * part, hidden)
        gup[owners] = (
            dot(tokens[:, :, :, span].reshape(-1, tile), gpre[...], 0, 0).astype(BF).reshape(shape)
        )
        gdown[owners] = (
            dot(upstream[:, :, :, span].reshape(-1, tile), act[...], 0, 0).astype(BF).reshape(shape)
        )
    keeps += [place.local(gup, o_gup), place.local(gdown, o_gdown)]
    place.drain()
    for copy in keeps:
        copy.wait()


def backward_kernel(
    count,
    media, latents, cotangent, middle, small,
    i_joined, i_kv, i_query, i_weights, i_mixed, i_latent, i_wkv, i_wquery, i_woutput,
    i_back, i_out, i_gup, i_gdown,
    o_out, o_lgrad, o_media, o_query, o_key, o_value, o_output, o_up, o_down, o_small,
    joined, kv, query, weights, mixed, latent, wkv, wq, wo,
    gmiddle, kept, near, far, out_far, gatt, gmixed, gquery, total, gkv, gq, go,
    slots, up_in, down_in, m_near, m_far, mstage, sums, sum_in, sum_near, sum_far,
    sems,
):
    place = Place(count, sems)
    items, local_media, width = media.shape
    local_latents = latents.shape[1]
    rows = local_media + local_latents
    keys_count = 4 * rows
    columns = wq.shape[2]
    block_rows = wq.shape[1]
    part = block_rows // 2
    latent_count = 4 * local_latents
    all_latents = items * latent_count
    hidden = up_in.shape[2]
    item, y, core = place.item, place.y, place.core
    local_frames = local_media // P_SIZE
    scale = HEAD_DIM ** (-0.5)
    place.barrier()

    back_scatter = GroupScatter(place, i_back, kept, near, far)

    def spread(source, slab):
        copies = []
        for k in (4, 3, 5, 2, 6, 1, 7):
            to = place.other(k)
            copies.append(
                place.send(source.at[to], slab.at[item], {"item": to, "head": place.head})
            )
        return copies, place.local(source.at[item], slab.at[item])

    loads = {}
    for name, src, dst in (
        ("wo", i_woutput, wo), ("mixed", i_mixed, mixed), ("query", i_query, query), ("kv", i_kv, kv),
        ("weights", i_weights, weights), ("joined", i_joined, joined), ("wkv", i_wkv, wkv),
        ("latent", i_latent, latent), ("wq", i_wquery, wq),
    ):
        loads[name] = place.local(src, dst)
    back_scatter.forward()
    up_copies, up_own = spread(i_gup, up_in)
    down_copies, down_own = spread(i_gdown, down_in)
    sums[...] = jnp.zeros_like(sums)

    grad_norm = back_scatter.finish()
    dx, dg, db = norm_back(grad_norm, middle[...], small[4:5])
    sums[4:5] = dg
    sums[5:6] = db
    grad_middle = cotangent[...].astype(F32).reshape(middle.shape) + dx
    gmiddle[...] = grad_middle
    gatt[y, core] = grad_middle.astype(BF)
    att_gather = HeadGather(place, gatt)
    att_gather.forward()
    att_gather.finish()
    loads["wo"].wait()
    loads["mixed"].wait()
    upstream = gatt[...].reshape(all_latents, width)
    gmixed[...] = dot(upstream, wo[...].reshape(width, columns), 1, 0).astype(BF).reshape(gmixed.shape)
    tile = 2 * block_rows
    for t in range(width // tile):
        span = pl.ds(t * tile, tile)
        go[pl.ds(2 * t, 2)] = (
            dot(gatt[:, :, :, span].reshape(all_latents, tile), mixed[...].reshape(all_latents, columns), 0, 0)
            .astype(BF)
            .reshape(2, block_rows, columns)
        )

    def pipes(first_slot, slab, lanes, result):
        made = []
        for half, way in ((0, 1), (1, -1)):
            span = pl.ds(half * part, part)

            def finish(value, span=span):
                result[span] = value

            made.append(
                ScatterPipe(
                    place,
                    lambda o, span=span: slab.at[o, span, lanes],
                    slots.at[first_slot + half],
                    finish,
                    way,
                )
            )
        return made

    whole, second = pl.ds(0, columns), pl.ds(columns, columns)
    ring = Pump(weave(*pipes(0, go, whole, o_output), steps=range(count - 1)))

    masks = head_masks(latent_count, columns)
    loads["query"].wait()
    loads["kv"].wait()
    loads["weights"].wait()
    loads["joined"].wait()
    loads["wkv"].wait()
    loads["wq"].wait()
    scatters = []
    tile = 2 * block_rows
    for b in range(items):
        mine = pl.ds(b * local_latents, local_latents)
        q_stack = stack_heads(query[:, mine].reshape(latent_count, columns), masks)
        g_stack = stack_heads(gmixed[:, mine].reshape(latent_count, columns), masks)
        weight = weights[b]
        grad_weight = dot(g_stack, kv[b, :, columns:], 1, 1)
        inner = jnp.sum(weight * grad_weight, axis=1, keepdims=True)
        grad_score = (weight * (grad_weight - inner)).astype(BF)
        gq_rows = fold_heads(dot(grad_score, kv[b, :, :columns], 1, 0), masks).astype(BF)
        gquery[:, mine] = gq_rows.reshape(4, local_latents, columns)
        kv[b, :, :columns] = dot(grad_score, q_stack, 0, 0).astype(BF)
        kv[b, :, columns:] = dot(weight.astype(BF), g_stack, 0, 0).astype(BF)
        for t in range(width // tile):
            span = pl.ds(t * tile, tile)
            value = dot(joined[b, :, :, :, span].reshape(keys_count, tile), kv[b], 0, 0)
            if b > 0:
                value = value + total[span]
            if b < items - 1:
                total[span] = value
            else:
                gkv[pl.ds(2 * t, 2)] = value.astype(BF).reshape(2, block_rows, 2 * columns)
        for t in range(width // tile):
            span = pl.ds(t * tile, tile)
            owners = pl.ds(2 * t, 2)
            value = dot(kv[b], wkv[owners].reshape(tile, 2 * columns), 1, 1)
            extra = scale * dot(gq_rows, wq[owners].reshape(tile, columns), 1, 1)
            for p in range(4):
                at = p * rows
                joined[b, p // 2, p % 2, pl.ds(0, local_media), span] = value[at : at + local_media].astype(BF)
                joined[b, p // 2, p % 2, pl.ds(local_media, local_latents), span] = (
                    value[at + local_media : at + rows] + extra[p * local_latents : (p + 1) * local_latents]
                ).astype(BF)
        scatters.append(HeadScatter(place, joined.at[b], m_near.at[b], m_far.at[b]))
        if b > 0:
            scatters[b - 1].forward()
        ring(3)
    kv_pipes = pipes(2, gkv, whole, o_key) + pipes(4, gkv, second, o_value)
    loads["latent"].wait()
    for t in range(width // tile):
        span = pl.ds(t * tile, tile)
        gq[pl.ds(2 * t, 2)] = (
            (scale * dot(latent[:, :, span].reshape(all_latents, tile), gquery[...].reshape(all_latents, columns), 0, 0))
            .astype(BF)
            .reshape(2, block_rows, columns)
        )
    scatters[-1].forward()
    ring()
    q_pipes = pipes(6, gq, whole, o_query)
    ring = Pump(weave(*kv_pipes, *q_pipes, steps=range(count - 1)))
    ring(6)

    for copy in back_scatter.copies:
        place.settle(copy)
    out_scatter = GroupScatter(place, i_out, kept, near, out_far)
    out_scatter.forward()
    ring(6)

    time_rows = [small[pl.ds(6 + place.head * local_frames + f, 1), :] for f in range(local_frames)]
    stores = []
    for b in range(items):
        grad = scatters[b].finish()
        if b >= 2:
            stores[b - 2].wait()
        for f in range(local_frames):
            span = slice(f * P_SIZE, (f + 1) * P_SIZE)
            dx, dg, db = norm_back(grad[span], media[b, span].astype(F32) + time_rows[f], small[0:1])
            mstage[b % 2, span] = dx
            sums[0:1] += dg
            sums[1:2] += db
            sums[pl.ds(6 + place.head * local_frames + f, 1), :] += jnp.sum(dx, axis=0, keepdims=True)
        stores.append(place.local(mstage.at[b % 2], o_media.at[b]))
        dx, dg, db = norm_back(grad[local_media:], latents[b].astype(F32), small[2:3])
        sums[2:3] += dg
        sums[3:4] += db
        o_lgrad[b] = gmiddle[pl.ds(b * local_latents, local_latents)] + dx
        ring(8)

    lanes = sum_in.shape[2]
    sum_copies = []
    for k in range(1, count):
        to = place.other(k)
        at = pl.multiple_of(window(width // count, to), 128)
        sum_copies.append(
            place.send(sums.at[:, pl.ds(at, lanes)], sum_in.at[item], {"item": to, "head": place.head})
        )
    o_out[...] = (middle[...] + out_scatter.finish()).astype(BF).reshape(o_out.shape)
    sum_in[item] = sums[:, pl.ds(pl.multiple_of(window(width // count, item), 128), lanes)]
    for copy in sum_copies:
        copy.wait_recv()
    value = jnp.sum(sum_in[...], axis=0)
    sum_in[0] = value
    copy = place.send(sum_in.at[0], sum_near, place.sibling)
    copy.wait_recv()
    value = value + sum_near[...]
    sum_in[1] = value
    copy = place.send(sum_in.at[1], sum_far, place.across)
    ring()
    for copies, own, slab, result in ((up_copies, up_own, up_in, o_up), (down_copies, down_own, down_in, o_down)):
        own.wait()
        for c in copies:
            c.wait_recv()
        for k in range(SPREAD):
            grad = slab[k].astype(F32)
            for group in range(1, count // SPREAD):
                grad = grad + slab[group * SPREAD + k].astype(F32)
            result[:, pl.ds(k * hidden, hidden)] = grad
    copy.wait_recv()
    o_small[...] = value + sum_far[...]
    place.drain()
    for store in stores[-2:]:
        store.wait()


def kernel_step(
    count, media, latents, cotangent, frame_counts,
    query_weight, key_weight, value_weight, output_weight, up_weight, down_weight,
    media_gain, media_bias, latent_gain, latent_bias, ffn_gain, ffn_bias, time_embed,
):
    items, local_media, width = media.shape
    local_latents = latents.shape[1]
    frames = time_embed.shape[0]
    block_rows, columns = query_weight.shape
    hidden = up_weight.shape[1] // SPREAD
    rows = local_media + local_latents
    keys_count = 4 * rows
    own_latents = items * local_latents
    stacked = columns // HEAD_DIM * 4 * local_latents
    group = 2 * SPREAD
    shift = block_rows * lax.axis_index("item") - window(block_rows, lax.axis_index("item"))
    vectors = jnp.stack([media_gain, media_bias, latent_gain, latent_bias, ffn_gain, ffn_bias])
    small = lax.dynamic_update_slice(
        jnp.zeros((16, 256), BF), jnp.concatenate([vectors, time_embed]), (0, shift)
    )

    def hbm(*shape, kind=BF):
        return jax.ShapeDtypeStruct(shape, kind)

    def buf(*shape, kind=BF):
        return pltpu.VMEM(shape, kind)

    vmem, anywhere = pl.BlockSpec(memory_space=pltpu.VMEM), pl.BlockSpec(memory_space=pl.ANY)
    big = dict(
        joined=(items, 2, 2, rows, width),
        kv=(items, keys_count, 2 * columns),
        query=(4, own_latents, columns),
        weights=(items, stacked, keys_count),
        mixed=(4, own_latents, columns),
        latent=(4, own_latents, width),
        wkv=(count, block_rows, 2 * columns),
        wq=(count, block_rows, columns),
        wo=(count, block_rows, columns),
    )
    kinds = dict(weights=F32)
    tokens = (2, group, own_latents, width)
    slab = (count, block_rows, hidden)
    kept = forward_results = pl.pallas_call(
        functools.partial(forward_kernel, count),
        out_shape=[hbm(*shape, kind=kinds.get(name, BF)) for name, shape in big.items()]
        + [hbm(*tokens)] * 2
        + [hbm(*slab)] * 2
        + [hbm(own_latents, width, kind=F32), hbm(16, width, kind=F32)],
        in_specs=[vmem, pl.BlockSpec(memory_space=pltpu.SMEM)] + [vmem] * 3 + [anywhere] * 6,
        out_specs=[anywhere] * 15,
        scratch_shapes=[buf(*shape, kind=kinds.get(name, BF)) for name, shape in big.items()]
        + [buf(*slab)] * 2
        + [buf(*tokens)] * 2
        + [
            buf(2 * group * own_latents, hidden, kind=F32),
            buf(2 * group * own_latents, hidden),
            buf(2 * group * own_latents, hidden),
        ]
        + [buf(*tokens)] * 2
        + [buf(*slab)] * 2
        + [
            buf(own_latents, width, kind=F32),
            buf(16, width, kind=F32),
            buf(count, 16, 256),
            buf(2, 2, own_latents, width),
            buf(2, own_latents, width),
            buf(own_latents, width),
            pltpu.SemaphoreType.DMA((320,)),
        ],
        compiler_params=pltpu.CompilerParams(
            collective_id=0, has_side_effects=True, vmem_limit_bytes=60 * 2**20
        ),
        name="gather_forward",
    )(
        small, frame_counts, media, latents, cotangent, query_weight, key_weight, value_weight,
        output_weight, up_weight, down_weight,
    )
    kept = forward_results[:13]
    middle, small = forward_results[13:]
    results = pl.pallas_call(
        functools.partial(backward_kernel, count),
        out_shape=[
            hbm(*latents.shape),
            hbm(*latents.shape, kind=F32),
            hbm(*media.shape, kind=F32),
        ]
        + [hbm(block_rows, columns, kind=F32)] * 4
        + [hbm(block_rows, SPREAD * hidden, kind=F32)] * 2
        + [hbm(16, 256, kind=F32)],
        in_specs=[vmem] * 5 + [anywhere] * 13,
        out_specs=[vmem, vmem, anywhere] + [vmem] * 7,
        scratch_shapes=[buf(*shape, kind=kinds.get(name, BF)) for name, shape in big.items()]
        + [
            buf(own_latents, width, kind=F32),
            buf(group, own_latents, width),
            buf(group, own_latents, width),
            buf(group - 1, own_latents, width),
            buf(group - 1, own_latents, width),
            buf(2, 2, own_latents, width),
            buf(4, own_latents, columns),
            buf(4, own_latents, columns),
            buf(width, 2 * columns, kind=F32),
            buf(count, block_rows, 2 * columns),
            buf(count, block_rows, columns),
            buf(count, block_rows, columns),
            buf(8, count - 1, block_rows // 2, columns),
            buf(*slab),
            buf(*slab),
            buf(items, 2, rows, width),
            buf(items, rows, width),
            buf(2, local_media, width, kind=F32),
            buf(16, width, kind=F32),
            buf(count, 16, 256, kind=F32),
            buf(16, 256, kind=F32),
            buf(16, 256, kind=F32),
            pltpu.SemaphoreType.DMA((320,)),
        ],
        compiler_params=pltpu.CompilerParams(
            collective_id=1, has_side_effects=True, vmem_limit_bytes=62 * 2**20
        ),
        name="backward_scatter",
    )(media, latents, cotangent, middle, small, *kept)
    sums = lax.dynamic_slice(results[9], (0, shift), (6 + frames, block_rows))
    return (*results[:9], *(sums[k] for k in range(6)), sums[6:])


def fits(mesh, media, query_weight, up_weight):
    count, heads = mesh.shape["item"], mesh.shape["head"]
    width, columns = query_weight.shape[0], query_weight.shape[1] // heads
    hidden = up_weight.shape[1] // heads
    block_rows = width // count
    return (
        heads == 4
        and count == 2 * SPREAD
        and block_rows % 64 == 0
        and columns % 128 == 0
        and hidden % (128 * SPREAD) == 0
    )


def solution(mesh):
    rows = P("item", "head", None)
    block = P("item", "head")
    vector = P("item")
    table = P(None, "item")

    def run(*arrays):
        count = mesh.shape["item"]
        step = plain_step
        if fits(mesh, arrays[0], arrays[4], arrays[8]):
            step = functools.partial(kernel_step, count)
        return jax.shard_map(
            step,
            mesh=mesh,
            in_specs=(rows,) * 3 + (vector,) + (block,) * 6 + (vector,) * 6 + (table,),
            out_specs=(rows,) * 3 + (block,) * 6 + (vector,) * 6 + (table,),
            check_vma=False,
        )(*arrays)

    return run
```

```python
import functools

import jax
import jax.numpy as jnp
from jax import lax
from jax.experimental import pallas as pl
from jax.experimental.pallas import tpu as pltpu
from jax.sharding import PartitionSpec as P

HEAD_DIM = 96
P_SIZE = 64
EPS = 1e-05
BF = jnp.bfloat16
F32 = jnp.float32


def norm_forward(rows, gain, bias):
    mean = jnp.mean(rows, axis=-1, keepdims=True)
    centered = rows - mean
    inverse = lax.rsqrt(jnp.mean(centered * centered, axis=-1, keepdims=True) + EPS)
    normed = centered * inverse
    return normed * gain + bias, normed, inverse


def norm_backward(upstream, normed, inverse, gain):
    scaled = upstream * gain
    first = jnp.mean(scaled, axis=-1, keepdims=True)
    second = jnp.mean(scaled * normed, axis=-1, keepdims=True)
    axes = tuple(range(upstream.ndim - 1))
    return (
        inverse * (scaled - first - normed * second),
        jnp.sum(upstream * normed, axis=axes),
        jnp.sum(upstream, axis=axes),
    )


def dot(left, right, a, b):
    return lax.dot_general(left, right, (((a,), (b,)), ((), ())), preferred_element_type=F32)


def gather_rows(rows):
    return lax.all_gather(rows, "head", axis=1, tiled=True)


def scatter_rows(rows):
    return lax.psum_scatter(rows.astype(BF), "head", scatter_dimension=1, tiled=True).astype(F32)


def item_scatter(grad):
    return lax.psum_scatter(grad.astype(BF), "item", scatter_dimension=0, tiled=True).astype(F32)


def plain_step(
    media, latents, cotangent, frame_counts,
    query_weight, key_weight, value_weight, output_weight, up_weight, down_weight,
    media_gain, media_bias, latent_gain, latent_bias, ffn_gain, ffn_bias, time_embed,
):
    items, local_media, width = media.shape
    frames = time_embed.shape[0]
    local_frames = local_media // P_SIZE
    place = lax.axis_index("head")
    scale = HEAD_DIM ** (-0.5)
    small = jnp.concatenate(
        [jnp.stack([media_gain, media_bias, latent_gain, latent_bias, ffn_gain, ffn_bias]), time_embed]
    )
    small = lax.all_gather(small, "item", axis=1, tiled=True).astype(F32)
    g_media, b_media, g_latent, b_latent, g_ffn, b_ffn = (small[k] for k in range(6))
    time_rows = lax.dynamic_slice_in_dim(small[6:], place * local_frames, local_frames, 0)
    w_query, w_key, w_value, w_output, w_up, w_down = (
        lax.all_gather(w, "item", axis=0, tiled=True)
        for w in (query_weight, key_weight, value_weight, output_weight, up_weight, down_weight)
    )
    shifted = (
        media.astype(F32).reshape(items, local_frames, P_SIZE, width) + time_rows[None, :, None, :]
    ).reshape(media.shape)
    media_norm, media_hat, media_inv = norm_forward(shifted, g_media, b_media)
    latent_f = latents.astype(F32)
    latent_norm, latent_hat, latent_inv = norm_forward(latent_f, g_latent, b_latent)
    media_all = gather_rows(media_norm.astype(BF))
    latent_all = gather_rows(latent_norm.astype(BF))
    upstream = gather_rows(cotangent)
    media_count, latent_count = media_all.shape[1], latent_all.shape[1]
    joined = jnp.concatenate([media_all, latent_all], axis=1)
    key_count = joined.shape[1]
    local_heads = w_query.shape[1] // HEAD_DIM
    query = (scale * dot(latent_all, w_query, 2, 0)).astype(BF)
    keys = dot(joined, w_key, 2, 0).astype(BF)
    values = dot(joined, w_value, 2, 0).astype(BF)
    query_h = query.reshape(items, latent_count, local_heads, HEAD_DIM)
    key_h = keys.reshape(items, key_count, local_heads, HEAD_DIM)
    value_h = values.reshape(items, key_count, local_heads, HEAD_DIM)
    index = jnp.arange(key_count, dtype=jnp.int32)
    valid = (index[None, :] // P_SIZE < frame_counts[:, None]) | (index[None, :] >= media_count)
    valid = valid[:, None, None, :]

    def mix(spec, left, right):
        return jnp.einsum(spec, left, right, preferred_element_type=F32)

    scores = jnp.where(valid, mix("blhe,bnhe->bhln", query_h, key_h), -1e30)
    peak = jnp.max(scores, axis=-1, keepdims=True)
    expo = jnp.exp(scores - peak)
    weights = expo / jnp.sum(expo, axis=-1, keepdims=True)
    weights_low = weights.astype(BF)
    mixed = mix("bhln,bnhe->blhe", weights_low, value_h).reshape(items, latent_count, -1).astype(BF)
    middle = latent_f + scatter_rows(dot(mixed, w_output, 2, 1))
    ffn_norm, ffn_hat, ffn_inv = norm_forward(middle, g_ffn, b_ffn)
    ffn_all = gather_rows(ffn_norm.astype(BF))
    rows = items * latent_count
    ffn_rows = ffn_all.reshape(rows, width)
    up_rows = upstream.reshape(rows, width)
    pre = dot(ffn_rows, w_up, 1, 0)
    act, gelu_back = jax.vjp(jax.nn.gelu, pre)
    act = act.astype(BF)
    ffn_out = scatter_rows(dot(act, w_down, 1, 1).reshape(items, latent_count, width))
    output = (middle + ffn_out).astype(BF)
    grad_down = dot(up_rows, act, 0, 0)
    grad_pre = gelu_back(dot(up_rows, w_down, 1, 0))[0].astype(BF)
    grad_up = dot(ffn_rows, grad_pre, 0, 0)
    grad_ffn = scatter_rows(dot(grad_pre, w_up, 1, 1).reshape(items, latent_count, width))
    grad_mid, grad_fgain, grad_fbias = norm_backward(grad_ffn, ffn_hat, ffn_inv, g_ffn)
    grad_middle = cotangent.astype(F32) + grad_mid
    attended_grad = gather_rows(grad_middle.astype(BF)).reshape(rows, width)
    grad_output = dot(attended_grad, mixed.reshape(rows, -1), 0, 0)
    grad_mixed = dot(attended_grad, w_output, 1, 0).astype(BF)
    gm_h = grad_mixed.reshape(items, latent_count, local_heads, HEAD_DIM)
    grad_values = mix("bhln,blhe->bnhe", weights_low, gm_h).astype(BF).reshape(items * key_count, -1)
    grad_weights = mix("blhe,bnhe->bhln", gm_h, value_h)
    inner = jnp.sum(weights * grad_weights, axis=-1, keepdims=True)
    grad_scores = (weights * (grad_weights - inner)).astype(BF)
    grad_query = mix("bhln,bnhe->blhe", grad_scores, key_h).astype(BF).reshape(rows, -1)
    grad_keys = mix("bhln,blhe->bnhe", grad_scores, query_h).astype(BF).reshape(items * key_count, -1)
    joined_rows = joined.reshape(items * key_count, width)
    grad_wquery = scale * dot(latent_all.reshape(rows, width), grad_query, 0, 0)
    grad_wkey = dot(joined_rows, grad_keys, 0, 0)
    grad_wvalue = dot(joined_rows, grad_values, 0, 0)
    grad_joined = dot(grad_keys, w_key, 1, 1) + dot(grad_values, w_value, 1, 1)
    grad_joined = grad_joined.reshape(items, key_count, width)
    grad_latent_all = grad_joined[:, media_count:] + scale * dot(grad_query, w_query, 1, 1).reshape(
        items, latent_count, width
    )
    media_back = scatter_rows(grad_joined[:, :media_count])
    latent_back = scatter_rows(grad_latent_all)
    grad_media, grad_mgain, grad_mbias = norm_backward(media_back, media_hat, media_inv, g_media)
    grad_lat, grad_lgain, grad_lbias = norm_backward(latent_back, latent_hat, latent_inv, g_latent)
    time_local = jnp.sum(grad_media.reshape(items, local_frames, P_SIZE, width), axis=(0, 2))
    grad_time = lax.dynamic_update_slice_in_dim(
        jnp.zeros((frames, width), F32), time_local, place * local_frames, 0
    )
    smalls = jnp.concatenate(
        [jnp.stack([grad_mgain, grad_mbias, grad_lgain, grad_lbias, grad_fgain, grad_fbias]), grad_time]
    )
    smalls = lax.psum_scatter(smalls, ("item",), scatter_dimension=1, tiled=True)
    smalls = lax.psum(smalls, "head")
    return (
        output,
        grad_middle + grad_lat,
        grad_media,
        *(item_scatter(g) for g in (grad_wquery, grad_wkey, grad_wvalue, grad_output, grad_up, grad_down)),
        *(smalls[k] for k in range(6)),
        smalls[6:],
    )


MESH = pl.DeviceIdType.MESH
VMEM = pltpu.VMEM
ANY = pl.ANY
SPREAD = 4


class Place:
    def __init__(self, count, sems):
        self.count = count
        self.sems = sems
        self.used = 0
        self.sent = []
        i, h = lax.axis_index("item"), lax.axis_index("head")
        self.item, self.head = i, h
        self.y, self.core = h // 2, h % 2
        self.quarter = i % SPREAD
        self.group = i // SPREAD
        odd = i % 2
        self.spot = (1 - odd) * (i // 2) + odd * (count - 1 - i // 2)
        self.sibling = {"item": i, "head": 2 * self.y + 1 - self.core}
        self.across = {"item": i, "head": 2 * (1 - self.y) + self.core}
        self.chip = 2 * self.quarter + self.y

    def ring(self, spot):
        spot = (spot + self.count) % self.count
        back = spot // (self.count // 2)
        return (1 - back) * 2 * spot + back * (2 * (self.count - 1 - spot) + 1)

    def member(self, k):
        bits = [self.quarter // 2, self.quarter % 2, self.y]
        want = [k // 4, (k // 2) % 2, k % 2]
        a, b, y = (u + w - 2 * u * w for u, w in zip(bits, want))
        quarter = 2 * a + b
        device = {"item": self.group * SPREAD + quarter, "head": 2 * y + self.core}
        return 2 * quarter + y, device

    def other(self, k):
        return (self.item + k) % self.count

    def barrier(self):
        sem = pltpu.get_barrier_semaphore()
        peers = [{"item": self.other(k), "head": self.head} for k in range(1, self.count)]
        peers += [self.sibling, self.across]
        peers += [self.member(k)[1] for k in (3, 5, 7)]
        for peer in peers:
            pl.semaphore_signal(sem, inc=1, device_id=peer, device_id_type=MESH)
        pl.semaphore_wait(sem, len(peers))

    def send(self, src, dst, device):
        copy = pltpu.make_async_remote_copy(
            src_ref=src,
            dst_ref=dst,
            send_sem=self.sems.at[self.used],
            recv_sem=self.sems.at[self.used + 1],
            device_id=device,
            device_id_type=MESH,
        )
        self.used += 2
        copy.start()
        self.sent.append(copy)
        return copy

    def local(self, src, dst):
        copy = pltpu.make_async_copy(src, dst, self.sems.at[self.used])
        self.used += 1
        copy.start()
        return copy

    def settle(self, copy):
        copy.wait_send()
        self.sent = [other for other in self.sent if other is not copy]

    def drain(self):
        for copy in self.sent:
            copy.wait_send()


class Pump:
    def __init__(self, steps):
        self.steps = list(steps)
        self.at = 0

    def __call__(self, count=None):
        end = len(self.steps) if count is None else min(self.at + count, len(self.steps))
        while self.at < end:
            self.steps[self.at]()
            self.at += 1


class GatherPipe:
    def __init__(self, place, source, target, way):
        self.place, self.target, self.way = place, target, way
        self.device = {"item": place.ring(place.spot + way), "head": place.head}
        self.copy = place.send(source, target(place.item), self.device)

    def step(self, s):
        self.copy.wait_recv()
        if s < self.place.count - 1:
            part = self.target(self.place.ring(self.place.spot - self.way * s))
            self.copy = self.place.send(part, part, self.device)


class ScatterPipe:
    def __init__(self, place, part, slots, finish, way):
        self.place, self.part, self.slots, self.finish, self.way = place, part, slots, finish, way
        self.device = {"item": place.ring(place.spot + way), "head": place.head}
        self.copy = place.send(part(place.ring(place.spot - way)), slots.at[0], self.device)

    def step(self, s):
        self.copy.wait_recv()
        if s < self.place.count - 2:
            own = self.part(self.place.ring(self.place.spot - self.way * (s + 2)))
            self.slots[s] = (self.slots[s].astype(F32) + own[...].astype(F32)).astype(BF)
            self.copy = self.place.send(self.slots.at[s], self.slots.at[s + 1], self.device)
        else:
            self.finish(self.slots[s].astype(F32) + self.part(self.place.item)[...].astype(F32))


def weave(*pipes, steps):
    return [functools.partial(pipe.step, s) for s in steps for pipe in pipes]


class HeadGather:
    def __init__(self, place, ref):
        self.place, self.ref = place, ref
        own = ref.at[place.y, place.core]
        self.near = place.send(own, own, place.sibling)
        self.far = place.send(own, own, place.across)

    def forward(self):
        place = self.place
        self.far.wait_recv()
        block = self.ref.at[1 - place.y, place.core]
        self.passed = place.send(block, block, place.sibling)

    def finish(self):
        self.near.wait_recv()
        self.passed.wait_recv()


class HeadScatter:
    def __init__(self, place, part, near, far):
        self.place, self.part, self.near, self.far = place, part, near, far
        self.copy = place.send(part.at[:, 1 - place.core], near, place.sibling)

    def forward(self):
        place, part, near = self.place, self.part, self.near
        self.copy.wait_recv()
        block = part.at[1 - place.y, place.core]
        block[...] = (block[...].astype(F32) + near[1 - place.y].astype(F32)).astype(BF)
        self.copy = place.send(block, self.far, place.across)

    def finish(self):
        place = self.place
        own = self.part[place.y, place.core].astype(F32) + self.near[place.y].astype(F32)
        self.copy.wait_recv()
        return own + self.far[...].astype(F32)


class GroupGather:
    def __init__(self, place, ref):
        self.place, self.ref = place, ref
        self.copies = {}
        self.passed = []
        self.share(0)

    def block(self, k):
        return self.ref.at[self.place.core, self.place.member(k)[0]]

    def share(self, k):
        self.passed.append(self.place.send(self.block(k), self.block(k), self.place.sibling))

    def push(self, k, *axes):
        for axis in axes:
            self.copies[axis, k] = self.place.send(self.block(k), self.block(k), self.place.member(axis)[1])

    def pull(self, axis, k):
        self.copies[axis, k].wait_recv()
        self.share(axis ^ k)

    def finish(self):
        for copy in self.passed:
            copy.wait_recv()


class GroupScatter:
    def __init__(self, place, part, kept, near, far, order):
        self.place, self.kept, self.near, self.far, self.order = place, kept, near, far, order
        self.copy = place.send(part.at[1 - place.core], near, place.sibling)
        self.load = place.local(part.at[place.core], kept)
        self.copies = {}
        self.arrived = {}

    def total(self, k):
        chip = self.place.member(k)[0]
        value = self.kept[chip].astype(F32) + self.near[chip].astype(F32)
        for axis, slot in self.arrived.get(k, ()):
            self.copies[axis, axis ^ k].wait_recv()
            value = value + self.far[slot].astype(F32)
        return value

    def push(self, axis, k, slot):
        chip = self.place.member(k)[0]
        self.kept[chip] = self.total(k).astype(BF)
        self.copies[axis, k] = self.place.send(
            self.kept.at[chip], self.far.at[slot], self.place.member(axis)[1]
        )
        self.arrived.setdefault(axis ^ k, []).append((axis, slot))

    def first(self):
        a, b, c = self.order
        self.load.wait()
        self.copy.wait_recv()
        for slot, k in enumerate((a ^ b ^ c, a ^ b, a ^ c, a)):
            self.push(a, k, slot)

    def second(self):
        a, b, c = self.order
        self.push(b, b ^ c, 4)
        self.push(b, b, 5)

    def third(self):
        a, b, c = self.order
        self.push(c, c, 6)

    def finish(self):
        return self.total(0)

    def settle(self):
        for copy in self.copies.values():
            self.place.settle(copy)


def head_masks(rows, columns):
    lane = lax.broadcasted_iota(jnp.int32, (rows, columns), 1)
    return [(lane >= at) & (lane < at + HEAD_DIM) for at in range(0, columns, HEAD_DIM)]


def stack_heads(block, masks):
    zero = jnp.zeros_like(block)
    return jnp.concatenate([jnp.where(mask, block, zero) for mask in masks], axis=0)


def fold_heads(block, masks):
    rows = masks[0].shape[0]
    total = 0.0
    for h, mask in enumerate(masks):
        total = total + jnp.where(mask, block[h * rows : (h + 1) * rows], 0.0)
    return total


def norm_parts(rows):
    mean = jnp.mean(rows, axis=-1, keepdims=True)
    centered = rows - mean
    inverse = lax.rsqrt(jnp.mean(centered * centered, axis=-1, keepdims=True) + EPS)
    return centered * inverse, inverse


def norm_back(upstream, rows, gain):
    normed, inverse = norm_parts(rows)
    scaled = upstream * gain
    first = jnp.mean(scaled, axis=-1, keepdims=True)
    second = jnp.mean(scaled * normed, axis=-1, keepdims=True)
    return (
        inverse * (scaled - first - normed * second),
        jnp.sum(upstream * normed, axis=0, keepdims=True),
        jnp.sum(upstream, axis=0, keepdims=True),
    )


def gelu_parts(x):
    root = 0.7978845608028654
    t = jnp.tanh(root * (x + 0.044715 * (x * x * x)))
    half = 0.5 * (1.0 + t)
    return x * half, half + 0.5 * x * (1.0 - t * t) * (root * (1.0 + 3 * 0.044715 * (x * x)))


def window(width, k):
    return (width * k) // 128 * 128


def forward_kernel(
    count,
    small_in, frames_ref, media, latents, cotangent, w_query, w_key, w_value, w_output, w_up, w_down,
    o_joined, o_kv, o_query, o_weights, o_mixed, o_latent, o_wkv, o_wquery, o_woutput,
    o_back, o_out, o_gup, o_gdown, o_middle, o_small,
    joined, kv, query, weights, mixed, latent, wkv, wq, wo, up, down,
    tokens, upstream, pre, act, gpre, back, out, gup, gdown, middle, small, smalls, att, att_near, att_far,
    sems,
):
    place = Place(count, sems)
    items, local_media, width = media.shape
    local_latents = latents.shape[1]
    rows = local_media + local_latents
    keys_count = 4 * rows
    columns = w_query.shape[1]
    part = w_query.shape[0] // 2
    latent_count = 4 * local_latents
    item, y, core = place.item, place.y, place.core
    place.barrier()

    shift = (width // count * item) % 128
    smalls[item] = pltpu.roll(small_in[...], shift, 1).astype(BF)
    small_copies = [
        place.send(smalls.at[item], smalls.at[item], {"item": place.other(k), "head": place.head})
        for k in range(1, count)
    ]

    upstream[core, place.chip] = cotangent[...].reshape(middle.shape)
    upstream_gather = GroupGather(place, upstream)
    upstream_gather.push(0, 1)

    def pipes(source, slab, lanes):
        made = []
        for half, way in ((0, 1), (1, -1)):
            span = pl.ds(half * part, part)
            made.append(
                GatherPipe(place, source.at[span], lambda o, span=span: slab.at[o, span, lanes], way)
            )
        return made

    whole, second = pl.ds(0, columns), pl.ds(columns, columns)
    ring_pipes = (
        pipes(w_key, wkv, whole) + pipes(w_value, wkv, second) + pipes(w_query, wq, whole) + pipes(w_output, wo, whole)
    )
    hidden = up.shape[2]
    quarter = pl.ds(pl.multiple_of(place.quarter * hidden, 128), hidden)
    owns = [
        place.local(w_key, wkv.at[item, :, whole]),
        place.local(w_value, wkv.at[item, :, second]),
        place.local(w_query, wq.at[item]),
        place.local(w_output, wo.at[item]),
    ]
    own_hidden = [
        place.local(w_up.at[:, quarter], up.at[item]),
        place.local(w_down.at[:, quarter], down.at[item]),
    ]

    for copy in small_copies:
        copy.wait_recv()
    small[...] = jnp.zeros_like(small)
    for j in range(count):
        lanes = pl.ds(window(width // count, j), smalls.shape[2])
        small[:, lanes] += smalls[j].astype(F32)
    local_frames = local_media // P_SIZE
    time_rows = [small[pl.ds(6 + place.head * local_frames + f, 1), :] for f in range(local_frames)]

    gathers = []
    for b in range(items):
        for f in range(local_frames):
            span = pl.ds(f * P_SIZE, P_SIZE)
            normed, _ = norm_parts(media[b, span].astype(F32) + time_rows[f])
            joined[b, y, core, span] = (normed * small[0:1] + small[1:2]).astype(BF)
        normed, _ = norm_parts(latents[b].astype(F32))
        joined[b, y, core, pl.ds(local_media, local_latents)] = (
            normed * small[2:3] + small[3:4]
        ).astype(BF)
        gathers.append(HeadGather(place, joined.at[b]))

    ring = Pump(weave(*ring_pipes, steps=range(1, count)))
    each = len(ring_pipes)

    def project(b):
        gathers[b].finish()
        kv[b] = dot(joined[b].reshape(keys_count, width), wkv[...].reshape(width, 2 * columns), 1, 0).astype(BF)
        for p in range(4):
            latent[p, pl.ds(b * local_latents, local_latents)] = joined[
                b, p // 2, p % 2, pl.ds(local_media, local_latents)
            ]

    ring(2 * each)
    gathers[0].forward()
    ring(2 * each)
    gathers[1].forward()
    ring(each)
    gathers[2].forward()
    ring()
    upstream_gather.push(0, 4, 2)
    def spread(source, slab):
        copies = []
        for k in (4, 3, 5, 2, 6, 1, 7):
            to = place.other(k)
            lanes = pl.ds(pl.multiple_of((to % SPREAD) * hidden, 128), hidden)
            copies.append(
                place.send(source.at[:, lanes], slab.at[item], {"item": to, "head": place.head})
            )
        return copies

    up_copies = spread(w_up, up)
    gathers[3].forward()
    for copy in owns:
        copy.wait()
    for b in range(items):
        project(b)
    upstream_gather.pull(4, 0)
    upstream_gather.push(4, 2)
    scale = HEAD_DIM ** (-0.5)
    query[...] = (
        (scale * dot(latent[...].reshape(4 * items * local_latents, width), wq[...].reshape(width, columns), 1, 0))
        .astype(BF)
        .reshape(query.shape)
    )
    keeps = [
        place.local(joined, o_joined),
        place.local(kv, o_kv),
        place.local(query, o_query),
        place.local(latent, o_latent),
        place.local(wkv, o_wkv),
        place.local(wq, o_wquery),
        place.local(wo, o_woutput),
        place.local(small, o_small),
    ]
    masks = head_masks(latent_count, columns)
    index = lax.broadcasted_iota(jnp.int32, (1, keys_count), 1)
    local = index % rows
    frame = jnp.where(local < local_media, (index // rows) * local_frames + local // P_SIZE, -1)
    for b in range(items):
        mine = pl.ds(b * local_latents, local_latents)
        stacked = stack_heads(query[:, mine].reshape(latent_count, columns), masks)
        scores = dot(stacked, kv[b, :, :columns], 1, 1)
        shown = jnp.broadcast_to(frame, scores.shape) < frames_ref[b]
        scores = jnp.where(shown, scores, -1e30)
        expo = jnp.exp(scores - jnp.max(scores, axis=1, keepdims=True))
        weight = expo / jnp.sum(expo, axis=1, keepdims=True)
        weights[b] = weight
        result = fold_heads(dot(weight.astype(BF), kv[b, :, columns:], 1, 0), masks)
        mixed[:, mine] = result.astype(BF).reshape(4, local_latents, columns)
    att[...] = (
        dot(mixed[...].reshape(4 * items * local_latents, columns), wo[...].reshape(width, columns), 1, 1)
        .astype(BF)
        .reshape(att.shape)
    )
    keeps += [place.local(weights, o_weights), place.local(mixed, o_mixed)]
    scatter = HeadScatter(place, att, att_near, att_far)
    scatter.forward()
    upstream_gather.push(4, 1)
    upstream_gather.pull(2, 0)
    upstream_gather.push(2, 1)
    middle[...] = latents[...].astype(F32).reshape(middle.shape) + scatter.finish()
    normed, _ = norm_parts(middle[...])
    tokens[core, place.chip] = (normed * small[4:5] + small[5:6]).astype(BF)
    token_gather = GroupGather(place, tokens)
    token_gather.push(0, 4, 2, 1)
    down_copies = spread(w_down, down)
    keeps.append(place.local(middle, o_middle))
    upstream_gather.pull(2, 4)
    upstream_gather.push(6, 1)
    token_gather.pull(4, 0)
    token_gather.push(4, 2, 1)
    token_gather.pull(2, 0)
    token_gather.push(2, 1)
    token_gather.pull(2, 4)
    token_gather.push(6, 1)
    upstream_gather.pull(1, 0)
    for k in (4, 2, 6):
        upstream_gather.pull(1, k)
    for k in (0, 4, 2, 6):
        token_gather.pull(1, k)
    token_gather.finish()
    for copy in own_hidden:
        copy.wait()
    for copy in up_copies:
        copy.wait_recv()
    blocks = 4
    size = 2 * SPREAD * 2 // blocks

    def block(ref, n):
        return ref[n // 2, pl.ds((n % 2) * size, size)].reshape(-1, width)

    tall = tokens.shape[2] * size
    for n in range(blocks):
        span = pl.ds(n * tall, tall)
        pre[span] = dot(block(tokens, n), up[...].reshape(width, hidden), 1, 0)
    upstream_gather.finish()
    for n in range(blocks):
        span = pl.ds(n * tall, tall)
        value, slope = gelu_parts(pre[span])
        act[span] = value.astype(BF)
        pre[span] = slope
    tile = 2 * part * 2
    for t in range(width // tile):
        span = pl.ds(t * tile, tile)
        gdown[pl.ds(2 * t, 2)] = (
            dot(upstream[:, :, :, span].reshape(-1, tile), act[...], 0, 0)
            .astype(BF)
            .reshape(2, 2 * part, hidden)
        )
    keeps.append(place.local(gdown, o_gdown))
    for copy in down_copies:
        copy.wait_recv()
    for n in range(blocks):
        span = pl.ds(n * tall, tall)
        grad_act = dot(block(upstream, n), down[...].reshape(width, hidden), 1, 0)
        gpre[span] = (grad_act * pre[span]).astype(BF)
        where = (n // 2, pl.ds((n % 2) * size, size))
        shape = (size, tokens.shape[2], width)
        back[where] = dot(gpre[span], up[...].reshape(width, hidden), 1, 1).astype(BF).reshape(shape)
        out[where] = dot(act[span], down[...].reshape(width, hidden), 1, 1).astype(BF).reshape(shape)
    keeps += [place.local(back, o_back), place.local(out, o_out)]
    for t in range(width // tile):
        span = pl.ds(t * tile, tile)
        gup[pl.ds(2 * t, 2)] = (
            dot(tokens[:, :, :, span].reshape(-1, tile), gpre[...], 0, 0)
            .astype(BF)
            .reshape(2, 2 * part, hidden)
        )
    keeps.append(place.local(gup, o_gup))
    place.drain()
    for copy in keeps:
        copy.wait()


def backward_kernel(
    count,
    media, latents, cotangent, middle, small,
    i_joined, i_kv, i_query, i_weights, i_mixed, i_latent, i_wkv, i_wquery, i_woutput,
    i_back, i_out, i_gup, i_gdown,
    o_out, o_lgrad, o_media, o_query, o_key, o_value, o_output, o_up, o_down, o_small,
    joined, kv, query, weights, mixed, latent, wkv, wq, wo,
    gmiddle, kept, near, far, out_far, gatt, gmixed, gquery, gkv, gq, go,
    slots, up_in, down_in, m_near, m_far, mstage, sums, sum_in, sum_near, sum_far,
    sems,
):
    place = Place(count, sems)
    items, local_media, width = media.shape
    local_latents = latents.shape[1]
    rows = local_media + local_latents
    keys_count = 4 * rows
    columns = wq.shape[2]
    block_rows = wq.shape[1]
    part = block_rows // 2
    latent_count = 4 * local_latents
    all_latents = items * latent_count
    hidden = up_in.shape[2]
    item, y, core = place.item, place.y, place.core
    local_frames = local_media // P_SIZE
    scale = HEAD_DIM ** (-0.5)
    place.barrier()

    back_scatter = GroupScatter(place, i_back, kept, near, far, (1, 2, 4))

    def spread(source, slab, offsets):
        copies = []
        for k in offsets:
            to = place.other(k)
            copies.append(
                place.send(source.at[to], slab.at[item], {"item": to, "head": place.head})
            )
        return copies

    loads = {}
    for name, src, dst in (
        ("wo", i_woutput, wo), ("mixed", i_mixed, mixed), ("query", i_query, query), ("kv", i_kv, kv),
        ("weights", i_weights, weights), ("joined", i_joined, joined), ("wkv", i_wkv, wkv),
        ("latent", i_latent, latent), ("wq", i_wquery, wq),
    ):
        loads[name] = place.local(src, dst)
    back_scatter.first()
    down_copies = spread(i_gdown, down_in, (4, 2, 6))
    up_copies = spread(i_gup, up_in, (4, 2, 6))
    down_own = place.local(i_gdown.at[item], down_in.at[item])
    up_own = place.local(i_gup.at[item], up_in.at[item])
    sums[...] = jnp.zeros_like(sums)

    back_scatter.second()
    back_scatter.third()
    down_copies += spread(i_gdown, down_in, (3, 5, 1, 7))
    up_copies += spread(i_gup, up_in, (3, 5, 1, 7))

    grad_norm = back_scatter.finish()
    dx, dg, db = norm_back(grad_norm, middle[...], small[4:5])
    sums[4:5] = dg
    sums[5:6] = db
    grad_middle = cotangent[...].astype(F32).reshape(middle.shape) + dx
    gmiddle[...] = grad_middle
    gatt[y, core] = grad_middle.astype(BF)
    att_gather = HeadGather(place, gatt)
    att_gather.forward()
    att_gather.finish()
    loads["wo"].wait()
    loads["mixed"].wait()
    upstream = gatt[...].reshape(all_latents, width)
    gmixed[...] = dot(upstream, wo[...].reshape(width, columns), 1, 0).astype(BF).reshape(gmixed.shape)
    tile = 2 * block_rows
    for t in range(width // tile):
        span = pl.ds(t * tile, tile)
        go[pl.ds(2 * t, 2)] = (
            dot(gatt[:, :, :, span].reshape(all_latents, tile), mixed[...].reshape(all_latents, columns), 0, 0)
            .astype(BF)
            .reshape(2, block_rows, columns)
        )

    def pipes(first_slot, slab, lanes, result):
        made = []
        for half, way in ((0, 1), (1, -1)):
            span = pl.ds(half * part, part)

            def finish(value, span=span):
                result[span] = value

            made.append(
                ScatterPipe(
                    place,
                    lambda o, span=span: slab.at[o, span, lanes],
                    slots.at[first_slot + half],
                    finish,
                    way,
                )
            )
        return made

    whole, second = pl.ds(0, columns), pl.ds(columns, columns)
    go_pipes = pipes(0, go, whole, o_output)

    masks = head_masks(latent_count, columns)
    loads["query"].wait()
    loads["kv"].wait()
    loads["weights"].wait()
    loads["joined"].wait()
    loads["wkv"].wait()
    loads["wq"].wait()
    back_scatter.settle()
    out_scatter = GroupScatter(place, i_out, kept, near, out_far, (2, 1, 4))
    scatters = []
    tile = 2 * block_rows
    for b in range(items):
        mine = pl.ds(b * local_latents, local_latents)
        q_stack = stack_heads(query[:, mine].reshape(latent_count, columns), masks)
        g_stack = stack_heads(gmixed[:, mine].reshape(latent_count, columns), masks)
        weight = weights[b]
        grad_weight = dot(g_stack, kv[b, :, columns:], 1, 1)
        inner = jnp.sum(weight * grad_weight, axis=1, keepdims=True)
        grad_score = (weight * (grad_weight - inner)).astype(BF)
        gq_rows = fold_heads(dot(grad_score, kv[b, :, :columns], 1, 0), masks).astype(BF)
        gquery[:, mine] = gq_rows.reshape(4, local_latents, columns)
        kv[b, :, :columns] = dot(grad_score, q_stack, 0, 0).astype(BF)
        kv[b, :, columns:] = dot(weight.astype(BF), g_stack, 0, 0).astype(BF)
    out_scatter.first()
    for t in range(width // tile):
        span = pl.ds(t * tile, tile)
        gkv[pl.ds(2 * t, 2)] = (
            dot(joined[:, :, :, :, span].reshape(items * keys_count, tile), kv[...].reshape(items * keys_count, 2 * columns), 0, 0)
            .astype(BF)
            .reshape(2, block_rows, 2 * columns)
        )
    kv_pipes = pipes(2, gkv, whole, o_key) + pipes(4, gkv, second, o_value)
    loads["latent"].wait()
    for t in range(width // tile):
        span = pl.ds(t * tile, tile)
        gq[pl.ds(2 * t, 2)] = (
            (scale * dot(latent[:, :, span].reshape(all_latents, tile), gquery[...].reshape(all_latents, columns), 0, 0))
            .astype(BF)
            .reshape(2, block_rows, columns)
        )
    q_pipes = pipes(6, gq, whole, o_query)
    ring = Pump(weave(*go_pipes, *kv_pipes, *q_pipes, steps=range(count - 1)))
    each = 8
    for b in range(items):
        mine = pl.ds(b * local_latents, local_latents)
        gq_rows = gquery[:, mine].reshape(latent_count, columns)
        for t in range(width // tile):
            span = pl.ds(t * tile, tile)
            owners = pl.ds(2 * t, 2)
            value = dot(kv[b], wkv[owners].reshape(tile, 2 * columns), 1, 1)
            extra = scale * dot(gq_rows, wq[owners].reshape(tile, columns), 1, 1)
            for p in range(4):
                at = p * rows
                joined[b, p // 2, p % 2, pl.ds(0, local_media), span] = value[at : at + local_media].astype(BF)
                joined[b, p // 2, p % 2, pl.ds(local_media, local_latents), span] = (
                    value[at + local_media : at + rows] + extra[p * local_latents : (p + 1) * local_latents]
                ).astype(BF)
        scatters.append(HeadScatter(place, joined.at[b], m_near.at[b], m_far.at[b]))
        if b > 0:
            scatters[b - 1].forward()
    ring(each)
    out_scatter.second()
    scatters[-1].forward()
    ring(each)
    out_scatter.third()
    ring(each)

    def combine(copies, own, slab, result):
        own.wait()
        for copy in copies:
            copy.wait_recv()
        for k in range(SPREAD):
            grad = slab[k].astype(F32)
            for group in range(1, count // SPREAD):
                grad = grad + slab[group * SPREAD + k].astype(F32)
            result[:, pl.ds(k * hidden, hidden)] = grad

    time_rows = [small[pl.ds(6 + place.head * local_frames + f, 1), :] for f in range(local_frames)]
    stores = []
    for b in range(items):
        grad = scatters[b].finish()
        if b >= 2:
            stores[b - 2].wait()
        for f in range(local_frames):
            span = slice(f * P_SIZE, (f + 1) * P_SIZE)
            dx, dg, db = norm_back(grad[span], media[b, span].astype(F32) + time_rows[f], small[0:1])
            mstage[b % 2, span] = dx
            sums[0:1] += dg
            sums[1:2] += db
            sums[pl.ds(6 + place.head * local_frames + f, 1), :] += jnp.sum(dx, axis=0, keepdims=True)
        stores.append(place.local(mstage.at[b % 2], o_media.at[b]))
        dx, dg, db = norm_back(grad[local_media:], latents[b].astype(F32), small[2:3])
        sums[2:3] += dg
        sums[3:4] += db
        o_lgrad[b] = gmiddle[pl.ds(b * local_latents, local_latents)] + dx
        if b == 1:
            combine(up_copies, up_own, up_in, o_up)
            combine(down_copies, down_own, down_in, o_down)
        ring((each, each, 4, 0)[b])

    lanes = sum_in.shape[2]
    sum_copies = []
    for k in range(1, count):
        to = place.other(k)
        at = pl.multiple_of(window(width // count, to), 128)
        sum_copies.append(
            place.send(sums.at[:, pl.ds(at, lanes)], sum_in.at[item], {"item": to, "head": place.head})
        )
    sum_in[item] = sums[:, pl.ds(pl.multiple_of(window(width // count, item), 128), lanes)]
    ring(6)
    for copy in sum_copies:
        copy.wait_recv()
    value = jnp.sum(sum_in[...], axis=0)
    sum_in[0] = value
    copy = place.send(sum_in.at[0], sum_near, place.sibling)
    ring(4)
    copy.wait_recv()
    value = value + sum_near[...]
    sum_in[1] = value
    o_out[...] = (middle[...] + out_scatter.finish()).astype(BF).reshape(o_out.shape)
    copy = place.send(sum_in.at[1], sum_far, place.across)
    ring()
    copy.wait_recv()
    shift = (width // count * item) % 128
    o_small[...] = pltpu.roll(value + sum_far[...], (lanes - shift) % lanes, 1)
    place.drain()
    for store in stores[-2:]:
        store.wait()


def hand_over(*refs):
    third = (len(refs) - 1) // 3
    sources, targets, stages, sems = refs[:third], refs[third : 2 * third], refs[2 * third : -1], refs[-1]
    loads = [pltpu.make_async_copy(a, b, sems.at[0, k]) for k, (a, b) in enumerate(zip(sources, stages))]
    stores = [pltpu.make_async_copy(a, b, sems.at[1, k]) for k, (a, b) in enumerate(zip(stages, targets))]
    for copy in loads:
        copy.start()
    for load, store in zip(loads, stores):
        load.wait()
        store.start()
    for copy in stores:
        copy.wait()


def kernel_step(
    count, media, latents, cotangent, frame_counts,
    query_weight, key_weight, value_weight, output_weight, up_weight, down_weight,
    media_gain, media_bias, latent_gain, latent_bias, ffn_gain, ffn_bias, time_embed,
):
    items, local_media, width = media.shape
    local_latents = latents.shape[1]
    frames = time_embed.shape[0]
    block_rows, columns = query_weight.shape
    hidden = up_weight.shape[1] // SPREAD
    rows = local_media + local_latents
    keys_count = 4 * rows
    own_latents = items * local_latents
    stacked = columns // HEAD_DIM * 4 * local_latents
    group = 2 * SPREAD
    row = lax.broadcasted_iota(jnp.int32, (16, 256), 0)
    small = jnp.zeros((16, 256), F32)
    for k, vector in enumerate(
        (media_gain, media_bias, latent_gain, latent_bias, ffn_gain, ffn_bias)
    ):
        padded = jnp.pad(vector.astype(F32), (0, 256 - block_rows))
        small = jnp.where(row == k, padded[None, :], small)
    small = small + jnp.pad(
        time_embed.astype(F32), ((6, 10 - frames), (0, 256 - block_rows))
    )

    def hbm(*shape, kind=BF):
        return jax.ShapeDtypeStruct(shape, kind)

    def buf(*shape, kind=BF):
        return pltpu.VMEM(shape, kind)

    vmem, anywhere = pl.BlockSpec(memory_space=pltpu.VMEM), pl.BlockSpec(memory_space=pl.ANY)
    big = dict(
        joined=(items, 2, 2, rows, width),
        kv=(items, keys_count, 2 * columns),
        query=(4, own_latents, columns),
        weights=(items, stacked, keys_count),
        mixed=(4, own_latents, columns),
        latent=(4, own_latents, width),
        wkv=(count, block_rows, 2 * columns),
        wq=(count, block_rows, columns),
        wo=(count, block_rows, columns),
    )
    kinds = dict(weights=F32)
    tokens = (2, group, own_latents, width)
    slab = (count, block_rows, hidden)
    kept = forward_results = pl.pallas_call(
        functools.partial(forward_kernel, count),
        out_shape=[hbm(*shape, kind=kinds.get(name, BF)) for name, shape in big.items()]
        + [hbm(*tokens)] * 2
        + [hbm(*slab)] * 2
        + [hbm(own_latents, width, kind=F32), hbm(16, width, kind=F32)],
        in_specs=[vmem, pl.BlockSpec(memory_space=pltpu.SMEM)] + [vmem] * 3 + [anywhere] * 6,
        out_specs=[anywhere] * 15,
        scratch_shapes=[buf(*shape, kind=kinds.get(name, BF)) for name, shape in big.items()]
        + [buf(*slab)] * 2
        + [buf(*tokens)] * 2
        + [
            buf(2 * group * own_latents, hidden, kind=F32),
            buf(2 * group * own_latents, hidden),
            buf(2 * group * own_latents, hidden),
        ]
        + [buf(*tokens)] * 2
        + [buf(*slab)] * 2
        + [
            buf(own_latents, width, kind=F32),
            buf(16, width, kind=F32),
            buf(count, 16, 256),
            buf(2, 2, own_latents, width),
            buf(2, own_latents, width),
            buf(own_latents, width),
            pltpu.SemaphoreType.DMA((320,)),
        ],
        compiler_params=pltpu.CompilerParams(
            collective_id=0, has_side_effects=True, vmem_limit_bytes=60 * 2**20
        ),
        name="gather_forward",
    )(
        small, frame_counts, media, latents, cotangent, query_weight, key_weight, value_weight,
        output_weight, up_weight, down_weight,
    )
    kept = forward_results[:13]
    middle, small = forward_results[13:]
    results = pl.pallas_call(
        functools.partial(backward_kernel, count),
        out_shape=[
            hbm(*latents.shape),
            hbm(*latents.shape, kind=F32),
            hbm(*media.shape, kind=F32),
        ]
        + [hbm(block_rows, columns, kind=F32)] * 4
        + [hbm(block_rows, SPREAD * hidden, kind=F32)] * 2
        + [hbm(16, 256, kind=F32)],
        in_specs=[vmem] * 5 + [anywhere] * 13,
        out_specs=[vmem, vmem, anywhere] + [vmem] * 7,
        scratch_shapes=[buf(*shape, kind=kinds.get(name, BF)) for name, shape in big.items()]
        + [
            buf(own_latents, width, kind=F32),
            buf(group, own_latents, width),
            buf(group, own_latents, width),
            buf(group - 1, own_latents, width),
            buf(group - 1, own_latents, width),
            buf(2, 2, own_latents, width),
            buf(4, own_latents, columns),
            buf(4, own_latents, columns),
            buf(count, block_rows, 2 * columns),
            buf(count, block_rows, columns),
            buf(count, block_rows, columns),
            buf(8, count - 1, block_rows // 2, columns),
            buf(*slab),
            buf(*slab),
            buf(items, 2, rows, width),
            buf(items, rows, width),
            buf(2, local_media, width, kind=F32),
            buf(16, width, kind=F32),
            buf(count, 16, 256, kind=F32),
            buf(16, 256, kind=F32),
            buf(16, 256, kind=F32),
            pltpu.SemaphoreType.DMA((320,)),
        ],
        compiler_params=pltpu.CompilerParams(
            collective_id=1, has_side_effects=True, vmem_limit_bytes=62 * 2**20
        ),
        name="backward_scatter",
    )(media, latents, cotangent, middle, small, *kept)
    shapes = [jax.ShapeDtypeStruct(r.shape, r.dtype) for r in results]
    results = pl.pallas_call(
        hand_over,
        out_shape=shapes,
        in_specs=[anywhere] * len(shapes),
        out_specs=[anywhere] * len(shapes),
        scratch_shapes=[pltpu.VMEM(s.shape, s.dtype) for s in shapes]
        + [pltpu.SemaphoreType.DMA((2, len(shapes)))],
        compiler_params=pltpu.CompilerParams(vmem_limit_bytes=60 * 2**20),
        name="hand_over",
    )(*results)
    sums = results[9]
    return (
        *results[:9],
        *(sums[k, :block_rows] for k in range(6)),
        sums[6 : 6 + frames, :block_rows],
    )


def fits(mesh, media, query_weight, up_weight):
    count, heads = mesh.shape["item"], mesh.shape["head"]
    width, columns = query_weight.shape[0], query_weight.shape[1] // heads
    hidden = up_weight.shape[1] // heads
    block_rows = width // count
    return (
        heads == 4
        and count == 2 * SPREAD
        and block_rows % 64 == 0
        and columns % 128 == 0
        and hidden % (128 * SPREAD) == 0
    )


def solution(mesh):
    rows = P("item", "head", None)
    block = P("item", "head")
    vector = P("item")
    table = P(None, "item")

    def run(*arrays):
        count = mesh.shape["item"]
        step = plain_step
        if fits(mesh, arrays[0], arrays[4], arrays[8]):
            step = functools.partial(kernel_step, count)
        return jax.shard_map(
            step,
            mesh=mesh,
            in_specs=(rows,) * 3 + (vector,) + (block,) * 6 + (vector,) * 6 + (table,),
            out_specs=(rows,) * 3 + (block,) * 6 + (vector,) * 6 + (table,),
            check_vma=False,
        )(*arrays)

    return run
```

```python
import functools

import jax
import jax.numpy as jnp
from jax import lax
from jax.experimental import pallas as pl
from jax.experimental.pallas import tpu as pltpu
from jax.sharding import PartitionSpec as P

HEAD_DIM = 96
P_SIZE = 64
EPS = 1e-05
BF = jnp.bfloat16
F32 = jnp.float32


def norm_forward(rows, gain, bias):
    mean = jnp.mean(rows, axis=-1, keepdims=True)
    centered = rows - mean
    inverse = lax.rsqrt(jnp.mean(centered * centered, axis=-1, keepdims=True) + EPS)
    normed = centered * inverse
    return normed * gain + bias, normed, inverse


def norm_backward(upstream, normed, inverse, gain):
    scaled = upstream * gain
    first = jnp.mean(scaled, axis=-1, keepdims=True)
    second = jnp.mean(scaled * normed, axis=-1, keepdims=True)
    axes = tuple(range(upstream.ndim - 1))
    return (
        inverse * (scaled - first - normed * second),
        jnp.sum(upstream * normed, axis=axes),
        jnp.sum(upstream, axis=axes),
    )


def dot(left, right, a, b):
    return lax.dot_general(left, right, (((a,), (b,)), ((), ())), preferred_element_type=F32)


def gather_rows(rows):
    return lax.all_gather(rows, "head", axis=1, tiled=True)


def scatter_rows(rows):
    return lax.psum_scatter(rows.astype(BF), "head", scatter_dimension=1, tiled=True).astype(F32)


def item_scatter(grad):
    return lax.psum_scatter(grad.astype(BF), "item", scatter_dimension=0, tiled=True).astype(F32)


def plain_step(
    media, latents, cotangent, frame_counts,
    query_weight, key_weight, value_weight, output_weight, up_weight, down_weight,
    media_gain, media_bias, latent_gain, latent_bias, ffn_gain, ffn_bias, time_embed,
):
    items, local_media, width = media.shape
    frames = time_embed.shape[0]
    local_frames = local_media // P_SIZE
    place = lax.axis_index("head")
    scale = HEAD_DIM ** (-0.5)
    small = jnp.concatenate(
        [jnp.stack([media_gain, media_bias, latent_gain, latent_bias, ffn_gain, ffn_bias]), time_embed]
    )
    small = lax.all_gather(small, "item", axis=1, tiled=True).astype(F32)
    g_media, b_media, g_latent, b_latent, g_ffn, b_ffn = (small[k] for k in range(6))
    time_rows = lax.dynamic_slice_in_dim(small[6:], place * local_frames, local_frames, 0)
    w_query, w_key, w_value, w_output, w_up, w_down = (
        lax.all_gather(w, "item", axis=0, tiled=True)
        for w in (query_weight, key_weight, value_weight, output_weight, up_weight, down_weight)
    )
    shifted = (
        media.astype(F32).reshape(items, local_frames, P_SIZE, width) + time_rows[None, :, None, :]
    ).reshape(media.shape)
    media_norm, media_hat, media_inv = norm_forward(shifted, g_media, b_media)
    latent_f = latents.astype(F32)
    latent_norm, latent_hat, latent_inv = norm_forward(latent_f, g_latent, b_latent)
    media_all = gather_rows(media_norm.astype(BF))
    latent_all = gather_rows(latent_norm.astype(BF))
    upstream = gather_rows(cotangent)
    media_count, latent_count = media_all.shape[1], latent_all.shape[1]
    joined = jnp.concatenate([media_all, latent_all], axis=1)
    key_count = joined.shape[1]
    local_heads = w_query.shape[1] // HEAD_DIM
    query = (scale * dot(latent_all, w_query, 2, 0)).astype(BF)
    keys = dot(joined, w_key, 2, 0).astype(BF)
    values = dot(joined, w_value, 2, 0).astype(BF)
    query_h = query.reshape(items, latent_count, local_heads, HEAD_DIM)
    key_h = keys.reshape(items, key_count, local_heads, HEAD_DIM)
    value_h = values.reshape(items, key_count, local_heads, HEAD_DIM)
    index = jnp.arange(key_count, dtype=jnp.int32)
    valid = (index[None, :] // P_SIZE < frame_counts[:, None]) | (index[None, :] >= media_count)
    valid = valid[:, None, None, :]

    def mix(spec, left, right):
        return jnp.einsum(spec, left, right, preferred_element_type=F32)

    scores = jnp.where(valid, mix("blhe,bnhe->bhln", query_h, key_h), -1e30)
    peak = jnp.max(scores, axis=-1, keepdims=True)
    expo = jnp.exp(scores - peak)
    weights = expo / jnp.sum(expo, axis=-1, keepdims=True)
    weights_low = weights.astype(BF)
    mixed = mix("bhln,bnhe->blhe", weights_low, value_h).reshape(items, latent_count, -1).astype(BF)
    middle = latent_f + scatter_rows(dot(mixed, w_output, 2, 1))
    ffn_norm, ffn_hat, ffn_inv = norm_forward(middle, g_ffn, b_ffn)
    ffn_all = gather_rows(ffn_norm.astype(BF))
    rows = items * latent_count
    ffn_rows = ffn_all.reshape(rows, width)
    up_rows = upstream.reshape(rows, width)
    pre = dot(ffn_rows, w_up, 1, 0)
    act, gelu_back = jax.vjp(jax.nn.gelu, pre)
    act = act.astype(BF)
    ffn_out = scatter_rows(dot(act, w_down, 1, 1).reshape(items, latent_count, width))
    output = (middle + ffn_out).astype(BF)
    grad_down = dot(up_rows, act, 0, 0)
    grad_pre = gelu_back(dot(up_rows, w_down, 1, 0))[0].astype(BF)
    grad_up = dot(ffn_rows, grad_pre, 0, 0)
    grad_ffn = scatter_rows(dot(grad_pre, w_up, 1, 1).reshape(items, latent_count, width))
    grad_mid, grad_fgain, grad_fbias = norm_backward(grad_ffn, ffn_hat, ffn_inv, g_ffn)
    grad_middle = cotangent.astype(F32) + grad_mid
    attended_grad = gather_rows(grad_middle.astype(BF)).reshape(rows, width)
    grad_output = dot(attended_grad, mixed.reshape(rows, -1), 0, 0)
    grad_mixed = dot(attended_grad, w_output, 1, 0).astype(BF)
    gm_h = grad_mixed.reshape(items, latent_count, local_heads, HEAD_DIM)
    grad_values = mix("bhln,blhe->bnhe", weights_low, gm_h).astype(BF).reshape(items * key_count, -1)
    grad_weights = mix("blhe,bnhe->bhln", gm_h, value_h)
    inner = jnp.sum(weights * grad_weights, axis=-1, keepdims=True)
    grad_scores = (weights * (grad_weights - inner)).astype(BF)
    grad_query = mix("bhln,bnhe->blhe", grad_scores, key_h).astype(BF).reshape(rows, -1)
    grad_keys = mix("bhln,blhe->bnhe", grad_scores, query_h).astype(BF).reshape(items * key_count, -1)
    joined_rows = joined.reshape(items * key_count, width)
    grad_wquery = scale * dot(latent_all.reshape(rows, width), grad_query, 0, 0)
    grad_wkey = dot(joined_rows, grad_keys, 0, 0)
    grad_wvalue = dot(joined_rows, grad_values, 0, 0)
    grad_joined = dot(grad_keys, w_key, 1, 1) + dot(grad_values, w_value, 1, 1)
    grad_joined = grad_joined.reshape(items, key_count, width)
    grad_latent_all = grad_joined[:, media_count:] + scale * dot(grad_query, w_query, 1, 1).reshape(
        items, latent_count, width
    )
    media_back = scatter_rows(grad_joined[:, :media_count])
    latent_back = scatter_rows(grad_latent_all)
    grad_media, grad_mgain, grad_mbias = norm_backward(media_back, media_hat, media_inv, g_media)
    grad_lat, grad_lgain, grad_lbias = norm_backward(latent_back, latent_hat, latent_inv, g_latent)
    time_local = jnp.sum(grad_media.reshape(items, local_frames, P_SIZE, width), axis=(0, 2))
    grad_time = lax.dynamic_update_slice_in_dim(
        jnp.zeros((frames, width), F32), time_local, place * local_frames, 0
    )
    smalls = jnp.concatenate(
        [jnp.stack([grad_mgain, grad_mbias, grad_lgain, grad_lbias, grad_fgain, grad_fbias]), grad_time]
    )
    smalls = lax.psum_scatter(smalls, ("item",), scatter_dimension=1, tiled=True)
    smalls = lax.psum(smalls, "head")
    return (
        output,
        grad_middle + grad_lat,
        grad_media,
        *(item_scatter(g) for g in (grad_wquery, grad_wkey, grad_wvalue, grad_output, grad_up, grad_down)),
        *(smalls[k] for k in range(6)),
        smalls[6:],
    )


MESH = pl.DeviceIdType.MESH
VMEM = pltpu.VMEM
ANY = pl.ANY
SPREAD = 4


class Place:
    def __init__(self, count, sems, chip_rows):
        self.count = count
        self.rows = chip_rows
        self.sems = sems
        self.used = 0
        self.sent = []
        i, h = lax.axis_index("item"), lax.axis_index("head")
        self.item, self.head = i, h
        self.y, self.core = h // 2, h % 2
        self.quarter = i % SPREAD
        self.group = i // SPREAD
        odd = i % 2
        self.spot = (1 - odd) * (i // 2) + odd * (count - 1 - i // 2)
        self.sibling = {"item": i, "head": 2 * self.y + 1 - self.core}
        self.across = {"item": i, "head": 2 * (1 - self.y) + self.core}
        self.opposite = {"item": i, "head": 2 * (1 - self.y) + 1 - self.core}
        self.chip = 2 * self.quarter + self.y

    def ring(self, spot):
        spot = (spot + self.count) % self.count
        back = spot // (self.count // 2)
        return (1 - back) * 2 * spot + back * (2 * (self.count - 1 - spot) + 1)

    def member(self, k):
        bits = [self.quarter // 2, self.quarter % 2, self.y]
        want = [k // 4, (k // 2) % 2, k % 2]
        a, b, y = (u + w - 2 * u * w for u, w in zip(bits, want))
        quarter = 2 * a + b
        device = {"item": self.group * SPREAD + quarter, "head": 2 * y + self.core}
        return 2 * quarter + y, device

    def chip_rows(self, core, chip):
        rows = self.rows
        return pl.ds(pl.multiple_of((core * 2 * SPREAD + chip) * rows, rows), rows)

    def other(self, k):
        return (self.item + k) % self.count

    def barrier(self):
        sem = pltpu.get_barrier_semaphore()
        peers = [{"item": self.other(k), "head": self.head} for k in range(1, self.count)]
        peers += [self.sibling, self.across, self.opposite]
        peers += [self.member(k)[1] for k in (3, 5, 7)]
        for peer in peers:
            pl.semaphore_signal(sem, inc=1, device_id=peer, device_id_type=MESH)
        pl.semaphore_wait(sem, len(peers))

    def send(self, src, dst, device):
        copy = pltpu.make_async_remote_copy(
            src_ref=src,
            dst_ref=dst,
            send_sem=self.sems.at[self.used],
            recv_sem=self.sems.at[self.used + 1],
            device_id=device,
            device_id_type=MESH,
        )
        self.used += 2
        copy.start()
        self.sent.append(copy)
        return copy

    def local(self, src, dst):
        copy = pltpu.make_async_copy(src, dst, self.sems.at[self.used])
        self.used += 1
        copy.start()
        return copy

    def settle(self, copy):
        copy.wait_send()
        self.sent = [other for other in self.sent if other is not copy]

    def drain(self):
        for copy in self.sent:
            copy.wait_send()


class Pump:
    def __init__(self, steps):
        self.steps = list(steps)
        self.at = 0

    def __call__(self, count=None):
        end = len(self.steps) if count is None else min(self.at + count, len(self.steps))
        while self.at < end:
            self.steps[self.at]()
            self.at += 1


class GatherPipe:
    def __init__(self, place, source, target, way):
        self.place, self.target, self.way = place, target, way
        self.device = {"item": place.ring(place.spot + way), "head": place.head}
        self.copy = place.send(source, target(place.item), self.device)

    def step(self, s):
        self.copy.wait_recv()
        if s < self.place.count - 1:
            part = self.target(self.place.ring(self.place.spot - self.way * s))
            self.copy = self.place.send(part, part, self.device)


class ScatterPipe:
    def __init__(self, place, part, slots, finish, way):
        self.place, self.part, self.slots, self.finish, self.way = place, part, slots, finish, way
        self.device = {"item": place.ring(place.spot + way), "head": place.head}
        self.copy = place.send(part(place.ring(place.spot - way)), slots.at[0], self.device)

    def step(self, s):
        self.copy.wait_recv()
        if s < self.place.count - 2:
            own = self.part(self.place.ring(self.place.spot - self.way * (s + 2)))
            self.slots[s] = (self.slots[s].astype(F32) + own[...].astype(F32)).astype(BF)
            self.copy = self.place.send(self.slots.at[s], self.slots.at[s + 1], self.device)
        else:
            self.finish(self.slots[s].astype(F32) + self.part(self.place.item)[...].astype(F32))


def weave(*pipes, steps):
    return [functools.partial(pipe.step, s) for s in steps for pipe in pipes]


class HeadGather:
    def __init__(self, place, ref):
        self.place, self.ref = place, ref
        own = ref.at[place.y, place.core]
        self.near = place.send(own, own, place.sibling)
        self.far = place.send(own, own, place.across)

    def forward(self):
        place = self.place
        self.far.wait_recv()
        block = self.ref.at[1 - place.y, place.core]
        self.passed = place.send(block, block, place.sibling)

    def finish(self):
        self.near.wait_recv()
        self.passed.wait_recv()

    def settle(self):
        for copy in (self.near, self.far, self.passed):
            self.place.settle(copy)


class HeadScatter:
    def __init__(self, place, part, near, far):
        self.place, self.part, self.near, self.far = place, part, near, far
        self.copies = [
            place.send(part.at[side, 1 - place.core], near[side], place.sibling) for side in range(2)
        ]

    def landed(self, side):
        first, second = self.near[0][...].astype(F32), self.near[1][...].astype(F32)
        return jnp.where(side == 0, first, second)

    def forward(self):
        place, part = self.place, self.part
        for copy in self.copies:
            copy.wait_recv()
        block = part.at[1 - place.y, place.core]
        block[...] = (block[...].astype(F32) + self.landed(1 - place.y)).astype(BF)
        self.copy = place.send(block, self.far, place.across)
        self.copies.append(self.copy)

    def finish(self):
        place = self.place
        own = self.part[place.y, place.core].astype(F32) + self.landed(place.y)
        self.copy.wait_recv()
        return own + self.far[...].astype(F32)

    def settle(self):
        for copy in self.copies:
            self.place.settle(copy)


class GroupGather:
    def __init__(self, place, ref):
        self.place, self.ref = place, ref
        self.copies = {}
        self.passed = []
        self.share(0)

    def block(self, k):
        return self.ref.at[self.place.chip_rows(self.place.core, self.place.member(k)[0])]

    def settle(self):
        for copy in self.passed + list(self.copies.values()):
            self.place.settle(copy)

    def share(self, k):
        self.passed.append(self.place.send(self.block(k), self.block(k), self.place.sibling))

    def push(self, k, *axes):
        for axis in axes:
            self.copies[axis, k] = self.place.send(self.block(k), self.block(k), self.place.member(axis)[1])

    def pull(self, axis, k):
        self.copies[axis, k].wait_recv()
        self.share(axis ^ k)

    def finish(self):
        for copy in self.passed:
            copy.wait_recv()


class GroupScatter:
    def __init__(self, place, part, near, far, order):
        self.place, self.part, self.near, self.far, self.order = place, part, near, far, order
        rows = near.shape[0]
        self.copy = place.send(
            part.at[pl.ds(pl.multiple_of((1 - place.core) * rows, rows), rows)], near, place.sibling
        )
        self.copies = {}
        self.arrived = {}

    def total(self, k):
        chip = self.place.member(k)[0]
        value = self.part[self.place.chip_rows(self.place.core, chip)].astype(F32)
        value = value + self.near[self.place.chip_rows(0, chip)].astype(F32)
        for axis, slot in self.arrived.get(k, ()):
            self.copies[axis, axis ^ k].wait_recv()
            value = value + self.far[slot].astype(F32)
        return value

    def push(self, axis, k, slot):
        chip, _ = self.place.member(k)
        block = self.part.at[self.place.chip_rows(self.place.core, chip)]
        block[...] = self.total(k).astype(BF)
        self.copies[axis, k] = self.place.send(block, self.far.at[slot], self.place.member(axis)[1])
        self.arrived.setdefault(axis ^ k, []).append((axis, slot))

    def first(self):
        a, b, c = self.order
        self.copy.wait_recv()
        for slot, k in enumerate((a ^ b ^ c, a ^ b, a ^ c, a)):
            self.push(a, k, slot)

    def second(self):
        a, b, c = self.order
        self.push(b, b ^ c, 4)
        self.push(b, b, 5)

    def third(self):
        a, b, c = self.order
        self.push(c, c, 6)

    def finish(self):
        return self.total(0)

    def settle(self):
        for copy in [self.copy, *self.copies.values()]:
            self.place.settle(copy)


def head_masks(rows, columns):
    lane = lax.broadcasted_iota(jnp.int32, (rows, columns), 1)
    return [(lane >= at) & (lane < at + HEAD_DIM) for at in range(0, columns, HEAD_DIM)]


def stack_heads(block, masks):
    zero = jnp.zeros_like(block)
    return jnp.concatenate([jnp.where(mask, block, zero) for mask in masks], axis=0)


def fold_heads(block, masks):
    rows = masks[0].shape[0]
    total = 0.0
    for h, mask in enumerate(masks):
        total = total + jnp.where(mask, block[h * rows : (h + 1) * rows], 0.0)
    return total


def norm_parts(rows):
    mean = jnp.mean(rows, axis=-1, keepdims=True)
    centered = rows - mean
    inverse = lax.rsqrt(jnp.mean(centered * centered, axis=-1, keepdims=True) + EPS)
    return centered * inverse, inverse


def norm_back(upstream, rows, gain):
    normed, inverse = norm_parts(rows)
    scaled = upstream * gain
    first = jnp.mean(scaled, axis=-1, keepdims=True)
    second = jnp.mean(scaled * normed, axis=-1, keepdims=True)
    return (
        inverse * (scaled - first - normed * second),
        jnp.sum(upstream * normed, axis=0, keepdims=True),
        jnp.sum(upstream, axis=0, keepdims=True),
    )


def gelu_parts(x):
    root = 0.7978845608028654
    t = jnp.tanh(root * (x + 0.044715 * (x * x * x)))
    half = 0.5 * (1.0 + t)
    return x * half, half + 0.5 * x * (1.0 - t * t) * (root * (1.0 + 3 * 0.044715 * (x * x)))


def window(width, k):
    return (width * k) // 128 * 128


def layer_kernel(
    count,
    small_in, frames_ref, media_in, latents_in, cotangent_in, w_query, w_key, w_value, w_output, w_up, w_down,
    o_out, o_lgrad, o_media, o_query, o_key, o_value, o_output, o_up, o_down, o_small,
    media, latents, cotangent,
    joined, kv, query, weights, mixed, latent, wkv, wq, wo, up, down,
    tokens, upstream, pre, act, gpre, back, gup, gdown, middle, gmiddle, small, smalls, att, att_near, att_far,
    near, far, out_far, gmixed, gquery, gkv, slots, up_in, down_in, mstage, sums, sum_in, sum_head,
    sems,
):
    place = Place(count, sems, latents_in.shape[0] * latents_in.shape[1])
    loads = [
        place.local(media_in, media),
        place.local(latents_in, latents),
        place.local(cotangent_in, cotangent),
    ]
    place.barrier()
    items, local_media, width = media.shape
    local_latents = latents.shape[1]
    rows = local_media + local_latents
    keys_count = 4 * rows
    block_rows, columns = w_query.shape
    hidden = up.shape[2]
    part = block_rows // 2
    latent_count = 4 * local_latents
    all_latents = items * latent_count
    own_latents = items * local_latents
    group_rows = 4 * SPREAD * own_latents
    local_frames = local_media // P_SIZE
    scale = HEAD_DIM ** (-0.5)
    tile = 2 * block_rows
    item, y, core = place.item, place.y, place.core

    shift = block_rows * item % 128
    smalls[item] = pltpu.roll(small_in[...], shift, 1).astype(BF)
    small_copies = [
        place.send(smalls.at[item], smalls.at[item], {"item": place.other(k), "head": place.head})
        for k in range(1, count)
    ]
    for load in loads:
        load.wait()
    own = place.chip_rows(core, place.chip)
    upstream[own] = cotangent[...].reshape(own_latents, width)
    upstream_gather = GroupGather(place, upstream)
    upstream_gather.push(0, 1)

    def gather_pipes(source, slab, lanes):
        made = []
        for half, way in ((0, 1), (1, -1)):
            span = pl.ds(half * part, part)
            made.append(
                GatherPipe(place, source.at[span], lambda o, span=span: slab.at[o, span, lanes], way)
            )
        return made

    whole, second = pl.ds(0, columns), pl.ds(columns, columns)
    ring_pipes = (
        gather_pipes(w_key, wkv, whole)
        + gather_pipes(w_value, wkv, second)
        + gather_pipes(w_query, wq, whole)
        + gather_pipes(w_output, wo, whole)
    )
    ring = Pump(weave(*ring_pipes, steps=range(1, count)))
    each = len(ring_pipes)
    quarter = pl.ds(pl.multiple_of(place.quarter * hidden, 128), hidden)
    owns = [
        place.local(w_key, wkv.at[item, :, whole]),
        place.local(w_value, wkv.at[item, :, second]),
        place.local(w_query, wq.at[item]),
        place.local(w_output, wo.at[item]),
    ]
    own_hidden = [
        place.local(w_up.at[:, quarter], up.at[item]),
        place.local(w_down.at[:, quarter], down.at[item]),
    ]
    for copy in small_copies:
        copy.wait_recv()
    small[...] = jnp.zeros_like(small)
    for j in range(count):
        lanes = pl.ds(window(block_rows, j), smalls.shape[2])
        small[:, lanes] += smalls[j].astype(F32)
    time_rows = [small[pl.ds(6 + place.head * local_frames + f, 1), :] for f in range(local_frames)]

    gathers = []
    for b in range(items):
        for f in range(local_frames):
            span = pl.ds(f * P_SIZE, P_SIZE)
            normed, _ = norm_parts(media[b, span].astype(F32) + time_rows[f])
            joined[b, y, core, span] = (normed * small[0:1] + small[1:2]).astype(BF)
        normed, _ = norm_parts(latents[b].astype(F32))
        joined[b, y, core, pl.ds(local_media, local_latents)] = (
            normed * small[2:3] + small[3:4]
        ).astype(BF)
        gathers.append(HeadGather(place, joined.at[b]))

    def project(b):
        gathers[b].finish()
        kv[b] = dot(joined[b].reshape(keys_count, width), wkv[...].reshape(width, 2 * columns), 1, 0).astype(BF)
        for p in range(4):
            latent[p, pl.ds(b * local_latents, local_latents)] = joined[
                b, p // 2, p % 2, pl.ds(local_media, local_latents)
            ]

    ring(2 * each)
    gathers[0].forward()
    ring(2 * each)
    gathers[1].forward()
    ring(each)
    gathers[2].forward()
    ring()
    upstream_gather.push(0, 4, 2)

    def spread(source, slab, offsets, lanes_of=None):
        copies = []
        for k in offsets:
            to = place.other(k)
            if lanes_of is None:
                block = source.at[to]
            else:
                block = source.at[:, pl.ds(pl.multiple_of((to % SPREAD) * hidden, 128), hidden)]
            copies.append(place.send(block, slab.at[item], {"item": to, "head": place.head}))
        return copies

    straight, turned = (4, 2, 6), (3, 5, 1, 7)
    mixed_order = (4, 3, 5, 2, 6, 1, 7)
    up_copies = spread(w_up, up, mixed_order, hidden)
    gathers[3].forward()
    for copy in owns:
        copy.wait()
    for b in range(items):
        project(b)
    upstream_gather.pull(4, 0)
    upstream_gather.push(4, 2)
    query[...] = (
        (scale * dot(latent[...].reshape(all_latents, width), wq[...].reshape(width, columns), 1, 0))
        .astype(BF)
        .reshape(query.shape)
    )
    masks = head_masks(latent_count, columns)
    index = lax.broadcasted_iota(jnp.int32, (1, keys_count), 1)
    local = index % rows
    frame = jnp.where(local < local_media, (index // rows) * local_frames + local // P_SIZE, -1)
    for b in range(items):
        mine = pl.ds(b * local_latents, local_latents)
        stacked = stack_heads(query[:, mine].reshape(latent_count, columns), masks)
        scores = dot(stacked, kv[b, :, :columns], 1, 1)
        shown = jnp.broadcast_to(frame, scores.shape) < frames_ref[b]
        scores = jnp.where(shown, scores, -1e30)
        expo = jnp.exp(scores - jnp.max(scores, axis=1, keepdims=True))
        weight = expo / jnp.sum(expo, axis=1, keepdims=True)
        weights[b] = weight
        result = fold_heads(dot(weight.astype(BF), kv[b, :, columns:], 1, 0), masks)
        mixed[:, mine] = result.astype(BF).reshape(4, local_latents, columns)
    att[...] = (
        dot(mixed[...].reshape(all_latents, columns), wo[...].reshape(width, columns), 1, 1)
        .astype(BF)
        .reshape(att.shape)
    )
    scatter = HeadScatter(place, att, [att_near.at[0], att_near.at[1]], att_far)
    scatter.forward()
    upstream_gather.push(4, 1)
    upstream_gather.pull(2, 0)
    upstream_gather.push(2, 1)
    middle[...] = latents[...].astype(F32).reshape(middle.shape) + scatter.finish()
    scatter.settle()
    normed, _ = norm_parts(middle[...])
    tokens[own] = (normed * small[4:5] + small[5:6]).astype(BF)
    token_gather = GroupGather(place, tokens)
    token_gather.push(0, 4, 2, 1)
    down_copies = spread(w_down, down, mixed_order, hidden)
    upstream_gather.pull(2, 4)
    upstream_gather.push(6, 1)
    token_gather.pull(4, 0)
    token_gather.push(4, 2, 1)
    token_gather.pull(2, 0)
    token_gather.push(2, 1)
    token_gather.pull(2, 4)
    token_gather.push(6, 1)
    for k in (0, 4, 2, 6):
        upstream_gather.pull(1, k)
    for k in (0, 4, 2, 6):
        token_gather.pull(1, k)
    token_gather.finish()

    for copy in own_hidden:
        copy.wait()
    for copy in up_copies:
        copy.wait_recv()
    blocks = 4
    tall = group_rows // blocks
    spans = [pl.ds(n * tall, tall) for n in range(blocks)]
    for span in spans:
        value, slope = gelu_parts(dot(tokens[span], up[...].reshape(width, hidden), 1, 0))
        act[span] = value.astype(BF)
        pre[span] = slope
    upstream_gather.finish()
    all_rows = pl.ds(0, group_rows)
    for t in range(width // tile):
        span = pl.ds(t * tile, tile)
        gdown[pl.ds(2 * t, 2)] = (
            dot(upstream[all_rows, span], act[...], 0, 0).astype(BF).reshape(2, block_rows, hidden)
        )
    down_sums = spread(gdown, down_in, straight)
    for copy in down_copies:
        copy.wait_recv()
    for span in spans:
        grad_act = dot(upstream[span], down[...].reshape(width, hidden), 1, 0)
        gpre[span] = (grad_act * pre[span]).astype(BF)
        back[span] = dot(gpre[span], up[...].reshape(width, hidden), 1, 1).astype(BF)
    back_scatter = GroupScatter(place, back, near, far, (1, 2, 4))
    for t in range(width // tile):
        span = pl.ds(t * tile, tile)
        gup[pl.ds(2 * t, 2)] = (
            dot(tokens[all_rows, span], gpre[...], 0, 0).astype(BF).reshape(2, block_rows, hidden)
        )
    back_scatter.first()
    down_sums += spread(gdown, down_in, turned)
    upstream_gather.settle()
    out = upstream
    for span in spans:
        out[span] = dot(act[span], down[...].reshape(width, hidden), 1, 1).astype(BF)
    token_gather.settle()
    back_scatter.second()
    back_scatter.third()
    up_sums = spread(gup, up_in, straight)
    down_own = place.local(gdown.at[item], down_in.at[item])
    up_own = place.local(gup.at[item], up_in.at[item])
    sums[...] = jnp.zeros_like(sums)
    grad_norm = back_scatter.finish()
    back_scatter.settle()

    dx, dg, db = norm_back(grad_norm, middle[...], small[4:5])
    sums[4:5] = dg
    sums[5:6] = db
    grad_middle = cotangent[...].astype(F32).reshape(middle.shape) + dx
    gmiddle[...] = grad_middle
    gatt = att
    gatt[y, core] = grad_middle.astype(BF)
    att_gather = HeadGather(place, gatt)
    up_sums += spread(gup, up_in, turned)
    att_gather.forward()
    att_gather.finish()
    out_scatter = GroupScatter(place, out, near, out_far, (1, 2, 4))
    go, gq = up, down
    gmixed[...] = (
        dot(gatt[...].reshape(all_latents, width), wo[...].reshape(width, columns), 1, 0)
        .astype(BF)
        .reshape(gmixed.shape)
    )
    out_scatter.first()
    for t in range(width // tile):
        span = pl.ds(t * tile, tile)
        go[pl.ds(2 * t, 2)] = (
            dot(gatt[:, :, :, span].reshape(all_latents, tile), mixed[...].reshape(all_latents, columns), 0, 0)
            .astype(BF)
            .reshape(2, block_rows, columns)
        )

    def scatter_pipes(first_slot, slab, lanes, result):
        made = []
        for half, way in ((0, 1), (1, -1)):
            span = pl.ds(half * part, part)

            def finish(value, span=span):
                result[span] = value

            made.append(
                ScatterPipe(
                    place,
                    lambda o, span=span: slab.at[o, span, lanes],
                    slots.at[first_slot + half],
                    finish,
                    way,
                )
            )
        return made

    for b in range(items):
        mine = pl.ds(b * local_latents, local_latents)
        q_stack = stack_heads(query[:, mine].reshape(latent_count, columns), masks)
        g_stack = stack_heads(gmixed[:, mine].reshape(latent_count, columns), masks)
        weight = weights[b]
        grad_weight = dot(g_stack, kv[b, :, columns:], 1, 1)
        inner = jnp.sum(weight * grad_weight, axis=1, keepdims=True)
        grad_score = (weight * (grad_weight - inner)).astype(BF)
        gq_rows = fold_heads(dot(grad_score, kv[b, :, :columns], 1, 0), masks).astype(BF)
        gquery[:, mine] = gq_rows.reshape(4, local_latents, columns)
        kv[b, :, :columns] = dot(grad_score, q_stack, 0, 0).astype(BF)
        kv[b, :, columns:] = dot(weight.astype(BF), g_stack, 0, 0).astype(BF)
    for t in range(width // tile):
        span = pl.ds(t * tile, tile)
        gkv[pl.ds(2 * t, 2)] = (
            dot(
                joined[:, :, :, :, span].reshape(items * keys_count, tile),
                kv[...].reshape(items * keys_count, 2 * columns),
                0,
                0,
            )
            .astype(BF)
            .reshape(2, block_rows, 2 * columns)
        )
    kv_pipes = scatter_pipes(2, gkv, whole, o_key) + scatter_pipes(4, gkv, second, o_value)
    for t in range(width // tile):
        span = pl.ds(t * tile, tile)
        gq[pl.ds(2 * t, 2)] = (
            (scale * dot(latent[:, :, span].reshape(all_latents, tile), gquery[...].reshape(all_latents, columns), 0, 0))
            .astype(BF)
            .reshape(2, block_rows, columns)
        )
    qo_pipes = scatter_pipes(6, gq, whole, o_query) + scatter_pipes(0, go, whole, o_output)
    ring = Pump(weave(*kv_pipes, *qo_pipes, steps=range(count - 1)))
    scatters = []
    for gather in gathers:
        gather.settle()
    for b in range(items):
        mine = pl.ds(b * local_latents, local_latents)
        gq_rows = gquery[:, mine].reshape(latent_count, columns)
        for t in range(width // tile):
            span = pl.ds(t * tile, tile)
            owners = pl.ds(2 * t, 2)
            value = dot(kv[b], wkv[owners].reshape(tile, 2 * columns), 1, 1)
            extra = scale * dot(gq_rows, wq[owners].reshape(tile, columns), 1, 1)
            for p in range(4):
                at = p * rows
                joined[b, p // 2, p % 2, pl.ds(0, local_media), span] = value[at : at + local_media].astype(BF)
                joined[b, p // 2, p % 2, pl.ds(local_media, local_latents), span] = (
                    value[at + local_media : at + rows] + extra[p * local_latents : (p + 1) * local_latents]
                ).astype(BF)
        lands = [tokens.at[pl.ds((2 * b + side) * rows, rows)] for side in range(2)]
        scatters.append(HeadScatter(place, joined.at[b], lands, back.at[pl.ds(b * rows, rows)]))
        if b > 0:
            scatters[b - 1].forward()
    scatters[-1].forward()
    ring(each)
    out_scatter.second()
    ring(each)
    out_scatter.third()

    def combine(copies, own, slab, result):
        own.wait()
        for copy in copies:
            copy.wait_recv()
        stores = []
        for k in range(SPREAD):
            grad = slab[k].astype(F32)
            for group in range(1, count // SPREAD):
                grad = grad + slab[group * SPREAD + k].astype(F32)
            span = pl.ds(k * block_rows, block_rows)
            pre[span] = grad
            stores.append(place.local(pre.at[span], result.at[:, pl.ds(k * hidden, hidden)]))
        return stores

    combined = combine(up_sums, up_own, up_in, o_up)
    for b in range(items):
        grad = scatters[b].finish()
        if b > 0:
            store.wait()
        for f in range(local_frames):
            span = slice(f * P_SIZE, (f + 1) * P_SIZE)
            dx, dg, db = norm_back(grad[span], media[b, span].astype(F32) + time_rows[f], small[0:1])
            mstage[span] = dx
            sums[0:1] += dg
            sums[1:2] += db
            sums[pl.ds(6 + place.head * local_frames + f, 1), :] += jnp.sum(dx, axis=0, keepdims=True)
        store = place.local(mstage, o_media.at[b])
        dx, dg, db = norm_back(grad[local_media:], latents[b].astype(F32), small[2:3])
        sums[2:3] += dg
        sums[3:4] += db
        o_lgrad[b] = gmiddle[pl.ds(b * local_latents, local_latents)] + dx
        if b == 0:
            for copy in combined:
                copy.wait()
            combined = combine(down_sums, down_own, down_in, o_down)
        ring((each, each, each, 0)[b])

    lanes = sum_in.shape[2]
    sum_copies = []
    for k in range(1, count):
        to = place.other(k)
        at = pl.multiple_of(window(block_rows, to), 128)
        sum_copies.append(
            place.send(sums.at[:, pl.ds(at, lanes)], sum_in.at[item], {"item": to, "head": place.head})
        )
    sum_in[item] = sums[:, pl.ds(pl.multiple_of(window(block_rows, item), 128), lanes)]
    o_out[...] = (middle[...] + out_scatter.finish()).astype(BF).reshape(o_out.shape)
    ring(each)
    for copy in sum_copies:
        copy.wait_recv()
    value = jnp.sum(sum_in[...], axis=0)
    sum_head[0] = value
    head_copies = [
        place.send(sum_head.at[0], sum_head.at[k], device)
        for k, device in ((1, place.sibling), (2, place.across), (3, place.opposite))
    ]
    ring()
    for copy in head_copies:
        copy.wait_recv()
    total = jnp.sum(sum_head[...], axis=0)
    o_small[...] = pltpu.roll(total, (lanes - shift) % lanes, 1)
    place.drain()
    store.wait()
    for copy in combined:
        copy.wait()
    assert place.used <= sems.shape[0], place.used


def hand_over(*refs):
    third = (len(refs) - 1) // 3
    sources, targets, stages, sems = refs[:third], refs[third : 2 * third], refs[2 * third : -1], refs[-1]
    loads = [pltpu.make_async_copy(a, b, sems.at[0, k]) for k, (a, b) in enumerate(zip(sources, stages))]
    stores = [pltpu.make_async_copy(a, b, sems.at[1, k]) for k, (a, b) in enumerate(zip(stages, targets))]
    for copy in loads:
        copy.start()
    for load, store in zip(loads, stores):
        load.wait()
        store.start()
    for copy in stores:
        copy.wait()


def kernel_step(
    count, media, latents, cotangent, frame_counts,
    query_weight, key_weight, value_weight, output_weight, up_weight, down_weight,
    media_gain, media_bias, latent_gain, latent_bias, ffn_gain, ffn_bias, time_embed,
):
    items, local_media, width = media.shape
    local_latents = latents.shape[1]
    frames = time_embed.shape[0]
    block_rows, columns = query_weight.shape
    hidden = up_weight.shape[1] // SPREAD
    rows = local_media + local_latents
    keys_count = 4 * rows
    own_latents = items * local_latents
    stacked = columns // HEAD_DIM * 4 * local_latents
    group = 2 * SPREAD
    row = lax.broadcasted_iota(jnp.int32, (16, 256), 0)
    small = jnp.zeros((16, 256), F32)
    for k, vector in enumerate(
        (media_gain, media_bias, latent_gain, latent_bias, ffn_gain, ffn_bias)
    ):
        padded = jnp.pad(vector.astype(F32), (0, 256 - block_rows))
        small = jnp.where(row == k, padded[None, :], small)
    small = small + jnp.pad(
        time_embed.astype(F32), ((6, 10 - frames), (0, 256 - block_rows))
    )

    def hbm(*shape, kind=BF):
        return jax.ShapeDtypeStruct(shape, kind)

    def buf(*shape, kind=BF):
        return pltpu.VMEM(shape, kind)

    vmem, anywhere = pl.BlockSpec(memory_space=pltpu.VMEM), pl.BlockSpec(memory_space=pl.ANY)
    all_rows = 2 * group * own_latents
    sum_rows = items * 2 * rows
    slab = (count, block_rows, hidden)
    results = pl.pallas_call(
        functools.partial(layer_kernel, count),
        out_shape=[
            hbm(*latents.shape),
            hbm(*latents.shape, kind=F32),
            hbm(*media.shape, kind=F32),
        ]
        + [hbm(block_rows, columns, kind=F32)] * 4
        + [hbm(block_rows, SPREAD * hidden, kind=F32)] * 2
        + [hbm(16, 256, kind=F32)],
        in_specs=[vmem, pl.BlockSpec(memory_space=pltpu.SMEM)] + [anywhere] * 9,
        out_specs=[vmem, vmem, anywhere] + [vmem] * 4 + [anywhere] * 2 + [vmem],
        scratch_shapes=[
            buf(*media.shape),
            buf(*latents.shape),
            buf(*latents.shape),
            buf(items, 2, 2, rows, width),
            buf(items, keys_count, 2 * columns),
            buf(4, own_latents, columns),
            buf(items, stacked, keys_count, kind=F32),
            buf(4, own_latents, columns),
            buf(4, own_latents, width),
            buf(count, block_rows, 2 * columns),
            buf(count, block_rows, columns),
            buf(count, block_rows, columns),
            buf(*slab),
            buf(*slab),
            buf(max(all_rows, sum_rows), width),
            buf(all_rows, width),
            buf(all_rows, hidden, kind=F32),
            buf(all_rows, hidden),
            buf(all_rows, hidden),
            buf(max(all_rows, items * rows), width),
            buf(*slab),
            buf(*slab),
            buf(own_latents, width, kind=F32),
            buf(own_latents, width, kind=F32),
            buf(16, width, kind=F32),
            buf(count, 16, 256),
            buf(2, 2, own_latents, width),
            buf(2, own_latents, width),
            buf(own_latents, width),
            buf(group * own_latents, width),
            buf(group - 1, own_latents, width),
            buf(group - 1, own_latents, width),
            buf(4, own_latents, columns),
            buf(4, own_latents, columns),
            buf(count, block_rows, 2 * columns),
            buf(8, count - 1, block_rows // 2, columns),
            buf(*slab),
            buf(*slab),
            buf(local_media, width, kind=F32),
            buf(16, width, kind=F32),
            buf(count, 16, 256, kind=F32),
            buf(4, 16, 256, kind=F32),
            pltpu.SemaphoreType.DMA((512,)),
        ],
        compiler_params=pltpu.CompilerParams(
            collective_id=0, has_side_effects=True, vmem_limit_bytes=62 * 2**20
        ),
        name="layer",
    )(
        small, frame_counts, media, latents, cotangent, query_weight, key_weight, value_weight,
        output_weight, up_weight, down_weight,
    )
    shapes = [jax.ShapeDtypeStruct(r.shape, r.dtype) for r in results]
    results = pl.pallas_call(
        hand_over,
        out_shape=shapes,
        in_specs=[anywhere] * len(shapes),
        out_specs=[anywhere] * len(shapes),
        scratch_shapes=[pltpu.VMEM(s.shape, s.dtype) for s in shapes]
        + [pltpu.SemaphoreType.DMA((2, len(shapes)))],
        compiler_params=pltpu.CompilerParams(vmem_limit_bytes=60 * 2**20),
        name="hand_over",
    )(*results)
    sums = results[9]
    return (
        *results[:9],
        *(sums[k, :block_rows] for k in range(6)),
        sums[6 : 6 + frames, :block_rows],
    )


def fits(mesh, media, query_weight, up_weight):
    count, heads = mesh.shape["item"], mesh.shape["head"]
    width, columns = query_weight.shape[0], query_weight.shape[1] // heads
    hidden = up_weight.shape[1] // heads
    block_rows = width // count
    return (
        heads == 4
        and count == 2 * SPREAD
        and block_rows % 64 == 0
        and columns % 128 == 0
        and hidden % (128 * SPREAD) == 0
    )


def solution(mesh):
    rows = P("item", "head", None)
    block = P("item", "head")
    vector = P("item")
    table = P(None, "item")

    def run(*arrays):
        count = mesh.shape["item"]
        step = plain_step
        if fits(mesh, arrays[0], arrays[4], arrays[8]):
            step = functools.partial(kernel_step, count)
        return jax.shard_map(
            step,
            mesh=mesh,
            in_specs=(rows,) * 3 + (vector,) + (block,) * 6 + (vector,) * 6 + (table,),
            out_specs=(rows,) * 3 + (block,) * 6 + (vector,) * 6 + (table,),
            check_vma=False,
        )(*arrays)

    return run
```

```python
import functools

import jax
import jax.numpy as jnp
from jax import lax
from jax.experimental import pallas as pl
from jax.experimental.pallas import tpu as pltpu
from jax.sharding import PartitionSpec as P

HEAD_DIM = 96
P_SIZE = 64
EPS = 1e-05
BF = jnp.bfloat16
F32 = jnp.float32


def norm_forward(rows, gain, bias):
    mean = jnp.mean(rows, axis=-1, keepdims=True)
    centered = rows - mean
    inverse = lax.rsqrt(jnp.mean(centered * centered, axis=-1, keepdims=True) + EPS)
    normed = centered * inverse
    return normed * gain + bias, normed, inverse


def norm_backward(upstream, normed, inverse, gain):
    scaled = upstream * gain
    first = jnp.mean(scaled, axis=-1, keepdims=True)
    second = jnp.mean(scaled * normed, axis=-1, keepdims=True)
    axes = tuple(range(upstream.ndim - 1))
    return (
        inverse * (scaled - first - normed * second),
        jnp.sum(upstream * normed, axis=axes),
        jnp.sum(upstream, axis=axes),
    )


def dot(left, right, a, b):
    return lax.dot_general(left, right, (((a,), (b,)), ((), ())), preferred_element_type=F32)


def gather_rows(rows):
    return lax.all_gather(rows, "head", axis=1, tiled=True)


def scatter_rows(rows):
    return lax.psum_scatter(rows.astype(BF), "head", scatter_dimension=1, tiled=True).astype(F32)


def item_scatter(grad):
    return lax.psum_scatter(grad.astype(BF), "item", scatter_dimension=0, tiled=True).astype(F32)


def plain_step(
    media, latents, cotangent, frame_counts,
    query_weight, key_weight, value_weight, output_weight, up_weight, down_weight,
    media_gain, media_bias, latent_gain, latent_bias, ffn_gain, ffn_bias, time_embed,
):
    items, local_media, width = media.shape
    frames = time_embed.shape[0]
    local_frames = local_media // P_SIZE
    place = lax.axis_index("head")
    scale = HEAD_DIM ** (-0.5)
    small = jnp.concatenate(
        [jnp.stack([media_gain, media_bias, latent_gain, latent_bias, ffn_gain, ffn_bias]), time_embed]
    )
    small = lax.all_gather(small, "item", axis=1, tiled=True).astype(F32)
    g_media, b_media, g_latent, b_latent, g_ffn, b_ffn = (small[k] for k in range(6))
    time_rows = lax.dynamic_slice_in_dim(small[6:], place * local_frames, local_frames, 0)
    w_query, w_key, w_value, w_output, w_up, w_down = (
        lax.all_gather(w, "item", axis=0, tiled=True)
        for w in (query_weight, key_weight, value_weight, output_weight, up_weight, down_weight)
    )
    shifted = (
        media.astype(F32).reshape(items, local_frames, P_SIZE, width) + time_rows[None, :, None, :]
    ).reshape(media.shape)
    media_norm, media_hat, media_inv = norm_forward(shifted, g_media, b_media)
    latent_f = latents.astype(F32)
    latent_norm, latent_hat, latent_inv = norm_forward(latent_f, g_latent, b_latent)
    media_all = gather_rows(media_norm.astype(BF))
    latent_all = gather_rows(latent_norm.astype(BF))
    upstream = gather_rows(cotangent)
    media_count, latent_count = media_all.shape[1], latent_all.shape[1]
    joined = jnp.concatenate([media_all, latent_all], axis=1)
    key_count = joined.shape[1]
    local_heads = w_query.shape[1] // HEAD_DIM
    query = (scale * dot(latent_all, w_query, 2, 0)).astype(BF)
    keys = dot(joined, w_key, 2, 0).astype(BF)
    values = dot(joined, w_value, 2, 0).astype(BF)
    query_h = query.reshape(items, latent_count, local_heads, HEAD_DIM)
    key_h = keys.reshape(items, key_count, local_heads, HEAD_DIM)
    value_h = values.reshape(items, key_count, local_heads, HEAD_DIM)
    index = jnp.arange(key_count, dtype=jnp.int32)
    valid = (index[None, :] // P_SIZE < frame_counts[:, None]) | (index[None, :] >= media_count)
    valid = valid[:, None, None, :]

    def mix(spec, left, right):
        return jnp.einsum(spec, left, right, preferred_element_type=F32)

    scores = jnp.where(valid, mix("blhe,bnhe->bhln", query_h, key_h), -1e30)
    peak = jnp.max(scores, axis=-1, keepdims=True)
    expo = jnp.exp(scores - peak)
    weights = expo / jnp.sum(expo, axis=-1, keepdims=True)
    weights_low = weights.astype(BF)
    mixed = mix("bhln,bnhe->blhe", weights_low, value_h).reshape(items, latent_count, -1).astype(BF)
    middle = latent_f + scatter_rows(dot(mixed, w_output, 2, 1))
    ffn_norm, ffn_hat, ffn_inv = norm_forward(middle, g_ffn, b_ffn)
    ffn_all = gather_rows(ffn_norm.astype(BF))
    rows = items * latent_count
    ffn_rows = ffn_all.reshape(rows, width)
    up_rows = upstream.reshape(rows, width)
    pre = dot(ffn_rows, w_up, 1, 0)
    act, gelu_back = jax.vjp(jax.nn.gelu, pre)
    act = act.astype(BF)
    ffn_out = scatter_rows(dot(act, w_down, 1, 1).reshape(items, latent_count, width))
    output = (middle + ffn_out).astype(BF)
    grad_down = dot(up_rows, act, 0, 0)
    grad_pre = gelu_back(dot(up_rows, w_down, 1, 0))[0].astype(BF)
    grad_up = dot(ffn_rows, grad_pre, 0, 0)
    grad_ffn = scatter_rows(dot(grad_pre, w_up, 1, 1).reshape(items, latent_count, width))
    grad_mid, grad_fgain, grad_fbias = norm_backward(grad_ffn, ffn_hat, ffn_inv, g_ffn)
    grad_middle = cotangent.astype(F32) + grad_mid
    attended_grad = gather_rows(grad_middle.astype(BF)).reshape(rows, width)
    grad_output = dot(attended_grad, mixed.reshape(rows, -1), 0, 0)
    grad_mixed = dot(attended_grad, w_output, 1, 0).astype(BF)
    gm_h = grad_mixed.reshape(items, latent_count, local_heads, HEAD_DIM)
    grad_values = mix("bhln,blhe->bnhe", weights_low, gm_h).astype(BF).reshape(items * key_count, -1)
    grad_weights = mix("blhe,bnhe->bhln", gm_h, value_h)
    inner = jnp.sum(weights * grad_weights, axis=-1, keepdims=True)
    grad_scores = (weights * (grad_weights - inner)).astype(BF)
    grad_query = mix("bhln,bnhe->blhe", grad_scores, key_h).astype(BF).reshape(rows, -1)
    grad_keys = mix("bhln,blhe->bnhe", grad_scores, query_h).astype(BF).reshape(items * key_count, -1)
    joined_rows = joined.reshape(items * key_count, width)
    grad_wquery = scale * dot(latent_all.reshape(rows, width), grad_query, 0, 0)
    grad_wkey = dot(joined_rows, grad_keys, 0, 0)
    grad_wvalue = dot(joined_rows, grad_values, 0, 0)
    grad_joined = dot(grad_keys, w_key, 1, 1) + dot(grad_values, w_value, 1, 1)
    grad_joined = grad_joined.reshape(items, key_count, width)
    grad_latent_all = grad_joined[:, media_count:] + scale * dot(grad_query, w_query, 1, 1).reshape(
        items, latent_count, width
    )
    media_back = scatter_rows(grad_joined[:, :media_count])
    latent_back = scatter_rows(grad_latent_all)
    grad_media, grad_mgain, grad_mbias = norm_backward(media_back, media_hat, media_inv, g_media)
    grad_lat, grad_lgain, grad_lbias = norm_backward(latent_back, latent_hat, latent_inv, g_latent)
    time_local = jnp.sum(grad_media.reshape(items, local_frames, P_SIZE, width), axis=(0, 2))
    grad_time = lax.dynamic_update_slice_in_dim(
        jnp.zeros((frames, width), F32), time_local, place * local_frames, 0
    )
    smalls = jnp.concatenate(
        [jnp.stack([grad_mgain, grad_mbias, grad_lgain, grad_lbias, grad_fgain, grad_fbias]), grad_time]
    )
    smalls = lax.psum_scatter(smalls, ("item",), scatter_dimension=1, tiled=True)
    smalls = lax.psum(smalls, "head")
    return (
        output,
        grad_middle + grad_lat,
        grad_media,
        *(item_scatter(g) for g in (grad_wquery, grad_wkey, grad_wvalue, grad_output, grad_up, grad_down)),
        *(smalls[k] for k in range(6)),
        smalls[6:],
    )


MESH = pl.DeviceIdType.MESH
VMEM = pltpu.VMEM
ANY = pl.ANY
SPREAD = 4


class Place:
    def __init__(self, count, sems, chip_rows):
        self.count = count
        self.rows = chip_rows
        self.sems = sems
        self.used = 0
        self.sent = []
        i, h = lax.axis_index("item"), lax.axis_index("head")
        self.item, self.head = i, h
        self.y, self.core = h // 2, h % 2
        self.quarter = i % SPREAD
        self.group = i // SPREAD
        odd = i % 2
        self.spot = (1 - odd) * (i // 2) + odd * (count - 1 - i // 2)
        self.sibling = {"item": i, "head": 2 * self.y + 1 - self.core}
        self.across = {"item": i, "head": 2 * (1 - self.y) + self.core}
        self.opposite = {"item": i, "head": 2 * (1 - self.y) + 1 - self.core}
        self.chip = 2 * self.quarter + self.y

    def ring(self, spot):
        spot = (spot + self.count) % self.count
        back = spot // (self.count // 2)
        return (1 - back) * 2 * spot + back * (2 * (self.count - 1 - spot) + 1)

    def member(self, k):
        bits = [self.quarter // 2, self.quarter % 2, self.y]
        want = [k // 4, (k // 2) % 2, k % 2]
        a, b, y = (u + w - 2 * u * w for u, w in zip(bits, want))
        quarter = 2 * a + b
        device = {"item": self.group * SPREAD + quarter, "head": 2 * y + self.core}
        return 2 * quarter + y, device

    def chip_rows(self, core, chip):
        rows = self.rows
        return pl.ds(pl.multiple_of((core * 2 * SPREAD + chip) * rows, rows), rows)

    def other(self, k):
        return (self.item + k) % self.count

    def barrier(self):
        sem = pltpu.get_barrier_semaphore()
        peers = [{"item": self.other(k), "head": self.head} for k in range(1, self.count)]
        peers += [self.sibling, self.across, self.opposite]
        peers += [self.member(k)[1] for k in (3, 5, 7)]
        for peer in peers:
            pl.semaphore_signal(sem, inc=1, device_id=peer, device_id_type=MESH)
        pl.semaphore_wait(sem, len(peers))

    def send(self, src, dst, device):
        copy = pltpu.make_async_remote_copy(
            src_ref=src,
            dst_ref=dst,
            send_sem=self.sems.at[self.used],
            recv_sem=self.sems.at[self.used + 1],
            device_id=device,
            device_id_type=MESH,
        )
        self.used += 2
        copy.start()
        self.sent.append(copy)
        return copy

    def local(self, src, dst):
        copy = pltpu.make_async_copy(src, dst, self.sems.at[self.used])
        self.used += 1
        copy.start()
        return copy

    def settle(self, copy):
        copy.wait_send()
        self.sent = [other for other in self.sent if other is not copy]

    def drain(self):
        for copy in self.sent:
            copy.wait_send()


class Pump:
    def __init__(self, steps):
        self.steps = list(steps)
        self.at = 0

    def __call__(self, count=None):
        end = len(self.steps) if count is None else min(self.at + count, len(self.steps))
        while self.at < end:
            self.steps[self.at]()
            self.at += 1


class GatherPipe:
    def __init__(self, place, source, target, way):
        self.place, self.target, self.way = place, target, way
        self.device = {"item": place.ring(place.spot + way), "head": place.head}
        self.copy = place.send(source, target(place.item), self.device)

    def step(self, s):
        self.copy.wait_recv()
        if s < self.place.count - 1:
            part = self.target(self.place.ring(self.place.spot - self.way * s))
            self.copy = self.place.send(part, part, self.device)


class ScatterPipe:
    def __init__(self, place, part, slots, finish, way):
        self.place, self.part, self.slots, self.finish, self.way = place, part, slots, finish, way
        self.device = {"item": place.ring(place.spot + way), "head": place.head}
        self.copy = place.send(part(place.ring(place.spot - way)), slots.at[0], self.device)

    def step(self, s):
        self.copy.wait_recv()
        if s < self.place.count - 2:
            own = self.part(self.place.ring(self.place.spot - self.way * (s + 2)))
            self.slots[s] = (self.slots[s].astype(F32) + own[...].astype(F32)).astype(BF)
            self.copy = self.place.send(self.slots.at[s], self.slots.at[s + 1], self.device)
        else:
            self.finish(self.slots[s].astype(F32) + self.part(self.place.item)[...].astype(F32))


def weave(*pipes, steps):
    return [functools.partial(pipe.step, s) for s in steps for pipe in pipes]


class HeadGather:
    def __init__(self, place, ref):
        self.place, self.ref = place, ref
        own = ref.at[place.y, place.core]
        self.near = place.send(own, own, place.sibling)
        self.far = place.send(own, own, place.across)

    def forward(self):
        place = self.place
        self.far.wait_recv()
        block = self.ref.at[1 - place.y, place.core]
        self.passed = place.send(block, block, place.sibling)

    def finish(self):
        self.near.wait_recv()
        self.passed.wait_recv()

    def settle(self):
        for copy in (self.near, self.far, self.passed):
            self.place.settle(copy)


class HeadScatter:
    def __init__(self, place, part, near, far):
        self.place, self.part, self.near, self.far = place, part, near, far
        self.copies = [
            place.send(part.at[side, 1 - place.core], near[side], place.sibling) for side in range(2)
        ]

    def landed(self, side):
        first, second = self.near[0][...].astype(F32), self.near[1][...].astype(F32)
        return jnp.where(side == 0, first, second)

    def forward(self):
        place, part = self.place, self.part
        for copy in self.copies:
            copy.wait_recv()
        block = part.at[1 - place.y, place.core]
        block[...] = (block[...].astype(F32) + self.landed(1 - place.y)).astype(BF)
        self.copy = place.send(block, self.far, place.across)
        self.copies.append(self.copy)

    def finish(self):
        place = self.place
        own = self.part[place.y, place.core].astype(F32) + self.landed(place.y)
        self.copy.wait_recv()
        return own + self.far[...].astype(F32)

    def settle(self):
        for copy in self.copies:
            self.place.settle(copy)


class GroupGather:
    def __init__(self, place, ref):
        self.place, self.ref = place, ref
        self.copies = {}
        self.passed = []
        self.share(0)

    def block(self, k):
        return self.ref.at[self.place.chip_rows(self.place.core, self.place.member(k)[0])]

    def settle(self):
        for copy in self.passed + list(self.copies.values()):
            self.place.settle(copy)

    def share(self, k):
        self.passed.append(self.place.send(self.block(k), self.block(k), self.place.sibling))

    def push(self, k, *axes):
        for axis in axes:
            self.copies[axis, k] = self.place.send(self.block(k), self.block(k), self.place.member(axis)[1])

    def pull(self, axis, k):
        self.copies[axis, k].wait_recv()
        self.share(axis ^ k)

    def finish(self):
        for copy in self.passed:
            copy.wait_recv()


class GroupScatter:
    def __init__(self, place, part, near, far, order):
        self.place, self.part, self.near, self.far, self.order = place, part, near, far, order
        rows, lanes = near[0].shape
        theirs = pl.ds(pl.multiple_of((1 - place.core) * rows, rows), rows)
        self.passed = [
            place.send(part.at[theirs, pl.ds(k * lanes, lanes)], piece, place.sibling)
            for k, piece in enumerate(near)
        ]
        self.copies = {}
        self.arrived = {}

    def total(self, k):
        chip = self.place.member(k)[0]
        value = self.part[self.place.chip_rows(self.place.core, chip)].astype(F32)
        pieces = [piece[self.place.chip_rows(0, chip)].astype(F32) for piece in self.near]
        if pieces:
            value = value + (pieces[0] if len(pieces) == 1 else jnp.concatenate(pieces, axis=1))
        for axis, slot in self.arrived.get(k, ()):
            self.copies[axis, axis ^ k].wait_recv()
            value = value + self.far[slot].astype(F32)
        return value

    def push(self, axis, k, slot):
        chip, _ = self.place.member(k)
        block = self.part.at[self.place.chip_rows(self.place.core, chip)]
        block[...] = self.total(k).astype(BF)
        self.copies[axis, k] = self.place.send(block, self.far.at[slot], self.place.member(axis)[1])
        self.arrived.setdefault(axis ^ k, []).append((axis, slot))

    def first(self):
        a, b, c = self.order
        for copy in self.passed:
            copy.wait_recv()
        for slot, k in enumerate((a ^ b ^ c, a ^ b, a ^ c, a)):
            self.push(a, k, slot)

    def absorb(self):
        a, b, c = self.order
        for k in (b ^ c, b, c, 0):
            rows = self.place.chip_rows(self.place.core, self.place.member(k)[0])
            near = self.place.chip_rows(0, self.place.member(k)[0])
            pieces = [piece[near].astype(F32) for piece in self.near]
            self.part[rows] = (self.part[rows].astype(F32) + jnp.concatenate(pieces, axis=1)).astype(BF)
        self.near = []

    def second(self):
        a, b, c = self.order
        self.push(b, b ^ c, 4)
        self.push(b, b, 5)

    def third(self):
        a, b, c = self.order
        self.push(c, c, 6)

    def finish(self):
        return self.total(0)

    def settle(self):
        for copy in [*self.passed, *self.copies.values()]:
            self.place.settle(copy)


def head_masks(rows, columns):
    lane = lax.broadcasted_iota(jnp.int32, (rows, columns), 1)
    return [(lane >= at) & (lane < at + HEAD_DIM) for at in range(0, columns, HEAD_DIM)]


def stack_heads(block, masks):
    zero = jnp.zeros_like(block)
    return jnp.concatenate([jnp.where(mask, block, zero) for mask in masks], axis=0)


def fold_heads(block, masks):
    rows = masks[0].shape[0]
    total = 0.0
    for h, mask in enumerate(masks):
        total = total + jnp.where(mask, block[h * rows : (h + 1) * rows], 0.0)
    return total


def norm_parts(rows):
    mean = jnp.mean(rows, axis=-1, keepdims=True)
    centered = rows - mean
    inverse = lax.rsqrt(jnp.mean(centered * centered, axis=-1, keepdims=True) + EPS)
    return centered * inverse, inverse


def norm_back(upstream, rows, gain):
    normed, inverse = norm_parts(rows)
    scaled = upstream * gain
    first = jnp.mean(scaled, axis=-1, keepdims=True)
    second = jnp.mean(scaled * normed, axis=-1, keepdims=True)
    return (
        inverse * (scaled - first - normed * second),
        jnp.sum(upstream * normed, axis=0, keepdims=True),
        jnp.sum(upstream, axis=0, keepdims=True),
    )


def gelu_parts(x):
    root = 0.7978845608028654
    t = jnp.tanh(root * (x + 0.044715 * (x * x * x)))
    half = 0.5 * (1.0 + t)
    return x * half, half + 0.5 * x * (1.0 - t * t) * (root * (1.0 + 3 * 0.044715 * (x * x)))


def window(width, k):
    return (width * k) // 128 * 128


def layer_kernel(
    count,
    small_in, frames_ref, media_in, latents_in, cotangent_in, w_query, w_key, w_value, w_output, w_up, w_down,
    o_out, o_lgrad, o_media, o_query, o_key, o_value, o_output, o_up, o_down, o_small,
    media, latents, cotangent,
    joined, kv, query, weights, mixed, latent, wkv, wq, wo, up, down,
    tokens, upstream, pre, act, gpre, back, gup, gdown, middle, gmiddle, small, smalls, att, att_near, att_far,
    near, far, out_far, gmixed, gquery, gkv, slots, up_in, down_in, mstage, sums, sum_in, sum_head,
    sems,
):
    place = Place(count, sems, latents_in.shape[0] * latents_in.shape[1])
    loads = [
        place.local(media_in, media),
        place.local(latents_in, latents),
        place.local(cotangent_in, cotangent),
    ]
    place.barrier()
    items, local_media, width = media.shape
    local_latents = latents.shape[1]
    rows = local_media + local_latents
    keys_count = 4 * rows
    block_rows, columns = w_query.shape
    hidden = up.shape[2]
    part = block_rows // 2
    latent_count = 4 * local_latents
    all_latents = items * latent_count
    own_latents = items * local_latents
    group_rows = 4 * SPREAD * own_latents
    local_frames = local_media // P_SIZE
    scale = HEAD_DIM ** (-0.5)
    tile = 2 * block_rows
    item, y, core = place.item, place.y, place.core

    shift = block_rows * item % 128
    sum_head[0] = jnp.zeros_like(sum_head[0])
    sum_head[0, :, pl.ds(0, block_rows)] = small_in[...].astype(F32)
    smalls[item] = pltpu.roll(sum_head[0], shift, 1).astype(BF)
    small_copies = [
        place.send(smalls.at[item], smalls.at[item], {"item": place.other(k), "head": place.head})
        for k in range(1, count)
    ]
    for load in loads:
        load.wait()
    own = place.chip_rows(core, place.chip)
    upstream[own] = cotangent[...].reshape(own_latents, width)
    upstream_gather = GroupGather(place, upstream)
    upstream_gather.push(0, 1)

    def gather_pipes(source, slab, lanes):
        made = []
        for half, way in ((0, 1), (1, -1)):
            span = pl.ds(half * part, part)
            made.append(
                GatherPipe(place, source.at[span], lambda o, span=span: slab.at[o, span, lanes], way)
            )
        return made

    whole, second = pl.ds(0, columns), pl.ds(columns, columns)
    ring_pipes = (
        gather_pipes(w_key, wkv, whole)
        + gather_pipes(w_value, wkv, second)
        + gather_pipes(w_query, wq, whole)
        + gather_pipes(w_output, wo, whole)
    )
    ring = Pump(weave(*ring_pipes, steps=range(1, count)))
    each = len(ring_pipes)
    quarter = pl.ds(pl.multiple_of(place.quarter * hidden, 128), hidden)
    owns = [
        place.local(w_key, wkv.at[item, :, whole]),
        place.local(w_value, wkv.at[item, :, second]),
        place.local(w_query, wq.at[item]),
        place.local(w_output, wo.at[item]),
    ]
    own_hidden = [
        place.local(w_up.at[:, quarter], up.at[item]),
        place.local(w_down.at[:, quarter], down.at[item]),
    ]
    for copy in small_copies:
        copy.wait_recv()
    small[...] = jnp.zeros_like(small)
    for j in range(count):
        lanes = pl.ds(window(block_rows, j), smalls.shape[2])
        small[:, lanes] += smalls[j].astype(F32)
    time_rows = [small[pl.ds(6 + place.head * local_frames + f, 1), :] for f in range(local_frames)]

    gathers = []
    for b in range(items):
        for f in range(local_frames):
            span = pl.ds(f * P_SIZE, P_SIZE)
            normed, _ = norm_parts(media[b, span].astype(F32) + time_rows[f])
            joined[b, y, core, span] = (normed * small[0:1] + small[1:2]).astype(BF)
        normed, _ = norm_parts(latents[b].astype(F32))
        joined[b, y, core, pl.ds(local_media, local_latents)] = (
            normed * small[2:3] + small[3:4]
        ).astype(BF)
        gathers.append(HeadGather(place, joined.at[b]))

    def project(b):
        gathers[b].finish()
        kv[b] = dot(joined[b].reshape(keys_count, width), wkv[...].reshape(width, 2 * columns), 1, 0).astype(BF)
        for p in range(4):
            latent[p, pl.ds(b * local_latents, local_latents)] = joined[
                b, p // 2, p % 2, pl.ds(local_media, local_latents)
            ]

    ring(2 * each)
    gathers[0].forward()
    ring(2 * each)
    gathers[1].forward()
    ring(each)
    gathers[2].forward()
    ring()
    upstream_gather.push(0, 4, 2)

    def spread(source, slab, offsets, lanes_of=None):
        copies = []
        for k in offsets:
            to = place.other(k)
            if lanes_of is None:
                block = source.at[to]
            else:
                block = source.at[:, pl.ds(pl.multiple_of((to % SPREAD) * hidden, 128), hidden)]
            copies.append(place.send(block, slab.at[item], {"item": to, "head": place.head}))
        return copies

    straight, turned = (4, 2, 6), (3, 5, 1, 7)
    mixed_order = (4, 3, 5, 2, 6, 1, 7)
    up_copies = spread(w_up, up, mixed_order, hidden)
    gathers[3].forward()
    for copy in owns:
        copy.wait()
    for b in range(items):
        project(b)
    upstream_gather.pull(4, 0)
    upstream_gather.push(4, 2)
    query[...] = (
        (scale * dot(latent[...].reshape(all_latents, width), wq[...].reshape(width, columns), 1, 0))
        .astype(BF)
        .reshape(query.shape)
    )
    masks = head_masks(latent_count, columns)
    index = lax.broadcasted_iota(jnp.int32, (1, keys_count), 1)
    local = index % rows
    frame = jnp.where(local < local_media, (index // rows) * local_frames + local // P_SIZE, -1)
    for b in range(items):
        mine = pl.ds(b * local_latents, local_latents)
        stacked = stack_heads(query[:, mine].reshape(latent_count, columns), masks)
        scores = dot(stacked, kv[b, :, :columns], 1, 1)
        shown = jnp.broadcast_to(frame, scores.shape) < frames_ref[b]
        scores = jnp.where(shown, scores, -1e30)
        expo = jnp.exp(scores - jnp.max(scores, axis=1, keepdims=True))
        weight = expo / jnp.sum(expo, axis=1, keepdims=True)
        weights[b] = weight
        result = fold_heads(dot(weight.astype(BF), kv[b, :, columns:], 1, 0), masks)
        mixed[:, mine] = result.astype(BF).reshape(4, local_latents, columns)
    att[...] = (
        dot(mixed[...].reshape(all_latents, columns), wo[...].reshape(width, columns), 1, 1)
        .astype(BF)
        .reshape(att.shape)
    )
    scatter = HeadScatter(place, att, [att_near.at[0], att_near.at[1]], att_far)
    scatter.forward()
    upstream_gather.push(4, 1)
    upstream_gather.pull(2, 0)
    upstream_gather.push(2, 1)
    middle[...] = latents[...].astype(F32).reshape(middle.shape) + scatter.finish()
    scatter.settle()
    normed, _ = norm_parts(middle[...])
    tokens[own] = (normed * small[4:5] + small[5:6]).astype(BF)
    token_gather = GroupGather(place, tokens)
    token_gather.push(0, 4, 2, 1)
    down_copies = spread(w_down, down, mixed_order, hidden)
    upstream_gather.pull(2, 4)
    upstream_gather.push(6, 1)
    token_gather.pull(4, 0)
    token_gather.push(4, 2, 1)
    token_gather.pull(2, 0)
    token_gather.push(2, 1)
    token_gather.pull(2, 4)
    token_gather.push(6, 1)
    for k in (0, 4, 2, 6):
        upstream_gather.pull(1, k)
    for k in (0, 4, 2, 6):
        token_gather.pull(1, k)
    token_gather.finish()

    for copy in own_hidden:
        copy.wait()
    for copy in up_copies:
        copy.wait_recv()
    blocks = 4
    tall = group_rows // blocks
    spans = [pl.ds(n * tall, tall) for n in range(blocks)]
    for span in spans:
        value, slope = gelu_parts(dot(tokens[span], up[...].reshape(width, hidden), 1, 0))
        act[span] = value.astype(BF)
        pre[span] = slope
    upstream_gather.finish()
    all_rows = pl.ds(0, group_rows)
    for t in range(width // tile):
        span = pl.ds(t * tile, tile)
        gdown[pl.ds(2 * t, 2)] = (
            dot(upstream[all_rows, span], act[...], 0, 0).astype(BF).reshape(2, block_rows, hidden)
        )
    down_sums = spread(gdown, down_in, straight)
    for copy in down_copies:
        copy.wait_recv()
    for span in spans:
        grad_act = dot(upstream[span], down[...].reshape(width, hidden), 1, 0)
        gpre[span] = (grad_act * pre[span]).astype(BF)
        back[span] = dot(gpre[span], up[...].reshape(width, hidden), 1, 1).astype(BF)
    back_scatter = GroupScatter(place, back, [near], far, (1, 2, 4))
    back_scatter.first()
    for t in range(width // tile):
        span = pl.ds(t * tile, tile)
        gup[pl.ds(2 * t, 2)] = (
            dot(tokens[all_rows, span], gpre[...], 0, 0).astype(BF).reshape(2, block_rows, hidden)
        )
    up_sums = spread(gup, up_in, straight)
    down_own = place.local(gdown.at[item], down_in.at[item])
    up_own = place.local(gup.at[item], up_in.at[item])
    upstream_gather.settle()
    token_gather.settle()
    back_scatter.second()
    out = upstream
    for span in spans:
        out[span] = dot(act[span], down[...].reshape(width, hidden), 1, 1).astype(BF)
    back_scatter.third()
    lands = [gkv.at[pl.ds(k * near.shape[0], near.shape[0])] for k in range(2)]
    out_scatter = GroupScatter(place, out, lands, out_far, (1, 2, 4))
    down_sums += spread(gdown, down_in, turned)
    sums[...] = jnp.zeros_like(sums)
    grad_norm = back_scatter.finish()
    back_scatter.settle()

    dx, dg, db = norm_back(grad_norm, middle[...], small[4:5])
    sums[4:5] = dg
    sums[5:6] = db
    grad_middle = cotangent[...].astype(F32).reshape(middle.shape) + dx
    gmiddle[...] = grad_middle
    gatt = att
    gatt[y, core] = grad_middle.astype(BF)
    att_gather = HeadGather(place, gatt)
    out_scatter.first()
    out_scatter.absorb()
    up_sums += spread(gup, up_in, turned)
    att_gather.forward()
    att_gather.finish()
    go, gq = up, down
    gmixed[...] = (
        dot(gatt[...].reshape(all_latents, width), wo[...].reshape(width, columns), 1, 0)
        .astype(BF)
        .reshape(gmixed.shape)
    )
    for t in range(width // tile):
        span = pl.ds(t * tile, tile)
        go[pl.ds(2 * t, 2)] = (
            dot(gatt[:, :, :, span].reshape(all_latents, tile), mixed[...].reshape(all_latents, columns), 0, 0)
            .astype(BF)
            .reshape(2, block_rows, columns)
        )

    def scatter_pipes(first_slot, slab, lanes, result):
        made = []
        for half, way in ((0, 1), (1, -1)):
            span = pl.ds(half * part, part)

            def finish(value, span=span):
                result[span] = value

            def of_owner(o, half=half):
                if len(slab.shape) == 3:
                    return slab.at[o, pl.ds(half * part, part), lanes]
                return slab.at[pl.ds(pl.multiple_of(o * block_rows + half * part, part), part), lanes]

            made.append(
                ScatterPipe(
                    place,
                    of_owner,
                    slots.at[first_slot + half],
                    finish,
                    way,
                )
            )
        return made

    go_pipes = scatter_pipes(0, go, whole, o_output)

    for b in range(items):
        mine = pl.ds(b * local_latents, local_latents)
        q_stack = stack_heads(query[:, mine].reshape(latent_count, columns), masks)
        g_stack = stack_heads(gmixed[:, mine].reshape(latent_count, columns), masks)
        weight = weights[b]
        grad_weight = dot(g_stack, kv[b, :, columns:], 1, 1)
        inner = jnp.sum(weight * grad_weight, axis=1, keepdims=True)
        grad_score = (weight * (grad_weight - inner)).astype(BF)
        gq_rows = fold_heads(dot(grad_score, kv[b, :, :columns], 1, 0), masks).astype(BF)
        gquery[:, mine] = gq_rows.reshape(4, local_latents, columns)
        kv[b, :, :columns] = dot(grad_score, q_stack, 0, 0).astype(BF)
        kv[b, :, columns:] = dot(weight.astype(BF), g_stack, 0, 0).astype(BF)
    for t in range(width // tile):
        span = pl.ds(t * tile, tile)
        gkv[span] = dot(
            joined[:, :, :, :, span].reshape(items * keys_count, tile),
            kv[...].reshape(items * keys_count, 2 * columns),
            0,
            0,
        ).astype(BF)
    kv_pipes = scatter_pipes(2, gkv, whole, o_key) + scatter_pipes(4, gkv, second, o_value)
    for t in range(width // tile):
        span = pl.ds(t * tile, tile)
        gq[pl.ds(2 * t, 2)] = (
            (scale * dot(latent[:, :, span].reshape(all_latents, tile), gquery[...].reshape(all_latents, columns), 0, 0))
            .astype(BF)
            .reshape(2, block_rows, columns)
        )
    q_pipes = scatter_pipes(6, gq, whole, o_query)
    steps = weave(*go_pipes, steps=[0])
    for s in range(count - 1):
        steps += weave(*kv_pipes, *q_pipes, steps=[s])
        if s + 1 < count - 1:
            steps += weave(*go_pipes, steps=[s + 1])
    ring = Pump(steps)
    scatters = []
    for gather in gathers:
        gather.settle()
    for b in range(items):
        mine = pl.ds(b * local_latents, local_latents)
        gq_rows = gquery[:, mine].reshape(latent_count, columns)
        for t in range(width // tile):
            span = pl.ds(t * tile, tile)
            owners = pl.ds(2 * t, 2)
            value = dot(kv[b], wkv[owners].reshape(tile, 2 * columns), 1, 1)
            extra = scale * dot(gq_rows, wq[owners].reshape(tile, columns), 1, 1)
            for p in range(4):
                at = p * rows
                joined[b, p // 2, p % 2, pl.ds(0, local_media), span] = value[at : at + local_media].astype(BF)
                joined[b, p // 2, p % 2, pl.ds(local_media, local_latents), span] = (
                    value[at + local_media : at + rows] + extra[p * local_latents : (p + 1) * local_latents]
                ).astype(BF)
        lands = [tokens.at[pl.ds((2 * b + side) * rows, rows)] for side in range(2)]
        scatters.append(HeadScatter(place, joined.at[b], lands, back.at[pl.ds(b * rows, rows)]))
        if b > 0:
            scatters[b - 1].forward()
        if b == 1:
            out_scatter.second()
    scatters[-1].forward()
    ring(each)
    out_scatter.third()
    ring(each)

    def combine(copies, own, slab, result):
        own.wait()
        for copy in copies:
            copy.wait_recv()
        stores = []
        for k in range(SPREAD):
            grad = slab[k].astype(F32)
            for group in range(1, count // SPREAD):
                grad = grad + slab[group * SPREAD + k].astype(F32)
            span = pl.ds(k * block_rows, block_rows)
            pre[span] = grad
            stores.append(place.local(pre.at[span], result.at[:, pl.ds(k * hidden, hidden)]))
        return stores

    combined = combine(up_sums, up_own, up_in, o_up)
    for b in range(items):
        grad = scatters[b].finish()
        if b > 0:
            store.wait()
        for f in range(local_frames):
            span = slice(f * P_SIZE, (f + 1) * P_SIZE)
            dx, dg, db = norm_back(grad[span], media[b, span].astype(F32) + time_rows[f], small[0:1])
            mstage[span] = dx
            sums[0:1] += dg
            sums[1:2] += db
            sums[pl.ds(6 + place.head * local_frames + f, 1), :] += jnp.sum(dx, axis=0, keepdims=True)
        store = place.local(mstage, o_media.at[b])
        dx, dg, db = norm_back(grad[local_media:], latents[b].astype(F32), small[2:3])
        sums[2:3] += dg
        sums[3:4] += db
        o_lgrad[b] = gmiddle[pl.ds(b * local_latents, local_latents)] + dx
        if b == 0:
            for copy in combined:
                copy.wait()
            combined = combine(down_sums, down_own, down_in, o_down)
        ring((each, each, each, 0)[b])

    lanes = sum_in.shape[2]
    sum_copies = []
    for k in range(1, count):
        to = place.other(k)
        at = pl.multiple_of(window(block_rows, to), 128)
        sum_copies.append(
            place.send(sums.at[:, pl.ds(at, lanes)], sum_in.at[item], {"item": to, "head": place.head})
        )
    sum_in[item] = sums[:, pl.ds(pl.multiple_of(window(block_rows, item), 128), lanes)]
    o_out[...] = (middle[...] + out_scatter.finish()).astype(BF).reshape(o_out.shape)
    ring(each)
    for copy in sum_copies:
        copy.wait_recv()
    value = jnp.sum(sum_in[...], axis=0)
    sum_head[0] = value
    head_copies = [
        place.send(sum_head.at[0], sum_head.at[k], device)
        for k, device in ((1, place.sibling), (2, place.across), (3, place.opposite))
    ]
    ring()
    for copy in head_copies:
        copy.wait_recv()
    total = jnp.sum(sum_head[...], axis=0)
    o_small[...] = pltpu.roll(total, (lanes - shift) % lanes, 1)
    place.drain()
    store.wait()
    for copy in combined:
        copy.wait()
    assert place.used <= sems.shape[0], place.used


def hand_over(*refs):
    third = (len(refs) - 1) // 3
    sources, targets, stages, sems = refs[:third], refs[third : 2 * third], refs[2 * third : -1], refs[-1]
    loads = [pltpu.make_async_copy(a, b, sems.at[0, k]) for k, (a, b) in enumerate(zip(sources, stages))]
    stores = [pltpu.make_async_copy(a, b, sems.at[1, k]) for k, (a, b) in enumerate(zip(stages, targets))]
    for copy in loads:
        copy.start()
    for load, store in zip(loads, stores):
        load.wait()
        store.start()
    for copy in stores:
        copy.wait()


def kernel_step(
    count, media, latents, cotangent, frame_counts,
    query_weight, key_weight, value_weight, output_weight, up_weight, down_weight,
    media_gain, media_bias, latent_gain, latent_bias, ffn_gain, ffn_bias, time_embed,
):
    items, local_media, width = media.shape
    local_latents = latents.shape[1]
    frames = time_embed.shape[0]
    block_rows, columns = query_weight.shape
    hidden = up_weight.shape[1] // SPREAD
    rows = local_media + local_latents
    keys_count = 4 * rows
    own_latents = items * local_latents
    stacked = columns // HEAD_DIM * 4 * local_latents
    group = 2 * SPREAD
    row = lax.broadcasted_iota(jnp.int32, (16, block_rows), 0)
    small = jnp.zeros((16, block_rows), BF)
    vectors = (media_gain, media_bias, latent_gain, latent_bias, ffn_gain, ffn_bias)
    for k, vector in enumerate(vectors):
        small = jnp.where(row == k, vector[None, :], small)
    for f in range(frames):
        small = jnp.where(row == len(vectors) + f, time_embed[f : f + 1], small)

    def hbm(*shape, kind=BF):
        return jax.ShapeDtypeStruct(shape, kind)

    def buf(*shape, kind=BF):
        return pltpu.VMEM(shape, kind)

    vmem, anywhere = pl.BlockSpec(memory_space=pltpu.VMEM), pl.BlockSpec(memory_space=pl.ANY)
    all_rows = 2 * group * own_latents
    sum_rows = items * 2 * rows
    slab = (count, block_rows, hidden)
    results = pl.pallas_call(
        functools.partial(layer_kernel, count),
        out_shape=[
            hbm(*latents.shape),
            hbm(*latents.shape, kind=F32),
            hbm(*media.shape, kind=F32),
        ]
        + [hbm(block_rows, columns, kind=F32)] * 4
        + [hbm(block_rows, SPREAD * hidden, kind=F32)] * 2
        + [hbm(16, 256, kind=F32)],
        in_specs=[vmem, pl.BlockSpec(memory_space=pltpu.SMEM)] + [anywhere] * 9,
        out_specs=[vmem, vmem, anywhere] + [vmem] * 4 + [anywhere] * 2 + [vmem],
        scratch_shapes=[
            buf(*media.shape),
            buf(*latents.shape),
            buf(*latents.shape),
            buf(items, 2, 2, rows, width),
            buf(items, keys_count, 2 * columns),
            buf(4, own_latents, columns),
            buf(items, stacked, keys_count, kind=F32),
            buf(4, own_latents, columns),
            buf(4, own_latents, width),
            buf(count, block_rows, 2 * columns),
            buf(count, block_rows, columns),
            buf(count, block_rows, columns),
            buf(*slab),
            buf(*slab),
            buf(max(all_rows, sum_rows), width),
            buf(all_rows, width),
            buf(all_rows, hidden, kind=F32),
            buf(all_rows, hidden),
            buf(all_rows, hidden),
            buf(max(all_rows, items * rows), width),
            buf(*slab),
            buf(*slab),
            buf(own_latents, width, kind=F32),
            buf(own_latents, width, kind=F32),
            buf(16, width, kind=F32),
            buf(count, 16, 256),
            buf(2, 2, own_latents, width),
            buf(2, own_latents, width),
            buf(own_latents, width),
            buf(group * own_latents, width),
            buf(group - 1, own_latents, width),
            buf(group - 1, own_latents, width),
            buf(4, own_latents, columns),
            buf(4, own_latents, columns),
            buf(width, 2 * columns),
            buf(8, count - 1, block_rows // 2, columns),
            buf(*slab),
            buf(*slab),
            buf(local_media, width, kind=F32),
            buf(16, width, kind=F32),
            buf(count, 16, 256, kind=F32),
            buf(4, 16, 256, kind=F32),
            pltpu.SemaphoreType.DMA((512,)),
        ],
        compiler_params=pltpu.CompilerParams(
            collective_id=0, has_side_effects=True, vmem_limit_bytes=62 * 2**20
        ),
        name="layer",
    )(
        small, frame_counts, media, latents, cotangent, query_weight, key_weight, value_weight,
        output_weight, up_weight, down_weight,
    )
    shapes = [jax.ShapeDtypeStruct(r.shape, r.dtype) for r in results]
    results = pl.pallas_call(
        hand_over,
        out_shape=shapes,
        in_specs=[anywhere] * len(shapes),
        out_specs=[anywhere] * len(shapes),
        scratch_shapes=[pltpu.VMEM(s.shape, s.dtype) for s in shapes]
        + [pltpu.SemaphoreType.DMA((2, len(shapes)))],
        compiler_params=pltpu.CompilerParams(vmem_limit_bytes=60 * 2**20),
        name="hand_over",
    )(*results)
    sums = results[9]
    return (
        *results[:9],
        *(sums[k, :block_rows] for k in range(6)),
        sums[6 : 6 + frames, :block_rows],
    )


def fits(mesh, media, query_weight, up_weight):
    count, heads = mesh.shape["item"], mesh.shape["head"]
    width, columns = query_weight.shape[0], query_weight.shape[1] // heads
    hidden = up_weight.shape[1] // heads
    block_rows = width // count
    return (
        heads == 4
        and count == 2 * SPREAD
        and block_rows % 64 == 0
        and columns % 128 == 0
        and hidden % (128 * SPREAD) == 0
    )


def solution(mesh):
    rows = P("item", "head", None)
    block = P("item", "head")
    vector = P("item")
    table = P(None, "item")

    def run(*arrays):
        count = mesh.shape["item"]
        step = plain_step
        if fits(mesh, arrays[0], arrays[4], arrays[8]):
            step = functools.partial(kernel_step, count)
        return jax.shard_map(
            step,
            mesh=mesh,
            in_specs=(rows,) * 3 + (vector,) + (block,) * 6 + (vector,) * 6 + (table,),
            out_specs=(rows,) * 3 + (block,) * 6 + (vector,) * 6 + (table,),
            check_vma=False,
        )(*arrays)

    return run
```

```python
import functools

import jax
import jax.numpy as jnp
from jax import lax
from jax.experimental import pallas as pl
from jax.experimental.pallas import tpu as pltpu
from jax.sharding import PartitionSpec as P

HEAD_DIM = 96
P_SIZE = 64
EPS = 1e-05
BF = jnp.bfloat16
F32 = jnp.float32


def norm_forward(rows, gain, bias):
    mean = jnp.mean(rows, axis=-1, keepdims=True)
    centered = rows - mean
    inverse = lax.rsqrt(jnp.mean(centered * centered, axis=-1, keepdims=True) + EPS)
    normed = centered * inverse
    return normed * gain + bias, normed, inverse


def norm_backward(upstream, normed, inverse, gain):
    scaled = upstream * gain
    first = jnp.mean(scaled, axis=-1, keepdims=True)
    second = jnp.mean(scaled * normed, axis=-1, keepdims=True)
    axes = tuple(range(upstream.ndim - 1))
    return (
        inverse * (scaled - first - normed * second),
        jnp.sum(upstream * normed, axis=axes),
        jnp.sum(upstream, axis=axes),
    )


def dot(left, right, a, b):
    return lax.dot_general(left, right, (((a,), (b,)), ((), ())), preferred_element_type=F32)


def gather_rows(rows):
    return lax.all_gather(rows, "head", axis=1, tiled=True)


def scatter_rows(rows):
    return lax.psum_scatter(rows.astype(BF), "head", scatter_dimension=1, tiled=True).astype(F32)


def item_scatter(grad):
    return lax.psum_scatter(grad.astype(BF), "item", scatter_dimension=0, tiled=True).astype(F32)


def plain_step(
    media, latents, cotangent, frame_counts,
    query_weight, key_weight, value_weight, output_weight, up_weight, down_weight,
    media_gain, media_bias, latent_gain, latent_bias, ffn_gain, ffn_bias, time_embed,
):
    items, local_media, width = media.shape
    frames = time_embed.shape[0]
    local_frames = local_media // P_SIZE
    place = lax.axis_index("head")
    scale = HEAD_DIM ** (-0.5)
    small = jnp.concatenate(
        [jnp.stack([media_gain, media_bias, latent_gain, latent_bias, ffn_gain, ffn_bias]), time_embed]
    )
    small = lax.all_gather(small, "item", axis=1, tiled=True).astype(F32)
    g_media, b_media, g_latent, b_latent, g_ffn, b_ffn = (small[k] for k in range(6))
    time_rows = lax.dynamic_slice_in_dim(small[6:], place * local_frames, local_frames, 0)
    w_query, w_key, w_value, w_output, w_up, w_down = (
        lax.all_gather(w, "item", axis=0, tiled=True)
        for w in (query_weight, key_weight, value_weight, output_weight, up_weight, down_weight)
    )
    shifted = (
        media.astype(F32).reshape(items, local_frames, P_SIZE, width) + time_rows[None, :, None, :]
    ).reshape(media.shape)
    media_norm, media_hat, media_inv = norm_forward(shifted, g_media, b_media)
    latent_f = latents.astype(F32)
    latent_norm, latent_hat, latent_inv = norm_forward(latent_f, g_latent, b_latent)
    media_all = gather_rows(media_norm.astype(BF))
    latent_all = gather_rows(latent_norm.astype(BF))
    upstream = gather_rows(cotangent)
    media_count, latent_count = media_all.shape[1], latent_all.shape[1]
    joined = jnp.concatenate([media_all, latent_all], axis=1)
    key_count = joined.shape[1]
    local_heads = w_query.shape[1] // HEAD_DIM
    query = (scale * dot(latent_all, w_query, 2, 0)).astype(BF)
    keys = dot(joined, w_key, 2, 0).astype(BF)
    values = dot(joined, w_value, 2, 0).astype(BF)
    query_h = query.reshape(items, latent_count, local_heads, HEAD_DIM)
    key_h = keys.reshape(items, key_count, local_heads, HEAD_DIM)
    value_h = values.reshape(items, key_count, local_heads, HEAD_DIM)
    index = jnp.arange(key_count, dtype=jnp.int32)
    valid = (index[None, :] // P_SIZE < frame_counts[:, None]) | (index[None, :] >= media_count)
    valid = valid[:, None, None, :]

    def mix(spec, left, right):
        return jnp.einsum(spec, left, right, preferred_element_type=F32)

    scores = jnp.where(valid, mix("blhe,bnhe->bhln", query_h, key_h), -1e30)
    peak = jnp.max(scores, axis=-1, keepdims=True)
    expo = jnp.exp(scores - peak)
    weights = expo / jnp.sum(expo, axis=-1, keepdims=True)
    weights_low = weights.astype(BF)
    mixed = mix("bhln,bnhe->blhe", weights_low, value_h).reshape(items, latent_count, -1).astype(BF)
    middle = latent_f + scatter_rows(dot(mixed, w_output, 2, 1))
    ffn_norm, ffn_hat, ffn_inv = norm_forward(middle, g_ffn, b_ffn)
    ffn_all = gather_rows(ffn_norm.astype(BF))
    rows = items * latent_count
    ffn_rows = ffn_all.reshape(rows, width)
    up_rows = upstream.reshape(rows, width)
    pre = dot(ffn_rows, w_up, 1, 0)
    act, gelu_back = jax.vjp(jax.nn.gelu, pre)
    act = act.astype(BF)
    ffn_out = scatter_rows(dot(act, w_down, 1, 1).reshape(items, latent_count, width))
    output = (middle + ffn_out).astype(BF)
    grad_down = dot(up_rows, act, 0, 0)
    grad_pre = gelu_back(dot(up_rows, w_down, 1, 0))[0].astype(BF)
    grad_up = dot(ffn_rows, grad_pre, 0, 0)
    grad_ffn = scatter_rows(dot(grad_pre, w_up, 1, 1).reshape(items, latent_count, width))
    grad_mid, grad_fgain, grad_fbias = norm_backward(grad_ffn, ffn_hat, ffn_inv, g_ffn)
    grad_middle = cotangent.astype(F32) + grad_mid
    attended_grad = gather_rows(grad_middle.astype(BF)).reshape(rows, width)
    grad_output = dot(attended_grad, mixed.reshape(rows, -1), 0, 0)
    grad_mixed = dot(attended_grad, w_output, 1, 0).astype(BF)
    gm_h = grad_mixed.reshape(items, latent_count, local_heads, HEAD_DIM)
    grad_values = mix("bhln,blhe->bnhe", weights_low, gm_h).astype(BF).reshape(items * key_count, -1)
    grad_weights = mix("blhe,bnhe->bhln", gm_h, value_h)
    inner = jnp.sum(weights * grad_weights, axis=-1, keepdims=True)
    grad_scores = (weights * (grad_weights - inner)).astype(BF)
    grad_query = mix("bhln,bnhe->blhe", grad_scores, key_h).astype(BF).reshape(rows, -1)
    grad_keys = mix("bhln,blhe->bnhe", grad_scores, query_h).astype(BF).reshape(items * key_count, -1)
    joined_rows = joined.reshape(items * key_count, width)
    grad_wquery = scale * dot(latent_all.reshape(rows, width), grad_query, 0, 0)
    grad_wkey = dot(joined_rows, grad_keys, 0, 0)
    grad_wvalue = dot(joined_rows, grad_values, 0, 0)
    grad_joined = dot(grad_keys, w_key, 1, 1) + dot(grad_values, w_value, 1, 1)
    grad_joined = grad_joined.reshape(items, key_count, width)
    grad_latent_all = grad_joined[:, media_count:] + scale * dot(grad_query, w_query, 1, 1).reshape(
        items, latent_count, width
    )
    media_back = scatter_rows(grad_joined[:, :media_count])
    latent_back = scatter_rows(grad_latent_all)
    grad_media, grad_mgain, grad_mbias = norm_backward(media_back, media_hat, media_inv, g_media)
    grad_lat, grad_lgain, grad_lbias = norm_backward(latent_back, latent_hat, latent_inv, g_latent)
    time_local = jnp.sum(grad_media.reshape(items, local_frames, P_SIZE, width), axis=(0, 2))
    grad_time = lax.dynamic_update_slice_in_dim(
        jnp.zeros((frames, width), F32), time_local, place * local_frames, 0
    )
    smalls = jnp.concatenate(
        [jnp.stack([grad_mgain, grad_mbias, grad_lgain, grad_lbias, grad_fgain, grad_fbias]), grad_time]
    )
    smalls = lax.psum_scatter(smalls, ("item",), scatter_dimension=1, tiled=True)
    smalls = lax.psum(smalls, "head")
    return (
        output,
        grad_middle + grad_lat,
        grad_media,
        *(item_scatter(g) for g in (grad_wquery, grad_wkey, grad_wvalue, grad_output, grad_up, grad_down)),
        *(smalls[k] for k in range(6)),
        smalls[6:],
    )


MESH = pl.DeviceIdType.MESH
VMEM = pltpu.VMEM
ANY = pl.ANY
SPREAD = 4


class Place:
    def __init__(self, count, sems, chip_rows):
        self.count = count
        self.rows = chip_rows
        self.sems = sems
        self.used = 0
        self.sent = []
        i, h = lax.axis_index("item"), lax.axis_index("head")
        self.item, self.head = i, h
        self.y, self.core = h // 2, h % 2
        self.quarter = i % SPREAD
        self.group = i // SPREAD
        odd = i % 2
        self.spot = (1 - odd) * (i // 2) + odd * (count - 1 - i // 2)
        self.sibling = {"item": i, "head": 2 * self.y + 1 - self.core}
        self.across = {"item": i, "head": 2 * (1 - self.y) + self.core}
        self.opposite = {"item": i, "head": 2 * (1 - self.y) + 1 - self.core}
        self.chip = 2 * self.quarter + self.y

    def ring(self, spot):
        spot = (spot + self.count) % self.count
        back = spot // (self.count // 2)
        return (1 - back) * 2 * spot + back * (2 * (self.count - 1 - spot) + 1)

    def member(self, k):
        bits = [self.quarter // 2, self.quarter % 2, self.y]
        want = [k // 4, (k // 2) % 2, k % 2]
        a, b, y = (u + w - 2 * u * w for u, w in zip(bits, want))
        quarter = 2 * a + b
        device = {"item": self.group * SPREAD + quarter, "head": 2 * y + self.core}
        return 2 * quarter + y, device

    def chip_rows(self, core, chip):
        rows = self.rows
        return pl.ds(pl.multiple_of((core * 2 * SPREAD + chip) * rows, rows), rows)

    def other(self, k):
        return (self.item + k) % self.count

    def barrier(self):
        sem = pltpu.get_barrier_semaphore()
        peers = [{"item": self.other(k), "head": self.head} for k in range(1, self.count)]
        peers += [self.sibling, self.across, self.opposite]
        peers += [self.member(k)[1] for k in (3, 5, 7)]
        for peer in peers:
            pl.semaphore_signal(sem, inc=1, device_id=peer, device_id_type=MESH)
        pl.semaphore_wait(sem, len(peers))

    def send(self, src, dst, device):
        copy = pltpu.make_async_remote_copy(
            src_ref=src,
            dst_ref=dst,
            send_sem=self.sems.at[self.used],
            recv_sem=self.sems.at[self.used + 1],
            device_id=device,
            device_id_type=MESH,
        )
        self.used += 2
        copy.start()
        self.sent.append(copy)
        return copy

    def local(self, src, dst):
        copy = pltpu.make_async_copy(src, dst, self.sems.at[self.used])
        self.used += 1
        copy.start()
        return copy

    def settle(self, copy):
        copy.wait_send()
        self.sent = [other for other in self.sent if other is not copy]

    def drain(self):
        for copy in self.sent:
            copy.wait_send()


class Pump:
    def __init__(self, steps):
        self.steps = list(steps)
        self.at = 0

    def __call__(self, count=None):
        end = len(self.steps) if count is None else min(self.at + count, len(self.steps))
        while self.at < end:
            self.steps[self.at]()
            self.at += 1


class GatherPipe:
    def __init__(self, place, source, target, way):
        self.place, self.target, self.way = place, target, way
        self.device = {"item": place.ring(place.spot + way), "head": place.head}
        self.copy = place.send(source, target(place.item), self.device)

    def step(self, s):
        self.copy.wait_recv()
        if s < self.place.count - 1:
            part = self.target(self.place.ring(self.place.spot - self.way * s))
            self.copy = self.place.send(part, part, self.device)


class ScatterPipe:
    def __init__(self, place, part, slots, finish, way):
        self.place, self.part, self.slots, self.finish, self.way = place, part, slots, finish, way
        self.device = {"item": place.ring(place.spot + way), "head": place.head}
        self.copy = place.send(part(place.ring(place.spot - way)), slots.at[0], self.device)

    def step(self, s):
        self.copy.wait_recv()
        if s < self.place.count - 2:
            own = self.part(self.place.ring(self.place.spot - self.way * (s + 2)))
            self.slots[s] = (self.slots[s].astype(F32) + own[...].astype(F32)).astype(BF)
            self.copy = self.place.send(self.slots.at[s], self.slots.at[s + 1], self.device)
        else:
            self.finish(self.slots[s].astype(F32) + self.part(self.place.item)[...].astype(F32))


def weave(*pipes, steps):
    return [functools.partial(pipe.step, s) for s in steps for pipe in pipes]


class HeadGather:
    def __init__(self, place, ref):
        self.place, self.ref = place, ref
        own = ref.at[place.y, place.core]
        self.near = place.send(own, own, place.sibling)
        self.far = place.send(own, own, place.across)

    def forward(self):
        place = self.place
        self.far.wait_recv()
        block = self.ref.at[1 - place.y, place.core]
        self.passed = place.send(block, block, place.sibling)

    def finish(self):
        self.near.wait_recv()
        self.passed.wait_recv()

    def settle(self):
        for copy in (self.near, self.far, self.passed):
            self.place.settle(copy)


class HeadScatter:
    def __init__(self, place, part, near, far):
        self.place, self.part, self.near, self.far = place, part, near, far
        self.copies = [
            place.send(part.at[side, 1 - place.core], near[side], place.sibling) for side in range(2)
        ]

    def landed(self, side):
        first, second = self.near[0][...].astype(F32), self.near[1][...].astype(F32)
        return jnp.where(side == 0, first, second)

    def forward(self):
        place, part = self.place, self.part
        for copy in self.copies:
            copy.wait_recv()
        block = part.at[1 - place.y, place.core]
        block[...] = (block[...].astype(F32) + self.landed(1 - place.y)).astype(BF)
        self.copy = place.send(block, self.far, place.across)
        self.copies.append(self.copy)

    def finish(self):
        place = self.place
        own = self.part[place.y, place.core].astype(F32) + self.landed(place.y)
        self.copy.wait_recv()
        return own + self.far[...].astype(F32)

    def settle(self):
        for copy in self.copies:
            self.place.settle(copy)


class GroupGather:
    def __init__(self, place, ref):
        self.place, self.ref = place, ref
        self.copies = {}
        self.passed = []
        self.share(0)

    def block(self, k):
        return self.ref.at[self.place.chip_rows(self.place.core, self.place.member(k)[0])]

    def settle(self):
        for copy in self.passed + list(self.copies.values()):
            self.place.settle(copy)

    def share(self, k):
        self.passed.append(self.place.send(self.block(k), self.block(k), self.place.sibling))

    def push(self, k, *axes):
        for axis in axes:
            self.copies[axis, k] = self.place.send(self.block(k), self.block(k), self.place.member(axis)[1])

    def pull(self, axis, k):
        self.copies[axis, k].wait_recv()
        self.share(axis ^ k)

    def finish(self):
        for copy in self.passed:
            copy.wait_recv()


class GroupScatter:
    def __init__(self, place, part, near, far, order):
        self.place, self.part, self.near, self.far, self.order = place, part, near, far, order
        rows, lanes = near[0].shape
        theirs = pl.ds(pl.multiple_of((1 - place.core) * rows, rows), rows)
        self.passed = [
            place.send(part.at[theirs, pl.ds(k * lanes, lanes)], piece, place.sibling)
            for k, piece in enumerate(near)
        ]
        self.copies = {}
        self.arrived = {}

    def total(self, k):
        chip = self.place.member(k)[0]
        value = self.part[self.place.chip_rows(self.place.core, chip)].astype(F32)
        pieces = [piece[self.place.chip_rows(0, chip)].astype(F32) for piece in self.near]
        if pieces:
            value = value + (pieces[0] if len(pieces) == 1 else jnp.concatenate(pieces, axis=1))
        for axis, slot in self.arrived.get(k, ()):
            self.copies[axis, axis ^ k].wait_recv()
            value = value + self.far[slot].astype(F32)
        return value

    def push(self, axis, k, slot):
        chip, _ = self.place.member(k)
        block = self.part.at[self.place.chip_rows(self.place.core, chip)]
        block[...] = self.total(k).astype(BF)
        self.copies[axis, k] = self.place.send(block, self.far.at[slot], self.place.member(axis)[1])
        self.arrived.setdefault(axis ^ k, []).append((axis, slot))

    def first(self):
        a, b, c = self.order
        for copy in self.passed:
            copy.wait_recv()
        for slot, k in enumerate((a ^ b ^ c, a ^ b, a ^ c, a)):
            self.push(a, k, slot)

    def absorb(self):
        a, b, c = self.order
        for k in (b ^ c, b, c, 0):
            rows = self.place.chip_rows(self.place.core, self.place.member(k)[0])
            near = self.place.chip_rows(0, self.place.member(k)[0])
            pieces = [piece[near].astype(F32) for piece in self.near]
            self.part[rows] = (self.part[rows].astype(F32) + jnp.concatenate(pieces, axis=1)).astype(BF)
        self.near = []

    def second(self):
        a, b, c = self.order
        self.push(b, b ^ c, 4)
        self.push(b, b, 5)

    def third(self):
        a, b, c = self.order
        self.push(c, c, 6)

    def finish(self):
        return self.total(0)

    def settle(self):
        for copy in [*self.passed, *self.copies.values()]:
            self.place.settle(copy)


def head_masks(rows, columns):
    lane = lax.broadcasted_iota(jnp.int32, (rows, columns), 1)
    return [(lane >= at) & (lane < at + HEAD_DIM) for at in range(0, columns, HEAD_DIM)]


def stack_heads(block, masks):
    zero = jnp.zeros_like(block)
    return jnp.concatenate([jnp.where(mask, block, zero) for mask in masks], axis=0)


def fold_heads(block, masks):
    rows = masks[0].shape[0]
    total = 0.0
    for h, mask in enumerate(masks):
        total = total + jnp.where(mask, block[h * rows : (h + 1) * rows], 0.0)
    return total


def norm_parts(rows):
    mean = jnp.mean(rows, axis=-1, keepdims=True)
    centered = rows - mean
    inverse = lax.rsqrt(jnp.mean(centered * centered, axis=-1, keepdims=True) + EPS)
    return centered * inverse, inverse


def norm_back(upstream, rows, gain):
    normed, inverse = norm_parts(rows)
    scaled = upstream * gain
    first = jnp.mean(scaled, axis=-1, keepdims=True)
    second = jnp.mean(scaled * normed, axis=-1, keepdims=True)
    return (
        inverse * (scaled - first - normed * second),
        jnp.sum(upstream * normed, axis=0, keepdims=True),
        jnp.sum(upstream, axis=0, keepdims=True),
    )


def gelu_parts(x):
    root = 0.7978845608028654
    t = jnp.tanh(root * (x + 0.044715 * (x * x * x)))
    half = 0.5 * (1.0 + t)
    return x * half, half + 0.5 * x * (1.0 - t * t) * (root * (1.0 + 3 * 0.044715 * (x * x)))


def window(width, k):
    return (width * k) // 128 * 128


def layer_kernel(
    count,
    small_in, frames_ref, media_in, latents_in, cotangent_in, w_query, w_key, w_value, w_output, w_up, w_down,
    o_out, o_lgrad, o_media, o_query, o_key, o_value, o_output, o_up, o_down, o_small,
    media, latents, cotangent,
    joined, kv, query, weights, mixed, latent, wkv, wq, wo, up, down,
    tokens, upstream, pre, act, gpre, back, gup, gdown, middle, gmiddle, small, smalls, att, att_near, att_far,
    near, far, out_far, gmixed, gquery, gkv, slots, up_in, down_in, mstage, sums, sum_in, sum_head,
    sems,
):
    place = Place(count, sems, latents_in.shape[0] * latents_in.shape[1])
    loads = [
        place.local(media_in, media),
        place.local(latents_in, latents),
        place.local(cotangent_in, cotangent),
    ]
    place.barrier()
    items, local_media, width = media.shape
    local_latents = latents.shape[1]
    rows = local_media + local_latents
    keys_count = 4 * rows
    block_rows, columns = w_query.shape
    hidden = up.shape[2]
    part = block_rows // 2
    latent_count = 4 * local_latents
    all_latents = items * latent_count
    own_latents = items * local_latents
    group_rows = 4 * SPREAD * own_latents
    local_frames = local_media // P_SIZE
    scale = HEAD_DIM ** (-0.5)
    tile = 2 * block_rows
    item, y, core = place.item, place.y, place.core

    shift = block_rows * item % 128
    sum_head[0] = jnp.zeros_like(sum_head[0])
    sum_head[0, :, pl.ds(0, block_rows)] = small_in[...].astype(F32)
    smalls[item] = pltpu.roll(sum_head[0], shift, 1).astype(BF)
    small_copies = [
        place.send(smalls.at[item], smalls.at[item], {"item": place.other(k), "head": place.head})
        for k in range(1, count)
    ]
    for load in loads:
        load.wait()
    own = place.chip_rows(core, place.chip)
    upstream[own] = cotangent[...].reshape(own_latents, width)
    upstream_gather = GroupGather(place, upstream)
    upstream_gather.push(0, 1)

    def gather_pipes(source, slab, lanes):
        made = []
        for half, way in ((0, 1), (1, -1)):
            span = pl.ds(half * part, part)
            made.append(
                GatherPipe(place, source.at[span], lambda o, span=span: slab.at[o, span, lanes], way)
            )
        return made

    whole, second = pl.ds(0, columns), pl.ds(columns, columns)
    ring_pipes = (
        gather_pipes(w_key, wkv, whole)
        + gather_pipes(w_value, wkv, second)
        + gather_pipes(w_query, wq, whole)
        + gather_pipes(w_output, wo, whole)
    )
    ring = Pump(weave(*ring_pipes, steps=range(1, count)))
    each = len(ring_pipes)
    quarter = pl.ds(pl.multiple_of(place.quarter * hidden, 128), hidden)
    owns = [
        place.local(w_key, wkv.at[item, :, whole]),
        place.local(w_value, wkv.at[item, :, second]),
        place.local(w_query, wq.at[item]),
        place.local(w_output, wo.at[item]),
    ]
    own_hidden = [
        place.local(w_up.at[:, quarter], up.at[item]),
        place.local(w_down.at[:, quarter], down.at[item]),
    ]
    for copy in small_copies:
        copy.wait_recv()
    small[...] = jnp.zeros_like(small)
    for j in range(count):
        lanes = pl.ds(window(block_rows, j), smalls.shape[2])
        small[:, lanes] += smalls[j].astype(F32)
    time_rows = [small[pl.ds(6 + place.head * local_frames + f, 1), :] for f in range(local_frames)]

    gathers = []
    for b in range(items):
        for f in range(local_frames):
            span = pl.ds(f * P_SIZE, P_SIZE)
            normed, _ = norm_parts(media[b, span].astype(F32) + time_rows[f])
            joined[b, y, core, span] = (normed * small[0:1] + small[1:2]).astype(BF)
        normed, _ = norm_parts(latents[b].astype(F32))
        joined[b, y, core, pl.ds(local_media, local_latents)] = (
            normed * small[2:3] + small[3:4]
        ).astype(BF)
        gathers.append(HeadGather(place, joined.at[b]))

    def project(b):
        gathers[b].finish()
        kv[b] = dot(joined[b].reshape(keys_count, width), wkv[...].reshape(width, 2 * columns), 1, 0).astype(BF)
        for p in range(4):
            latent[p, pl.ds(b * local_latents, local_latents)] = joined[
                b, p // 2, p % 2, pl.ds(local_media, local_latents)
            ]

    ring(2 * each)
    gathers[0].forward()
    ring(2 * each)
    gathers[1].forward()
    ring(each)
    gathers[2].forward()
    ring()
    upstream_gather.push(0, 4, 2)

    def spread(source, slab, offsets, lanes_of=None):
        copies = []
        for k in offsets:
            to = place.other(k)
            if lanes_of is None:
                block = source.at[to]
            else:
                block = source.at[:, pl.ds(pl.multiple_of((to % SPREAD) * hidden, 128), hidden)]
            copies.append(place.send(block, slab.at[item], {"item": to, "head": place.head}))
        return copies

    straight, turned = (4, 2, 6), (3, 5, 1, 7)
    mixed_order = (4, 3, 5, 2, 6, 1, 7)
    up_copies = spread(w_up, up, mixed_order, hidden)
    gathers[3].forward()
    for copy in owns:
        copy.wait()
    for b in range(items):
        project(b)
    upstream_gather.pull(4, 0)
    upstream_gather.push(4, 2, 1)
    query[...] = (
        (scale * dot(latent[...].reshape(all_latents, width), wq[...].reshape(width, columns), 1, 0))
        .astype(BF)
        .reshape(query.shape)
    )
    masks = head_masks(latent_count, columns)
    index = lax.broadcasted_iota(jnp.int32, (1, keys_count), 1)
    local = index % rows
    frame = jnp.where(local < local_media, (index // rows) * local_frames + local // P_SIZE, -1)
    for b in range(items):
        mine = pl.ds(b * local_latents, local_latents)
        stacked = stack_heads(query[:, mine].reshape(latent_count, columns), masks)
        scores = dot(stacked, kv[b, :, :columns], 1, 1)
        shown = jnp.broadcast_to(frame, scores.shape) < frames_ref[b]
        scores = jnp.where(shown, scores, -1e30)
        expo = jnp.exp(scores - jnp.max(scores, axis=1, keepdims=True))
        weight = expo / jnp.sum(expo, axis=1, keepdims=True)
        weights[b] = weight
        result = fold_heads(dot(weight.astype(BF), kv[b, :, columns:], 1, 0), masks)
        mixed[:, mine] = result.astype(BF).reshape(4, local_latents, columns)
    att[...] = (
        dot(mixed[...].reshape(all_latents, columns), wo[...].reshape(width, columns), 1, 1)
        .astype(BF)
        .reshape(att.shape)
    )
    scatter = HeadScatter(place, att, [att_near.at[0], att_near.at[1]], att_far)
    scatter.forward()
    upstream_gather.pull(2, 0)
    upstream_gather.push(2, 1)
    middle[...] = latents[...].astype(F32).reshape(middle.shape) + scatter.finish()
    scatter.settle()
    normed, _ = norm_parts(middle[...])
    tokens[own] = (normed * small[4:5] + small[5:6]).astype(BF)
    token_gather = GroupGather(place, tokens)
    token_gather.push(0, 4, 2, 1)
    down_copies = spread(w_down, down, mixed_order, hidden)
    upstream_gather.pull(2, 4)
    upstream_gather.push(6, 1)
    token_gather.pull(4, 0)
    token_gather.push(4, 2, 1)
    token_gather.pull(2, 0)
    token_gather.push(2, 1)
    token_gather.pull(2, 4)
    token_gather.push(6, 1)
    for k in (0, 4, 2, 6):
        upstream_gather.pull(1, k)
    for k in (0, 4, 2, 6):
        token_gather.pull(1, k)
    token_gather.finish()

    for copy in own_hidden:
        copy.wait()
    for copy in up_copies:
        copy.wait_recv()
    blocks = 4
    tall = group_rows // blocks
    spans = [pl.ds(n * tall, tall) for n in range(blocks)]
    for span in spans:
        value, slope = gelu_parts(dot(tokens[span], up[...].reshape(width, hidden), 1, 0))
        act[span] = value.astype(BF)
        pre[span] = slope
    upstream_gather.finish()
    all_rows = pl.ds(0, group_rows)
    for t in range(width // tile):
        span = pl.ds(t * tile, tile)
        gdown[pl.ds(2 * t, 2)] = (
            dot(upstream[all_rows, span], act[...], 0, 0).astype(BF).reshape(2, block_rows, hidden)
        )
    down_sums = spread(gdown, down_in, straight)
    for copy in down_copies:
        copy.wait_recv()
    for n in range(blocks):
        if n == blocks // 2:
            back_scatter = GroupScatter(place, back, [near], far, (1, 2, 4))
        start = (blocks // 2 * (1 - core) + n) % blocks * tall
        span = pl.ds(pl.multiple_of(start, tall), tall)
        grad_act = dot(upstream[span], down[...].reshape(width, hidden), 1, 0)
        gpre[span] = (grad_act * pre[span]).astype(BF)
        back[span] = dot(gpre[span], up[...].reshape(width, hidden), 1, 1).astype(BF)
    back_scatter.first()
    for t in range(width // tile):
        span = pl.ds(t * tile, tile)
        gup[pl.ds(2 * t, 2)] = (
            dot(tokens[all_rows, span], gpre[...], 0, 0).astype(BF).reshape(2, block_rows, hidden)
        )
    up_sums = spread(gup, up_in, straight)
    down_own = place.local(gdown.at[item], down_in.at[item])
    up_own = place.local(gup.at[item], up_in.at[item])
    upstream_gather.settle()
    token_gather.settle()
    back_scatter.second()
    out = upstream
    for span in spans:
        out[span] = dot(act[span], down[...].reshape(width, hidden), 1, 1).astype(BF)
    back_scatter.third()
    lands = [gkv.at[pl.ds(k * near.shape[0], near.shape[0])] for k in range(2)]
    out_scatter = GroupScatter(place, out, lands, out_far, (1, 2, 4))
    down_sums += spread(gdown, down_in, turned)
    sums[...] = jnp.zeros_like(sums)
    grad_norm = back_scatter.finish()
    back_scatter.settle()

    dx, dg, db = norm_back(grad_norm, middle[...], small[4:5])
    sums[4:5] = dg
    sums[5:6] = db
    grad_middle = cotangent[...].astype(F32).reshape(middle.shape) + dx
    gmiddle[...] = grad_middle
    gatt = att
    gatt[y, core] = grad_middle.astype(BF)
    att_gather = HeadGather(place, gatt)
    out_scatter.first()
    out_scatter.absorb()
    up_sums += spread(gup, up_in, turned)
    att_gather.forward()
    att_gather.finish()
    go, gq = up, down
    gmixed[...] = (
        dot(gatt[...].reshape(all_latents, width), wo[...].reshape(width, columns), 1, 0)
        .astype(BF)
        .reshape(gmixed.shape)
    )
    for t in range(width // tile):
        span = pl.ds(t * tile, tile)
        go[pl.ds(2 * t, 2)] = (
            dot(gatt[:, :, :, span].reshape(all_latents, tile), mixed[...].reshape(all_latents, columns), 0, 0)
            .astype(BF)
            .reshape(2, block_rows, columns)
        )

    def scatter_pipes(first_slot, slab, lanes, result):
        made = []
        for half, way in ((0, 1), (1, -1)):
            span = pl.ds(half * part, part)

            def finish(value, span=span):
                result[span] = value

            def of_owner(o, half=half):
                if len(slab.shape) == 3:
                    return slab.at[o, pl.ds(half * part, part), lanes]
                return slab.at[pl.ds(pl.multiple_of(o * block_rows + half * part, part), part), lanes]

            made.append(
                ScatterPipe(
                    place,
                    of_owner,
                    slots.at[first_slot + half],
                    finish,
                    way,
                )
            )
        return made

    go_pipes = scatter_pipes(0, go, whole, o_output)

    for b in range(items):
        mine = pl.ds(b * local_latents, local_latents)
        q_stack = stack_heads(query[:, mine].reshape(latent_count, columns), masks)
        g_stack = stack_heads(gmixed[:, mine].reshape(latent_count, columns), masks)
        weight = weights[b]
        grad_weight = dot(g_stack, kv[b, :, columns:], 1, 1)
        inner = jnp.sum(weight * grad_weight, axis=1, keepdims=True)
        grad_score = (weight * (grad_weight - inner)).astype(BF)
        gq_rows = fold_heads(dot(grad_score, kv[b, :, :columns], 1, 0), masks).astype(BF)
        gquery[:, mine] = gq_rows.reshape(4, local_latents, columns)
        kv[b, :, :columns] = dot(grad_score, q_stack, 0, 0).astype(BF)
        kv[b, :, columns:] = dot(weight.astype(BF), g_stack, 0, 0).astype(BF)
    for t in range(width // tile):
        span = pl.ds(t * tile, tile)
        gkv[span] = dot(
            joined[:, :, :, :, span].reshape(items * keys_count, tile),
            kv[...].reshape(items * keys_count, 2 * columns),
            0,
            0,
        ).astype(BF)
    kv_pipes = scatter_pipes(2, gkv, whole, o_key) + scatter_pipes(4, gkv, second, o_value)
    for t in range(width // tile):
        span = pl.ds(t * tile, tile)
        gq[pl.ds(2 * t, 2)] = (
            (scale * dot(latent[:, :, span].reshape(all_latents, tile), gquery[...].reshape(all_latents, columns), 0, 0))
            .astype(BF)
            .reshape(2, block_rows, columns)
        )
    q_pipes = scatter_pipes(6, gq, whole, o_query)
    steps = weave(*go_pipes, steps=[0])
    for s in range(count - 1):
        steps += weave(*kv_pipes, *q_pipes, steps=[s])
        if s + 1 < count - 1:
            steps += weave(*go_pipes, steps=[s + 1])
    ring = Pump(steps)
    scatters = []
    for gather in gathers:
        gather.settle()
    for b in range(items):
        mine = pl.ds(b * local_latents, local_latents)
        gq_rows = gquery[:, mine].reshape(latent_count, columns)
        for t in range(width // tile):
            span = pl.ds(t * tile, tile)
            owners = pl.ds(2 * t, 2)
            value = dot(kv[b], wkv[owners].reshape(tile, 2 * columns), 1, 1)
            extra = scale * dot(gq_rows, wq[owners].reshape(tile, columns), 1, 1)
            for p in range(4):
                at = p * rows
                joined[b, p // 2, p % 2, pl.ds(0, local_media), span] = value[at : at + local_media].astype(BF)
                joined[b, p // 2, p % 2, pl.ds(local_media, local_latents), span] = (
                    value[at + local_media : at + rows] + extra[p * local_latents : (p + 1) * local_latents]
                ).astype(BF)
        lands = [tokens.at[pl.ds((2 * b + side) * rows, rows)] for side in range(2)]
        scatters.append(HeadScatter(place, joined.at[b], lands, back.at[pl.ds(b * rows, rows)]))
        if b > 0:
            scatters[b - 1].forward()
        if b == 1:
            out_scatter.second()
        if b == 2:
            ring(each)
    scatters[-1].forward()
    out_scatter.third()
    ring(each)

    def combine(copies, own, slab, result):
        own.wait()
        for copy in copies:
            copy.wait_recv()
        stores = []
        for k in range(SPREAD):
            grad = slab[k].astype(F32)
            for group in range(1, count // SPREAD):
                grad = grad + slab[group * SPREAD + k].astype(F32)
            span = pl.ds(k * block_rows, block_rows)
            pre[span] = grad
            stores.append(place.local(pre.at[span], result.at[:, pl.ds(k * hidden, hidden)]))
        return stores

    combined = combine(up_sums, up_own, up_in, o_up)
    for b in range(items):
        grad = scatters[b].finish()
        if b > 0:
            store.wait()
        for f in range(local_frames):
            span = slice(f * P_SIZE, (f + 1) * P_SIZE)
            dx, dg, db = norm_back(grad[span], media[b, span].astype(F32) + time_rows[f], small[0:1])
            mstage[span] = dx
            sums[0:1] += dg
            sums[1:2] += db
            sums[pl.ds(6 + place.head * local_frames + f, 1), :] += jnp.sum(dx, axis=0, keepdims=True)
        store = place.local(mstage, o_media.at[b])
        dx, dg, db = norm_back(grad[local_media:], latents[b].astype(F32), small[2:3])
        sums[2:3] += dg
        sums[3:4] += db
        o_lgrad[b] = gmiddle[pl.ds(b * local_latents, local_latents)] + dx
        if b == 0:
            for copy in combined:
                copy.wait()
            combined = combine(down_sums, down_own, down_in, o_down)
        ring((each, each, 2 * each, 0)[b])

    lanes = sum_in.shape[2]
    sum_copies = []
    for k in range(1, count):
        to = place.other(k)
        at = pl.multiple_of(window(block_rows, to), 128)
        sum_copies.append(
            place.send(sums.at[:, pl.ds(at, lanes)], sum_in.at[item], {"item": to, "head": place.head})
        )
    sum_in[item] = sums[:, pl.ds(pl.multiple_of(window(block_rows, item), 128), lanes)]
    o_out[...] = (middle[...] + out_scatter.finish()).astype(BF).reshape(o_out.shape)
    for copy in sum_copies:
        copy.wait_recv()
    value = jnp.sum(sum_in[...], axis=0)
    sum_head[0] = value
    head_copies = [
        place.send(sum_head.at[0], sum_head.at[k], device)
        for k, device in ((1, place.sibling), (2, place.across), (3, place.opposite))
    ]
    ring()
    for copy in head_copies:
        copy.wait_recv()
    total = jnp.sum(sum_head[...], axis=0)
    o_small[...] = pltpu.roll(total, (lanes - shift) % lanes, 1)
    place.drain()
    store.wait()
    for copy in combined:
        copy.wait()
    assert place.used <= sems.shape[0], place.used


def hand_over(*refs):
    third = (len(refs) - 1) // 3
    sources, targets, stages, sems = refs[:third], refs[third : 2 * third], refs[2 * third : -1], refs[-1]
    loads = [pltpu.make_async_copy(a, b, sems.at[0, k]) for k, (a, b) in enumerate(zip(sources, stages))]
    stores = [pltpu.make_async_copy(a, b, sems.at[1, k]) for k, (a, b) in enumerate(zip(stages, targets))]
    for copy in loads:
        copy.start()
    for load, store in zip(loads, stores):
        load.wait()
        store.start()
    for copy in stores:
        copy.wait()


def kernel_step(
    count, media, latents, cotangent, frame_counts,
    query_weight, key_weight, value_weight, output_weight, up_weight, down_weight,
    media_gain, media_bias, latent_gain, latent_bias, ffn_gain, ffn_bias, time_embed,
):
    items, local_media, width = media.shape
    local_latents = latents.shape[1]
    frames = time_embed.shape[0]
    block_rows, columns = query_weight.shape
    hidden = up_weight.shape[1] // SPREAD
    rows = local_media + local_latents
    keys_count = 4 * rows
    own_latents = items * local_latents
    stacked = columns // HEAD_DIM * 4 * local_latents
    group = 2 * SPREAD
    row = lax.broadcasted_iota(jnp.int32, (16, block_rows), 0)
    small = jnp.zeros((16, block_rows), BF)
    vectors = (media_gain, media_bias, latent_gain, latent_bias, ffn_gain, ffn_bias)
    for k, vector in enumerate(vectors):
        small = jnp.where(row == k, vector[None, :], small)
    for f in range(frames):
        small = jnp.where(row == len(vectors) + f, time_embed[f : f + 1], small)

    def hbm(*shape, kind=BF):
        return jax.ShapeDtypeStruct(shape, kind)

    def buf(*shape, kind=BF):
        return pltpu.VMEM(shape, kind)

    vmem, anywhere = pl.BlockSpec(memory_space=pltpu.VMEM), pl.BlockSpec(memory_space=pl.ANY)
    all_rows = 2 * group * own_latents
    sum_rows = items * 2 * rows
    slab = (count, block_rows, hidden)
    results = pl.pallas_call(
        functools.partial(layer_kernel, count),
        out_shape=[
            hbm(*latents.shape),
            hbm(*latents.shape, kind=F32),
            hbm(*media.shape, kind=F32),
        ]
        + [hbm(block_rows, columns, kind=F32)] * 4
        + [hbm(block_rows, SPREAD * hidden, kind=F32)] * 2
        + [hbm(16, 256, kind=F32)],
        in_specs=[vmem, pl.BlockSpec(memory_space=pltpu.SMEM)] + [anywhere] * 9,
        out_specs=[vmem, vmem, anywhere] + [vmem] * 4 + [anywhere] * 2 + [vmem],
        scratch_shapes=[
            buf(*media.shape),
            buf(*latents.shape),
            buf(*latents.shape),
            buf(items, 2, 2, rows, width),
            buf(items, keys_count, 2 * columns),
            buf(4, own_latents, columns),
            buf(items, stacked, keys_count, kind=F32),
            buf(4, own_latents, columns),
            buf(4, own_latents, width),
            buf(count, block_rows, 2 * columns),
            buf(count, block_rows, columns),
            buf(count, block_rows, columns),
            buf(*slab),
            buf(*slab),
            buf(max(all_rows, sum_rows), width),
            buf(all_rows, width),
            buf(all_rows, hidden, kind=F32),
            buf(all_rows, hidden),
            buf(all_rows, hidden),
            buf(max(all_rows, items * rows), width),
            buf(*slab),
            buf(*slab),
            buf(own_latents, width, kind=F32),
            buf(own_latents, width, kind=F32),
            buf(16, width, kind=F32),
            buf(count, 16, 256),
            buf(2, 2, own_latents, width),
            buf(2, own_latents, width),
            buf(own_latents, width),
            buf(group * own_latents, width),
            buf(group - 1, own_latents, width),
            buf(group - 1, own_latents, width),
            buf(4, own_latents, columns),
            buf(4, own_latents, columns),
            buf(width, 2 * columns),
            buf(8, count - 1, block_rows // 2, columns),
            buf(*slab),
            buf(*slab),
            buf(local_media, width, kind=F32),
            buf(16, width, kind=F32),
            buf(count, 16, 256, kind=F32),
            buf(4, 16, 256, kind=F32),
            pltpu.SemaphoreType.DMA((512,)),
        ],
        compiler_params=pltpu.CompilerParams(
            collective_id=0, has_side_effects=True, vmem_limit_bytes=62 * 2**20
        ),
        name="layer",
    )(
        small, frame_counts, media, latents, cotangent, query_weight, key_weight, value_weight,
        output_weight, up_weight, down_weight,
    )
    shapes = [jax.ShapeDtypeStruct(r.shape, r.dtype) for r in results]
    results = pl.pallas_call(
        hand_over,
        out_shape=shapes,
        in_specs=[anywhere] * len(shapes),
        out_specs=[anywhere] * len(shapes),
        scratch_shapes=[pltpu.VMEM(s.shape, s.dtype) for s in shapes]
        + [pltpu.SemaphoreType.DMA((2, len(shapes)))],
        compiler_params=pltpu.CompilerParams(vmem_limit_bytes=60 * 2**20),
        name="hand_over",
    )(*results)
    sums = results[9]
    return (
        *results[:9],
        *(sums[k, :block_rows] for k in range(6)),
        sums[6 : 6 + frames, :block_rows],
    )


def fits(mesh, media, query_weight, up_weight):
    count, heads = mesh.shape["item"], mesh.shape["head"]
    width, columns = query_weight.shape[0], query_weight.shape[1] // heads
    hidden = up_weight.shape[1] // heads
    block_rows = width // count
    return (
        heads == 4
        and count == 2 * SPREAD
        and block_rows % 64 == 0
        and columns % 128 == 0
        and hidden % (128 * SPREAD) == 0
    )


def solution(mesh):
    rows = P("item", "head", None)
    block = P("item", "head")
    vector = P("item")
    table = P(None, "item")

    def run(*arrays):
        count = mesh.shape["item"]
        step = plain_step
        if fits(mesh, arrays[0], arrays[4], arrays[8]):
            step = functools.partial(kernel_step, count)
        return jax.shard_map(
            step,
            mesh=mesh,
            in_specs=(rows,) * 3 + (vector,) + (block,) * 6 + (vector,) * 6 + (table,),
            out_specs=(rows,) * 3 + (block,) * 6 + (vector,) * 6 + (table,),
            check_vma=False,
        )(*arrays)

    return run
```

```python
import functools
import math

import jax
import jax.numpy as jnp
from jax import lax
from jax.experimental import pallas as pl
from jax.experimental.pallas import tpu as pltpu
from jax.sharding import PartitionSpec as P

HEAD_DIM = 96
P_SIZE = 64
EPS = 1e-05
BF = jnp.bfloat16
F32 = jnp.float32


def norm_forward(rows, gain, bias):
    mean = jnp.mean(rows, axis=-1, keepdims=True)
    centered = rows - mean
    inverse = lax.rsqrt(jnp.mean(centered * centered, axis=-1, keepdims=True) + EPS)
    normed = centered * inverse
    return normed * gain + bias, normed, inverse


def norm_backward(upstream, normed, inverse, gain):
    scaled = upstream * gain
    first = jnp.mean(scaled, axis=-1, keepdims=True)
    second = jnp.mean(scaled * normed, axis=-1, keepdims=True)
    axes = tuple(range(upstream.ndim - 1))
    return (
        inverse * (scaled - first - normed * second),
        jnp.sum(upstream * normed, axis=axes),
        jnp.sum(upstream, axis=axes),
    )


def dot(left, right, a, b):
    return lax.dot_general(left, right, (((a,), (b,)), ((), ())), preferred_element_type=F32)


def gather_rows(rows):
    return lax.all_gather(rows, "head", axis=1, tiled=True)


def scatter_rows(rows):
    return lax.psum_scatter(rows.astype(BF), "head", scatter_dimension=1, tiled=True).astype(F32)


def item_scatter(grad):
    return lax.psum_scatter(grad.astype(BF), "item", scatter_dimension=0, tiled=True).astype(F32)


def plain_step(
    media, latents, cotangent, frame_counts,
    query_weight, key_weight, value_weight, output_weight, up_weight, down_weight,
    media_gain, media_bias, latent_gain, latent_bias, ffn_gain, ffn_bias, time_embed,
):
    items, local_media, width = media.shape
    frames = time_embed.shape[0]
    local_frames = local_media // P_SIZE
    place = lax.axis_index("head")
    scale = HEAD_DIM ** (-0.5)
    small = jnp.concatenate(
        [jnp.stack([media_gain, media_bias, latent_gain, latent_bias, ffn_gain, ffn_bias]), time_embed]
    )
    small = lax.all_gather(small, "item", axis=1, tiled=True).astype(F32)
    g_media, b_media, g_latent, b_latent, g_ffn, b_ffn = (small[k] for k in range(6))
    time_rows = lax.dynamic_slice_in_dim(small[6:], place * local_frames, local_frames, 0)
    w_query, w_key, w_value, w_output, w_up, w_down = (
        lax.all_gather(w, "item", axis=0, tiled=True)
        for w in (query_weight, key_weight, value_weight, output_weight, up_weight, down_weight)
    )
    shifted = (
        media.astype(F32).reshape(items, local_frames, P_SIZE, width) + time_rows[None, :, None, :]
    ).reshape(media.shape)
    media_norm, media_hat, media_inv = norm_forward(shifted, g_media, b_media)
    latent_f = latents.astype(F32)
    latent_norm, latent_hat, latent_inv = norm_forward(latent_f, g_latent, b_latent)
    media_all = gather_rows(media_norm.astype(BF))
    latent_all = gather_rows(latent_norm.astype(BF))
    upstream = gather_rows(cotangent)
    media_count, latent_count = media_all.shape[1], latent_all.shape[1]
    joined = jnp.concatenate([media_all, latent_all], axis=1)
    key_count = joined.shape[1]
    local_heads = w_query.shape[1] // HEAD_DIM
    query = (scale * dot(latent_all, w_query, 2, 0)).astype(BF)
    keys = dot(joined, w_key, 2, 0).astype(BF)
    values = dot(joined, w_value, 2, 0).astype(BF)
    query_h = query.reshape(items, latent_count, local_heads, HEAD_DIM)
    key_h = keys.reshape(items, key_count, local_heads, HEAD_DIM)
    value_h = values.reshape(items, key_count, local_heads, HEAD_DIM)
    index = jnp.arange(key_count, dtype=jnp.int32)
    valid = (index[None, :] // P_SIZE < frame_counts[:, None]) | (index[None, :] >= media_count)
    valid = valid[:, None, None, :]

    def mix(spec, left, right):
        return jnp.einsum(spec, left, right, preferred_element_type=F32)

    scores = jnp.where(valid, mix("blhe,bnhe->bhln", query_h, key_h), -1e30)
    peak = jnp.max(scores, axis=-1, keepdims=True)
    expo = jnp.exp(scores - peak)
    weights = expo / jnp.sum(expo, axis=-1, keepdims=True)
    weights_low = weights.astype(BF)
    mixed = mix("bhln,bnhe->blhe", weights_low, value_h).reshape(items, latent_count, -1).astype(BF)
    middle = latent_f + scatter_rows(dot(mixed, w_output, 2, 1))
    ffn_norm, ffn_hat, ffn_inv = norm_forward(middle, g_ffn, b_ffn)
    ffn_all = gather_rows(ffn_norm.astype(BF))
    rows = items * latent_count
    ffn_rows = ffn_all.reshape(rows, width)
    up_rows = upstream.reshape(rows, width)
    pre = dot(ffn_rows, w_up, 1, 0)
    act, gelu_back = jax.vjp(jax.nn.gelu, pre)
    act = act.astype(BF)
    ffn_out = scatter_rows(dot(act, w_down, 1, 1).reshape(items, latent_count, width))
    output = (middle + ffn_out).astype(BF)
    grad_down = dot(up_rows, act, 0, 0)
    grad_pre = gelu_back(dot(up_rows, w_down, 1, 0))[0].astype(BF)
    grad_up = dot(ffn_rows, grad_pre, 0, 0)
    grad_ffn = scatter_rows(dot(grad_pre, w_up, 1, 1).reshape(items, latent_count, width))
    grad_mid, grad_fgain, grad_fbias = norm_backward(grad_ffn, ffn_hat, ffn_inv, g_ffn)
    grad_middle = cotangent.astype(F32) + grad_mid
    attended_grad = gather_rows(grad_middle.astype(BF)).reshape(rows, width)
    grad_output = dot(attended_grad, mixed.reshape(rows, -1), 0, 0)
    grad_mixed = dot(attended_grad, w_output, 1, 0).astype(BF)
    gm_h = grad_mixed.reshape(items, latent_count, local_heads, HEAD_DIM)
    grad_values = mix("bhln,blhe->bnhe", weights_low, gm_h).astype(BF).reshape(items * key_count, -1)
    grad_weights = mix("blhe,bnhe->bhln", gm_h, value_h)
    inner = jnp.sum(weights * grad_weights, axis=-1, keepdims=True)
    grad_scores = (weights * (grad_weights - inner)).astype(BF)
    grad_query = mix("bhln,bnhe->blhe", grad_scores, key_h).astype(BF).reshape(rows, -1)
    grad_keys = mix("bhln,blhe->bnhe", grad_scores, query_h).astype(BF).reshape(items * key_count, -1)
    joined_rows = joined.reshape(items * key_count, width)
    grad_wquery = scale * dot(latent_all.reshape(rows, width), grad_query, 0, 0)
    grad_wkey = dot(joined_rows, grad_keys, 0, 0)
    grad_wvalue = dot(joined_rows, grad_values, 0, 0)
    grad_joined = dot(grad_keys, w_key, 1, 1) + dot(grad_values, w_value, 1, 1)
    grad_joined = grad_joined.reshape(items, key_count, width)
    grad_latent_all = grad_joined[:, media_count:] + scale * dot(grad_query, w_query, 1, 1).reshape(
        items, latent_count, width
    )
    media_back = scatter_rows(grad_joined[:, :media_count])
    latent_back = scatter_rows(grad_latent_all)
    grad_media, grad_mgain, grad_mbias = norm_backward(media_back, media_hat, media_inv, g_media)
    grad_lat, grad_lgain, grad_lbias = norm_backward(latent_back, latent_hat, latent_inv, g_latent)
    time_local = jnp.sum(grad_media.reshape(items, local_frames, P_SIZE, width), axis=(0, 2))
    grad_time = lax.dynamic_update_slice_in_dim(
        jnp.zeros((frames, width), F32), time_local, place * local_frames, 0
    )
    smalls = jnp.concatenate(
        [jnp.stack([grad_mgain, grad_mbias, grad_lgain, grad_lbias, grad_fgain, grad_fbias]), grad_time]
    )
    smalls = lax.psum_scatter(smalls, ("item",), scatter_dimension=1, tiled=True)
    smalls = lax.psum(smalls, "head")
    return (
        output,
        grad_middle + grad_lat,
        grad_media,
        *(item_scatter(g) for g in (grad_wquery, grad_wkey, grad_wvalue, grad_output, grad_up, grad_down)),
        *(smalls[k] for k in range(6)),
        smalls[6:],
    )


MESH = pl.DeviceIdType.MESH
VMEM = pltpu.VMEM
ANY = pl.ANY
SPREAD = 4


class Place:
    def __init__(self, count, sems, chip_rows):
        self.count = count
        self.rows = chip_rows
        self.sems = sems
        self.used = 0
        self.sent = []
        i, h = lax.axis_index("item"), lax.axis_index("head")
        self.item, self.head = i, h
        self.y, self.core = h // 2, h % 2
        self.quarter = i % SPREAD
        self.group = i // SPREAD
        odd = i % 2
        self.spot = (1 - odd) * (i // 2) + odd * (count - 1 - i // 2)
        self.sibling = {"item": i, "head": 2 * self.y + 1 - self.core}
        self.across = {"item": i, "head": 2 * (1 - self.y) + self.core}
        self.opposite = {"item": i, "head": 2 * (1 - self.y) + 1 - self.core}
        self.chip = 2 * self.quarter + self.y

    def ring(self, spot):
        spot = (spot + self.count) % self.count
        back = spot // (self.count // 2)
        return (1 - back) * 2 * spot + back * (2 * (self.count - 1 - spot) + 1)

    def member(self, k):
        bits = [self.quarter // 2, self.quarter % 2, self.y]
        want = [k // 4, (k // 2) % 2, k % 2]
        a, b, y = (u + w - 2 * u * w for u, w in zip(bits, want))
        quarter = 2 * a + b
        device = {"item": self.group * SPREAD + quarter, "head": 2 * y + self.core}
        return 2 * quarter + y, device

    def chip_rows(self, core, chip):
        rows = self.rows
        return pl.ds(pl.multiple_of((core * 2 * SPREAD + chip) * rows, rows), rows)

    def other(self, k):
        return (self.item + k) % self.count

    def barrier(self):
        sem = pltpu.get_barrier_semaphore()
        peers = [{"item": self.other(k), "head": self.head} for k in range(1, self.count)]
        peers += [self.sibling, self.across, self.opposite]
        peers += [self.member(k)[1] for k in (3, 5, 7)]
        for peer in peers:
            pl.semaphore_signal(sem, inc=1, device_id=peer, device_id_type=MESH)
        pl.semaphore_wait(sem, len(peers))

    def send(self, src, dst, device):
        copy = pltpu.make_async_remote_copy(
            src_ref=src,
            dst_ref=dst,
            send_sem=self.sems.at[self.used],
            recv_sem=self.sems.at[self.used + 1],
            device_id=device,
            device_id_type=MESH,
        )
        self.used += 2
        copy.start()
        self.sent.append(copy)
        return copy

    def local(self, src, dst):
        copy = pltpu.make_async_copy(src, dst, self.sems.at[self.used])
        self.used += 1
        copy.start()
        return copy

    def settle(self, copy):
        copy.wait_send()
        self.sent = [other for other in self.sent if other is not copy]

    def drain(self):
        for copy in self.sent:
            copy.wait_send()


class Pump:
    def __init__(self, steps):
        self.steps = list(steps)
        self.at = 0

    def __call__(self, count=None):
        end = len(self.steps) if count is None else min(self.at + count, len(self.steps))
        while self.at < end:
            self.steps[self.at]()
            self.at += 1


class GatherPipe:
    def __init__(self, place, source, target, way):
        self.place, self.target, self.way = place, target, way
        self.device = {"item": place.ring(place.spot + way), "head": place.head}
        self.copy = place.send(source, target(place.item), self.device)

    def step(self, s):
        self.copy.wait_recv()
        if s < self.place.count - 1:
            part = self.target(self.place.ring(self.place.spot - self.way * s))
            self.copy = self.place.send(part, part, self.device)


class ScatterPipe:
    def __init__(self, place, part, slots, finish, way):
        self.place, self.part, self.slots, self.finish, self.way = place, part, slots, finish, way
        self.device = {"item": place.ring(place.spot + way), "head": place.head}
        self.copy = place.send(part(place.ring(place.spot - way)), slots.at[0], self.device)

    def step(self, s):
        self.copy.wait_recv()
        if s < self.place.count - 2:
            own = self.part(self.place.ring(self.place.spot - self.way * (s + 2)))
            self.slots[s] = (self.slots[s].astype(F32) + own[...].astype(F32)).astype(BF)
            self.copy = self.place.send(self.slots.at[s], self.slots.at[s + 1], self.device)
        else:
            self.finish(self.slots[s].astype(F32) + self.part(self.place.item)[...].astype(F32))


def weave(*pipes, steps):
    return [functools.partial(pipe.step, s) for s in steps for pipe in pipes]


class HeadGather:
    def __init__(self, place, ref):
        self.place, self.ref = place, ref
        own = ref.at[place.y, place.core]
        self.near = place.send(own, own, place.sibling)
        self.far = place.send(own, own, place.across)

    def forward(self):
        place = self.place
        self.far.wait_recv()
        block = self.ref.at[1 - place.y, place.core]
        self.passed = place.send(block, block, place.sibling)

    def finish(self):
        self.near.wait_recv()
        self.passed.wait_recv()

    def settle(self):
        for copy in (self.near, self.far, self.passed):
            self.place.settle(copy)


class HeadScatter:
    def __init__(self, place, part, near, far):
        self.place, self.part, self.near, self.far = place, part, near, far
        self.copies = [
            place.send(part.at[side, 1 - place.core], near[side], place.sibling) for side in range(2)
        ]

    def landed(self, side):
        first, second = self.near[0][...].astype(F32), self.near[1][...].astype(F32)
        return jnp.where(side == 0, first, second)

    def forward(self):
        place, part = self.place, self.part
        for copy in self.copies:
            copy.wait_recv()
        block = part.at[1 - place.y, place.core]
        block[...] = (block[...].astype(F32) + self.landed(1 - place.y)).astype(BF)
        self.copy = place.send(block, self.far, place.across)
        self.copies.append(self.copy)

    def finish(self):
        place = self.place
        own = self.part[place.y, place.core].astype(F32) + self.landed(place.y)
        self.copy.wait_recv()
        return own + self.far[...].astype(F32)

    def settle(self):
        for copy in self.copies:
            self.place.settle(copy)


class GroupGather:
    def __init__(self, place, ref):
        self.place, self.ref = place, ref
        self.copies = {}
        self.passed = []
        self.share(0)

    def block(self, k):
        return self.ref.at[self.place.chip_rows(self.place.core, self.place.member(k)[0])]

    def settle(self):
        for copy in self.passed + list(self.copies.values()):
            self.place.settle(copy)

    def share(self, k):
        self.passed.append(self.place.send(self.block(k), self.block(k), self.place.sibling))

    def push(self, k, *axes):
        for axis in axes:
            self.copies[axis, k] = self.place.send(self.block(k), self.block(k), self.place.member(axis)[1])

    def pull(self, axis, k):
        self.copies[axis, k].wait_recv()
        self.share(axis ^ k)

    def finish(self):
        for copy in self.passed:
            copy.wait_recv()


class GroupScatter:
    def __init__(self, place, part, near, far, order):
        self.place, self.part, self.near, self.far, self.order = place, part, near, far, order
        rows, lanes = near[0].shape
        theirs = pl.ds(pl.multiple_of((1 - place.core) * rows, rows), rows)
        self.passed = [
            place.send(part.at[theirs, pl.ds(k * lanes, lanes)], piece, place.sibling)
            for k, piece in enumerate(near)
        ]
        self.copies = {}
        self.arrived = {}

    def total(self, k):
        chip = self.place.member(k)[0]
        value = self.part[self.place.chip_rows(self.place.core, chip)].astype(F32)
        pieces = [piece[self.place.chip_rows(0, chip)].astype(F32) for piece in self.near]
        if pieces:
            value = value + (pieces[0] if len(pieces) == 1 else jnp.concatenate(pieces, axis=1))
        for axis, slot in self.arrived.get(k, ()):
            self.copies[axis, axis ^ k].wait_recv()
            value = value + self.far[slot].astype(F32)
        return value

    def push(self, axis, k, slot):
        chip, _ = self.place.member(k)
        block = self.part.at[self.place.chip_rows(self.place.core, chip)]
        block[...] = self.total(k).astype(BF)
        self.copies[axis, k] = self.place.send(block, self.far.at[slot], self.place.member(axis)[1])
        self.arrived.setdefault(axis ^ k, []).append((axis, slot))

    def first(self):
        a, b, c = self.order
        for copy in self.passed:
            copy.wait_recv()
        for slot, k in enumerate((a ^ b ^ c, a ^ b, a ^ c, a)):
            self.push(a, k, slot)

    def absorb(self):
        a, b, c = self.order
        for k in (b ^ c, b, c, 0):
            rows = self.place.chip_rows(self.place.core, self.place.member(k)[0])
            near = self.place.chip_rows(0, self.place.member(k)[0])
            pieces = [piece[near].astype(F32) for piece in self.near]
            self.part[rows] = (self.part[rows].astype(F32) + jnp.concatenate(pieces, axis=1)).astype(BF)
        self.near = []

    def second(self):
        a, b, c = self.order
        self.push(b, b ^ c, 4)
        self.push(b, b, 5)

    def third(self):
        a, b, c = self.order
        self.push(c, c, 6)

    def finish(self):
        return self.total(0)

    def settle(self):
        for copy in [*self.passed, *self.copies.values()]:
            self.place.settle(copy)


def head_masks(rows, columns):
    lane = lax.broadcasted_iota(jnp.int32, (rows, columns), 1)
    return [(lane >= at) & (lane < at + HEAD_DIM) for at in range(0, columns, HEAD_DIM)]


def stack_heads(block, masks):
    zero = jnp.zeros_like(block)
    return jnp.concatenate([jnp.where(mask, block, zero) for mask in masks], axis=0)


def fold_heads(block, masks):
    rows = masks[0].shape[0]
    total = 0.0
    for h, mask in enumerate(masks):
        total = total + jnp.where(mask, block[h * rows : (h + 1) * rows], 0.0)
    return total


def norm_parts(rows):
    mean = jnp.mean(rows, axis=-1, keepdims=True)
    centered = rows - mean
    inverse = lax.rsqrt(jnp.mean(centered * centered, axis=-1, keepdims=True) + EPS)
    return centered * inverse, inverse


def norm_back(upstream, rows, gain):
    normed, inverse = norm_parts(rows)
    scaled = upstream * gain
    first = jnp.mean(scaled, axis=-1, keepdims=True)
    second = jnp.mean(scaled * normed, axis=-1, keepdims=True)
    return (
        inverse * (scaled - first - normed * second),
        jnp.sum(upstream * normed, axis=0, keepdims=True),
        jnp.sum(upstream, axis=0, keepdims=True),
    )


def gelu_parts(x):
    root = 0.7978845608028654
    t = jnp.tanh(root * (x + 0.044715 * (x * x * x)))
    half = 0.5 * (1.0 + t)
    return x * half, half + 0.5 * x * (1.0 - t * t) * (root * (1.0 + 3 * 0.044715 * (x * x)))


def window(width, k):
    return (width * k) // 128 * 128


def layer_kernel(
    count,
    small_in, frames_ref, media_in, latents_in, cotangent_in, w_query, w_key, w_value, w_output, w_up, w_down,
    o_out, o_lgrad, o_media, o_query, o_key, o_value, o_output, o_up, o_down, o_small,
    media, latents, cotangent,
    joined, kv, query, weights, mixed, latent, wkv, wq, wo, up, down,
    tokens, upstream, pre, act, gpre, back, gup, gdown, middle, gmiddle, small, smalls, att, att_near, att_far,
    near, far, out_far, gmixed, gquery, gkv, slots, up_in, down_in, mstage, sums, sum_in, sum_head,
    sems,
):
    place = Place(count, sems, latents_in.shape[0] * latents_in.shape[1])
    loads = [
        place.local(media_in, media),
        place.local(latents_in, latents),
        place.local(cotangent_in, cotangent),
    ]
    place.barrier()
    items, local_media, width = media.shape
    local_latents = latents.shape[1]
    rows = local_media + local_latents
    keys_count = 4 * rows
    block_rows, columns = w_query.shape
    hidden = up.shape[2]
    part = block_rows // 2
    latent_count = 4 * local_latents
    all_latents = items * latent_count
    own_latents = items * local_latents
    group_rows = 4 * SPREAD * own_latents
    local_frames = local_media // P_SIZE
    scale = HEAD_DIM ** (-0.5)
    tile = 2 * block_rows
    item, y, core = place.item, place.y, place.core

    shift = block_rows * item % 128
    sum_head[0] = jnp.zeros_like(sum_head[0])
    sum_head[0, :, pl.ds(0, block_rows)] = small_in[...].astype(F32)
    smalls[item] = pltpu.roll(sum_head[0], shift, 1).astype(BF)
    small_copies = [
        place.send(smalls.at[item], smalls.at[item], {"item": place.other(k), "head": place.head})
        for k in range(1, count)
    ]
    for load in loads:
        load.wait()
    own = place.chip_rows(core, place.chip)
    upstream[own] = cotangent[...].reshape(own_latents, width)
    upstream_gather = GroupGather(place, upstream)
    upstream_gather.push(0, 1)

    def gather_pipes(source, slab, lanes):
        made = []
        for half, way in ((0, 1), (1, -1)):
            span = pl.ds(half * part, part)
            made.append(
                GatherPipe(place, source.at[span], lambda o, span=span: slab.at[o, span, lanes], way)
            )
        return made

    whole, second = pl.ds(0, columns), pl.ds(columns, columns)
    ring_pipes = (
        gather_pipes(w_key, wkv, whole)
        + gather_pipes(w_value, wkv, second)
        + gather_pipes(w_query, wq, whole)
        + gather_pipes(w_output, wo, whole)
    )
    ring = Pump(weave(*ring_pipes, steps=range(1, count)))
    each = len(ring_pipes)
    quarter = pl.ds(pl.multiple_of(place.quarter * hidden, 128), hidden)
    owns = [
        place.local(w_key, wkv.at[item, :, whole]),
        place.local(w_value, wkv.at[item, :, second]),
        place.local(w_query, wq.at[item]),
        place.local(w_output, wo.at[item]),
    ]
    own_hidden = [
        place.local(w_up.at[:, quarter], up.at[item]),
        place.local(w_down.at[:, quarter], down.at[item]),
    ]
    for copy in small_copies:
        copy.wait_recv()
    small[...] = jnp.zeros_like(small)
    for j in range(count):
        lanes = pl.ds(window(block_rows, j), smalls.shape[2])
        small[:, lanes] += smalls[j].astype(F32)
    time_rows = [small[pl.ds(6 + place.head * local_frames + f, 1), :] for f in range(local_frames)]

    gathers = []
    for b in range(items):
        for f in range(local_frames):
            span = pl.ds(f * P_SIZE, P_SIZE)
            normed, _ = norm_parts(media[b, span].astype(F32) + time_rows[f])
            joined[b, y, core, span] = (normed * small[0:1] + small[1:2]).astype(BF)
        normed, _ = norm_parts(latents[b].astype(F32))
        joined[b, y, core, pl.ds(local_media, local_latents)] = (
            normed * small[2:3] + small[3:4]
        ).astype(BF)
        gathers.append(HeadGather(place, joined.at[b]))

    def project(b):
        gathers[b].finish()
        kv[b] = dot(joined[b].reshape(keys_count, width), wkv[...].reshape(width, 2 * columns), 1, 0).astype(BF)
        for p in range(4):
            latent[p, pl.ds(b * local_latents, local_latents)] = joined[
                b, p // 2, p % 2, pl.ds(local_media, local_latents)
            ]

    ring(2 * each)
    gathers[0].forward()
    ring(2 * each)
    gathers[1].forward()
    ring(each)
    gathers[2].forward()
    ring()
    upstream_gather.push(0, 4, 2)

    def spread(source, slab, offsets, lanes_of=None):
        copies = []
        for k in offsets:
            to = place.other(k)
            if lanes_of is None:
                block = source.at[to]
            else:
                block = source.at[:, pl.ds(pl.multiple_of((to % SPREAD) * hidden, 128), hidden)]
            copies.append(place.send(block, slab.at[item], {"item": to, "head": place.head}))
        return copies

    straight, turned = (4, 2, 6), (3, 5, 1, 7)
    mixed_order = (4, 3, 5, 2, 6, 1, 7)
    up_copies = spread(w_up, up, mixed_order, hidden)
    gathers[3].forward()
    for copy in owns:
        copy.wait()
    for b in range(items):
        project(b)
    upstream_gather.pull(4, 0)
    upstream_gather.push(4, 2, 1)
    query[...] = (
        (scale * dot(latent[...].reshape(all_latents, width), wq[...].reshape(width, columns), 1, 0))
        .astype(BF)
        .reshape(query.shape)
    )
    masks = head_masks(latent_count, columns)
    index = lax.broadcasted_iota(jnp.int32, (1, keys_count), 1)
    local = index % rows
    frame = jnp.where(local < local_media, (index // rows) * local_frames + local // P_SIZE, -1)
    for b in range(items):
        mine = pl.ds(b * local_latents, local_latents)
        stacked = stack_heads(query[:, mine].reshape(latent_count, columns), masks)
        scores = dot(stacked, kv[b, :, :columns], 1, 1)
        shown = jnp.broadcast_to(frame, scores.shape) < frames_ref[b]
        scores = jnp.where(shown, scores, -1e30)
        expo = jnp.exp(scores - jnp.max(scores, axis=1, keepdims=True))
        weight = expo / jnp.sum(expo, axis=1, keepdims=True)
        weights[b] = weight
        result = fold_heads(dot(weight.astype(BF), kv[b, :, columns:], 1, 0), masks)
        mixed[:, mine] = result.astype(BF).reshape(4, local_latents, columns)
    att[...] = (
        dot(mixed[...].reshape(all_latents, columns), wo[...].reshape(width, columns), 1, 1)
        .astype(BF)
        .reshape(att.shape)
    )
    scatter = HeadScatter(place, att, [att_near.at[0], att_near.at[1]], att_far)
    scatter.forward()
    upstream_gather.pull(2, 0)
    upstream_gather.push(2, 1)
    middle[...] = latents[...].astype(F32).reshape(middle.shape) + scatter.finish()
    scatter.settle()
    normed, _ = norm_parts(middle[...])
    tokens[own] = (normed * small[4:5] + small[5:6]).astype(BF)
    token_gather = GroupGather(place, tokens)
    token_gather.push(0, 4, 2, 1)
    down_copies = spread(w_down, down, mixed_order, hidden)
    upstream_gather.pull(2, 4)
    upstream_gather.push(6, 1)
    token_gather.pull(4, 0)
    token_gather.push(4, 2, 1)
    token_gather.pull(2, 0)
    token_gather.push(2, 1)
    token_gather.pull(2, 4)
    token_gather.push(6, 1)
    for k in (0, 4, 2, 6):
        upstream_gather.pull(1, k)
    for k in (0, 4, 2, 6):
        token_gather.pull(1, k)
    token_gather.finish()

    for copy in own_hidden:
        copy.wait()
    for copy in up_copies:
        copy.wait_recv()
    blocks = 4
    tall = group_rows // blocks
    spans = [pl.ds(n * tall, tall) for n in range(blocks)]
    for span in spans:
        value, slope = gelu_parts(dot(tokens[span], up[...].reshape(width, hidden), 1, 0))
        act[span] = value.astype(BF)
        pre[span] = slope
    upstream_gather.finish()
    all_rows = pl.ds(0, group_rows)
    for t in range(width // tile):
        span = pl.ds(t * tile, tile)
        gdown[pl.ds(2 * t, 2)] = (
            dot(upstream[all_rows, span], act[...], 0, 0).astype(BF).reshape(2, block_rows, hidden)
        )
    down_sums = spread(gdown, down_in, straight)
    for copy in down_copies:
        copy.wait_recv()
    for n in range(blocks):
        if n == blocks // 2:
            back_scatter = GroupScatter(place, back, [near], far, (1, 2, 4))
        start = (blocks // 2 * (1 - core) + n) % blocks * tall
        span = pl.ds(pl.multiple_of(start, tall), tall)
        grad_act = dot(upstream[span], down[...].reshape(width, hidden), 1, 0)
        gpre[span] = (grad_act * pre[span]).astype(BF)
        back[span] = dot(gpre[span], up[...].reshape(width, hidden), 1, 1).astype(BF)
    back_scatter.first()
    for t in range(width // tile):
        span = pl.ds(t * tile, tile)
        gup[pl.ds(2 * t, 2)] = (
            dot(tokens[all_rows, span], gpre[...], 0, 0).astype(BF).reshape(2, block_rows, hidden)
        )
    up_sums = spread(gup, up_in, straight)
    down_own = place.local(gdown.at[item], down_in.at[item])
    up_own = place.local(gup.at[item], up_in.at[item])
    upstream_gather.settle()
    token_gather.settle()
    back_scatter.second()
    out = upstream
    for span in spans:
        out[span] = dot(act[span], down[...].reshape(width, hidden), 1, 1).astype(BF)
    back_scatter.third()
    lands = [gkv.at[pl.ds(k * near.shape[0], near.shape[0])] for k in range(2)]
    out_scatter = GroupScatter(place, out, lands, out_far, (1, 2, 4))
    down_sums += spread(gdown, down_in, turned)
    sums[...] = jnp.zeros_like(sums)
    grad_norm = back_scatter.finish()
    back_scatter.settle()

    dx, dg, db = norm_back(grad_norm, middle[...], small[4:5])
    sums[4:5] = dg
    sums[5:6] = db
    grad_middle = cotangent[...].astype(F32).reshape(middle.shape) + dx
    gmiddle[...] = grad_middle
    gatt = att
    gatt[y, core] = grad_middle.astype(BF)
    att_gather = HeadGather(place, gatt)
    out_scatter.first()
    out_scatter.absorb()
    up_sums += spread(gup, up_in, turned)
    att_gather.forward()
    att_gather.finish()
    go, gq = up, down
    gmixed[...] = (
        dot(gatt[...].reshape(all_latents, width), wo[...].reshape(width, columns), 1, 0)
        .astype(BF)
        .reshape(gmixed.shape)
    )
    for t in range(width // tile):
        span = pl.ds(t * tile, tile)
        go[pl.ds(2 * t, 2)] = (
            dot(gatt[:, :, :, span].reshape(all_latents, tile), mixed[...].reshape(all_latents, columns), 0, 0)
            .astype(BF)
            .reshape(2, block_rows, columns)
        )

    def scatter_pipes(first_slot, slab, lanes, result):
        made = []
        for half, way in ((0, 1), (1, -1)):
            span = pl.ds(half * part, part)

            def finish(value, span=span):
                result[span] = value

            def of_owner(o, half=half):
                if len(slab.shape) == 3:
                    return slab.at[o, pl.ds(half * part, part), lanes]
                return slab.at[pl.ds(pl.multiple_of(o * block_rows + half * part, part), part), lanes]

            made.append(
                ScatterPipe(
                    place,
                    of_owner,
                    slots.at[first_slot + half],
                    finish,
                    way,
                )
            )
        return made

    go_pipes = scatter_pipes(0, go, whole, o_output)

    for b in range(items):
        mine = pl.ds(b * local_latents, local_latents)
        q_stack = stack_heads(query[:, mine].reshape(latent_count, columns), masks)
        g_stack = stack_heads(gmixed[:, mine].reshape(latent_count, columns), masks)
        weight = weights[b]
        grad_weight = dot(g_stack, kv[b, :, columns:], 1, 1)
        inner = jnp.sum(weight * grad_weight, axis=1, keepdims=True)
        grad_score = (weight * (grad_weight - inner)).astype(BF)
        gq_rows = fold_heads(dot(grad_score, kv[b, :, :columns], 1, 0), masks).astype(BF)
        gquery[:, mine] = gq_rows.reshape(4, local_latents, columns)
        kv[b, :, :columns] = dot(grad_score, q_stack, 0, 0).astype(BF)
        kv[b, :, columns:] = dot(weight.astype(BF), g_stack, 0, 0).astype(BF)
    for t in range(width // tile):
        span = pl.ds(t * tile, tile)
        gkv[span] = dot(
            joined[:, :, :, :, span].reshape(items * keys_count, tile),
            kv[...].reshape(items * keys_count, 2 * columns),
            0,
            0,
        ).astype(BF)
    kv_pipes = scatter_pipes(2, gkv, whole, o_key) + scatter_pipes(4, gkv, second, o_value)
    for t in range(width // tile):
        span = pl.ds(t * tile, tile)
        gq[pl.ds(2 * t, 2)] = (
            (scale * dot(latent[:, :, span].reshape(all_latents, tile), gquery[...].reshape(all_latents, columns), 0, 0))
            .astype(BF)
            .reshape(2, block_rows, columns)
        )
    q_pipes = scatter_pipes(6, gq, whole, o_query)
    steps = weave(*go_pipes, steps=[0])
    for s in range(count - 1):
        steps += weave(*kv_pipes, *q_pipes, steps=[s])
        if s + 1 < count - 1:
            steps += weave(*go_pipes, steps=[s + 1])
    ring = Pump(steps)
    scatters = []
    for gather in gathers:
        gather.settle()
    for b in range(items):
        mine = pl.ds(b * local_latents, local_latents)
        gq_rows = gquery[:, mine].reshape(latent_count, columns)
        for t in range(width // tile):
            span = pl.ds(t * tile, tile)
            owners = pl.ds(2 * t, 2)
            value = dot(kv[b], wkv[owners].reshape(tile, 2 * columns), 1, 1)
            extra = scale * dot(gq_rows, wq[owners].reshape(tile, columns), 1, 1)
            for p in range(4):
                at = p * rows
                joined[b, p // 2, p % 2, pl.ds(0, local_media), span] = value[at : at + local_media].astype(BF)
                joined[b, p // 2, p % 2, pl.ds(local_media, local_latents), span] = (
                    value[at + local_media : at + rows] + extra[p * local_latents : (p + 1) * local_latents]
                ).astype(BF)
        lands = [tokens.at[pl.ds((2 * b + side) * rows, rows)] for side in range(2)]
        scatters.append(HeadScatter(place, joined.at[b], lands, back.at[pl.ds(b * rows, rows)]))
        if b > 0:
            scatters[b - 1].forward()
        if b == 1:
            out_scatter.second()
        if b == 2:
            ring(each)
    scatters[-1].forward()
    out_scatter.third()
    ring(each)

    def combine(copies, own, slab, result):
        own.wait()
        for copy in copies:
            copy.wait_recv()
        stores = []
        for k in range(SPREAD):
            grad = slab[k].astype(F32)
            for group in range(1, count // SPREAD):
                grad = grad + slab[group * SPREAD + k].astype(F32)
            span = pl.ds(k * block_rows, block_rows)
            pre[span] = grad
            stores.append(place.local(pre.at[span], result.at[:, pl.ds(k * hidden, hidden)]))
        return stores

    combined = combine(up_sums, up_own, up_in, o_up)
    for b in range(items):
        grad = scatters[b].finish()
        if b > 0:
            store.wait()
        for f in range(local_frames):
            span = slice(f * P_SIZE, (f + 1) * P_SIZE)
            dx, dg, db = norm_back(grad[span], media[b, span].astype(F32) + time_rows[f], small[0:1])
            mstage[span] = dx
            sums[0:1] += dg
            sums[1:2] += db
            sums[pl.ds(6 + place.head * local_frames + f, 1), :] += jnp.sum(dx, axis=0, keepdims=True)
        store = place.local(mstage, o_media.at[b])
        dx, dg, db = norm_back(grad[local_media:], latents[b].astype(F32), small[2:3])
        sums[2:3] += dg
        sums[3:4] += db
        o_lgrad[b] = gmiddle[pl.ds(b * local_latents, local_latents)] + dx
        if b == 0:
            for copy in combined:
                copy.wait()
            combined = combine(down_sums, down_own, down_in, o_down)
        ring((each, each, 2 * each, 0)[b])

    lanes = sum_in.shape[2]
    sum_copies = []
    for k in range(1, count):
        to = place.other(k)
        at = pl.multiple_of(window(block_rows, to), 128)
        sum_copies.append(
            place.send(sums.at[:, pl.ds(at, lanes)], sum_in.at[item], {"item": to, "head": place.head})
        )
    sum_in[item] = sums[:, pl.ds(pl.multiple_of(window(block_rows, item), 128), lanes)]
    o_out[...] = (middle[...] + out_scatter.finish()).astype(BF).reshape(o_out.shape)
    for copy in sum_copies:
        copy.wait_recv()
    value = jnp.sum(sum_in[...], axis=0)
    sum_head[0] = value
    head_copies = [
        place.send(sum_head.at[0], sum_head.at[k], device)
        for k, device in ((1, place.sibling), (2, place.across), (3, place.opposite))
    ]
    ring()
    for copy in head_copies:
        copy.wait_recv()
    total = jnp.sum(sum_head[...], axis=0)
    total = pltpu.roll(total, (lanes - shift) % lanes, 1)[:, :block_rows]
    frames = 4 * local_frames
    o_small[pl.ds(0, frames)] = total[6 : 6 + frames]
    o_small[pl.ds(frames, 6)] = total[:6]
    o_small[pl.ds(frames + 6, 2)] = jnp.zeros((2, block_rows), F32)
    place.drain()
    store.wait()
    for copy in combined:
        copy.wait()
    assert place.used <= sems.shape[0], place.used


def hand_over(frames, *refs):
    third = (len(refs) - 2) // 3
    sources, targets = refs[:third], refs[third : 2 * third + 1]
    stages, sems = refs[2 * third + 1 : -1], refs[-1]
    pieces = []
    for source, stage, target in sorted(
        zip(sources[:-1], stages[:-1], targets), key=lambda each: -math.prod(each[0].shape)
    ):
        pieces.append((source, stage, target))
    for span, target in ((pl.ds(0, frames), targets[-2]), (pl.ds(frames, 8), targets[-1])):
        pieces.append((sources[-1].at[span], stages[-1].at[span], target))
    loads = [pltpu.make_async_copy(a, b, sems.at[0, k]) for k, (a, b, _) in enumerate(pieces)]
    stores = [pltpu.make_async_copy(b, c, sems.at[1, k]) for k, (_, b, c) in enumerate(pieces)]
    for copy in loads:
        copy.start()
    for load, store in zip(loads, stores):
        load.wait()
        store.start()
    for copy in stores:
        copy.wait()


def kernel_step(
    count, media, latents, cotangent, frame_counts,
    query_weight, key_weight, value_weight, output_weight, up_weight, down_weight,
    media_gain, media_bias, latent_gain, latent_bias, ffn_gain, ffn_bias, time_embed,
):
    items, local_media, width = media.shape
    local_latents = latents.shape[1]
    frames = time_embed.shape[0]
    block_rows, columns = query_weight.shape
    hidden = up_weight.shape[1] // SPREAD
    rows = local_media + local_latents
    keys_count = 4 * rows
    own_latents = items * local_latents
    stacked = columns // HEAD_DIM * 4 * local_latents
    group = 2 * SPREAD
    row = lax.broadcasted_iota(jnp.int32, (16, block_rows), 0)
    small = jnp.zeros((16, block_rows), BF)
    vectors = (media_gain, media_bias, latent_gain, latent_bias, ffn_gain, ffn_bias)
    for k, vector in enumerate(vectors):
        small = jnp.where(row == k, vector[None, :], small)
    for f in range(frames):
        small = jnp.where(row == len(vectors) + f, time_embed[f : f + 1], small)

    def hbm(*shape, kind=BF):
        return jax.ShapeDtypeStruct(shape, kind)

    def buf(*shape, kind=BF):
        return pltpu.VMEM(shape, kind)

    vmem, anywhere = pl.BlockSpec(memory_space=pltpu.VMEM), pl.BlockSpec(memory_space=pl.ANY)
    all_rows = 2 * group * own_latents
    sum_rows = items * 2 * rows
    slab = (count, block_rows, hidden)
    results = pl.pallas_call(
        functools.partial(layer_kernel, count),
        out_shape=[
            hbm(*latents.shape),
            hbm(*latents.shape, kind=F32),
            hbm(*media.shape, kind=F32),
        ]
        + [hbm(block_rows, columns, kind=F32)] * 4
        + [hbm(block_rows, SPREAD * hidden, kind=F32)] * 2
        + [hbm(16, block_rows, kind=F32)],
        in_specs=[vmem, pl.BlockSpec(memory_space=pltpu.SMEM)] + [anywhere] * 9,
        out_specs=[vmem, vmem, anywhere] + [vmem] * 4 + [anywhere] * 2 + [vmem],
        scratch_shapes=[
            buf(*media.shape),
            buf(*latents.shape),
            buf(*latents.shape),
            buf(items, 2, 2, rows, width),
            buf(items, keys_count, 2 * columns),
            buf(4, own_latents, columns),
            buf(items, stacked, keys_count, kind=F32),
            buf(4, own_latents, columns),
            buf(4, own_latents, width),
            buf(count, block_rows, 2 * columns),
            buf(count, block_rows, columns),
            buf(count, block_rows, columns),
            buf(*slab),
            buf(*slab),
            buf(max(all_rows, sum_rows), width),
            buf(all_rows, width),
            buf(all_rows, hidden, kind=F32),
            buf(all_rows, hidden),
            buf(all_rows, hidden),
            buf(max(all_rows, items * rows), width),
            buf(*slab),
            buf(*slab),
            buf(own_latents, width, kind=F32),
            buf(own_latents, width, kind=F32),
            buf(16, width, kind=F32),
            buf(count, 16, 256),
            buf(2, 2, own_latents, width),
            buf(2, own_latents, width),
            buf(own_latents, width),
            buf(group * own_latents, width),
            buf(group - 1, own_latents, width),
            buf(group - 1, own_latents, width),
            buf(4, own_latents, columns),
            buf(4, own_latents, columns),
            buf(width, 2 * columns),
            buf(8, count - 1, block_rows // 2, columns),
            buf(*slab),
            buf(*slab),
            buf(local_media, width, kind=F32),
            buf(16, width, kind=F32),
            buf(count, 16, 256, kind=F32),
            buf(4, 16, 256, kind=F32),
            pltpu.SemaphoreType.DMA((512,)),
        ],
        compiler_params=pltpu.CompilerParams(
            collective_id=0, has_side_effects=True, vmem_limit_bytes=62 * 2**20
        ),
        name="layer",
    )(
        small, frame_counts, media, latents, cotangent, query_weight, key_weight, value_weight,
        output_weight, up_weight, down_weight,
    )
    shapes = [jax.ShapeDtypeStruct(r.shape, r.dtype) for r in results]
    results = pl.pallas_call(
        functools.partial(hand_over, frames),
        out_shape=shapes[:-1] + [hbm(frames, block_rows, kind=F32), hbm(8, block_rows, kind=F32)],
        in_specs=[anywhere] * len(shapes),
        out_specs=[anywhere] * (len(shapes) + 1),
        scratch_shapes=[pltpu.VMEM(s.shape, s.dtype) for s in shapes]
        + [pltpu.SemaphoreType.DMA((2, 40))],
        compiler_params=pltpu.CompilerParams(vmem_limit_bytes=60 * 2**20),
        name="hand_over",
    )(*results)
    times, vectors = results[9:]
    return (*results[:9], *(vectors[k] for k in range(6)), times)


def fits(mesh, media, query_weight, up_weight):
    count, heads = mesh.shape["item"], mesh.shape["head"]
    width, columns = query_weight.shape[0], query_weight.shape[1] // heads
    hidden = up_weight.shape[1] // heads
    block_rows = width // count
    return (
        heads == 4
        and count == 2 * SPREAD
        and block_rows % 64 == 0
        and block_rows <= 192
        and columns % 128 == 0
        and hidden % (128 * SPREAD) == 0
    )


def solution(mesh):
    rows = P("item", "head", None)
    block = P("item", "head")
    vector = P("item")
    table = P(None, "item")

    def run(*arrays):
        count = mesh.shape["item"]
        step = plain_step
        if fits(mesh, arrays[0], arrays[4], arrays[8]):
            step = functools.partial(kernel_step, count)
        return jax.shard_map(
            step,
            mesh=mesh,
            in_specs=(rows,) * 3 + (vector,) + (block,) * 6 + (vector,) * 6 + (table,),
            out_specs=(rows,) * 3 + (block,) * 6 + (vector,) * 6 + (table,),
            check_vma=False,
        )(*arrays)

    return run
```
